512 devices in a mesh: row: 32 (over y, z_hi, core), col: 16 (over x, z_lo).
Axes of the slice: x: 4, y: 8, z: 8 (z_hi: 2, z_lo: 4; z = z_hi * 4 + z_lo), core: 2. Of those that a mesh axis runs over, the one named last changes fastest.
Arguments:
- obj_field: float32 [2, 2, 2048, 4096], P(None, None, 'row', 'col'), may hold values from -5 to 5
- probe: float32 [2, 4, 128, 128], replicated, may hold values from -4 to 4
- scan_pos: int32 [32, 16, 1, 2], P('row', 'col'), may hold values from -64 to 4031, as said below
- live_count: int32 [32, 16], P('row', 'col'), may hold values from 0 to 1, as said below
- patterns: float32 [32, 16, 1, 128, 128], P('row', 'col'), may hold values from 0 to 4
Outputs:
- obj_grad: float32 [2, 2, 2048, 4096], P(None, None, 'row', 'col')
- probe_grad: float32 [2, 4, 128, 128], replicated
The draws below stay inside these ranges and needn't reach their ends.
Inputs may be any that keep to these rules, and one draw needn't show every extreme that they name: For slot k of tile (r, c), the window's centre (scan_pos[r, c, k, 0] + 64, scan_pos[r, c, k, 1] + 64) lies in that tile, rows r * 64 to (r + 1) * 64 - 1 and columns c * 256 to (c + 1) * 256 - 1. `live_count`: some tile holds 1 positions and some tile none.
All inputs are finite; a program needn't handle non-finite values.
Results may differ from the reference program's by a relative error of at most 0.0003.
Values sent between devices are 32-bit elements; how exact they have to be, the bound alone decides.
No kernel may reach another device: no remote copies, remote signals or barrier semaphores. Data moves between devices by JAX's collectives and lax.ppermute only.
A program may use at most 64 MiB of HBM per device.

```python
import jax
import jax.numpy as jnp
from jax import lax

P_SIZE = 128
MODES = 4
SLICES = 2
TR = 64
TC = 256
SLOTS = 1
NR = 2048
NC = 4096
N_ROW = 32
N_COL = 16


def draw_scan_pos(key, part):
    key = jax.random.fold_in(key, 11)
    row_key, col_key = jax.random.split(key)
    row_shift = jax.random.randint(row_key, (N_ROW, N_COL, SLOTS), 0, TR)
    col_shift = jax.random.randint(col_key, (N_ROW, N_COL, SLOTS), 0, TC)
    row_base = (jnp.arange(N_ROW, dtype=jnp.int32) * TR - P_SIZE // 2)[:, None, None]
    col_base = (jnp.arange(N_COL, dtype=jnp.int32) * TC - P_SIZE // 2)[None, :, None]
    rows = row_base + row_shift
    cols = col_base + col_shift
    rows = rows.at[0, 0, 0].set(-(P_SIZE // 2))
    cols = cols.at[0, 0, 0].set(-(P_SIZE // 2))
    rows = rows.at[N_ROW - 1, N_COL - 1, SLOTS - 1].set(N_ROW * TR - P_SIZE // 2 - 1)
    cols = cols.at[N_ROW - 1, N_COL - 1, SLOTS - 1].set(N_COL * TC - P_SIZE // 2 - 1)
    return jnp.stack([rows, cols], axis=-1).astype(jnp.int32)


def draw_live_count(key, part):
    key = jax.random.fold_in(key, 23)
    first_key, second_key = jax.random.split(key)
    total = N_ROW * N_COL
    counts = jax.random.randint(first_key, (total,), 0, SLOTS + 1)
    chosen = jax.random.randint(second_key, (), 0, total)
    places = jnp.arange(total, dtype=jnp.int32)
    counts = jnp.where(places == chosen, SLOTS, counts)
    counts = jnp.where(places == (chosen + 1) % total, 0, counts)
    return counts.reshape(N_ROW, N_COL).astype(jnp.int32)


def levels(own_key, extent, cuts, smallest, high):
    factor_of = 1.0
    for dim, blocks in cuts:
        draws = jax.random.uniform(jax.random.fold_in(jax.random.fold_in(own_key, 6), dim), (blocks,), jnp.float32, smallest / len(cuts), high / len(cuts))
        factor_of = factor_of * jnp.repeat(jnp.exp(draws), extent[dim] // blocks).reshape((-1,) + (1,) * (len(extent) - 1 - dim))
    return factor_of


def normal_values(key, dims, spread, most, cuts=(), kind=jnp.bfloat16):
    gain = levels(key, dims, cuts, -0.22, 0.18) if cuts else 1.0
    values = jax.random.normal(key, dims, jnp.float32) * spread * gain
    return jnp.minimum(jnp.maximum(values, -most), most).astype(kind)


def setup_inputs(seed: int = 0) -> dict:
    keys = jax.random.split(jax.random.key(seed), 6)
    obj_field = normal_values(keys[0], (2, SLICES, NR, NC), 0.7, 5.0, ((2, 32), (3, 16)), jnp.float32)
    probe = normal_values(keys[1], (2, MODES, P_SIZE, P_SIZE), 0.5, 4.0, (), jnp.float32)
    scan_pos = draw_scan_pos(jax.random.fold_in(keys[5], 71), 0)
    live_count = draw_live_count(jax.random.fold_in(keys[5], 71), 0)
    patterns = jnp.clip(4.0 * jax.random.uniform(keys[4], (N_ROW, N_COL, SLOTS, P_SIZE, P_SIZE), jnp.float32) ** levels(keys[4], (N_ROW, N_COL, SLOTS, P_SIZE, P_SIZE), ((0, 32), (1, 16)), -0.2, 0.2), 0.0, 4.0)
    return dict(obj_field=obj_field, probe=probe, scan_pos=scan_pos, live_count=live_count, patterns=patterns)


PHASE_COEF = 20.0
LOSS_WEIGHT = 0.125

def propagator():
    counter = jnp.arange(P_SIZE)
    spatial = ((counter + P_SIZE // 2) % P_SIZE - P_SIZE // 2).astype(jnp.float32) / P_SIZE
    phase = -PHASE_COEF * (spatial[:, None] * spatial[:, None] + spatial[None, :] * spatial[None, :])
    return (jnp.cos(phase), jnp.sin(phase))

def complex_times(first_real, first_imaginary, second_real, second_imaginary):
    return (first_real * second_real - first_imaginary * second_imaginary, first_real * second_imaginary + first_imaginary * second_real)

def exit_loss(window, probe, pattern, forward, backward):
    kernel_real, kernel_imaginary = propagator()
    wave_real, wave_imaginary = (probe[0], probe[1])
    for layer in range(SLICES):
        wave_real, wave_imaginary = complex_times(wave_real, wave_imaginary, window[0, layer], window[1, layer])
        if layer + 1 < SLICES:
            spectral_real, spectral_imaginary = forward(wave_real, wave_imaginary)
            spectral_real, spectral_imaginary = complex_times(spectral_real, spectral_imaginary, kernel_real, kernel_imaginary)
            wave_real, wave_imaginary = backward(spectral_real, spectral_imaginary)
    far_real, far_imaginary = forward(wave_real, wave_imaginary)
    intensity = lax.optimization_barrier(jnp.sum(far_real * far_real + far_imaginary * far_imaginary, axis=0))
    residue = intensity - pattern
    return LOSS_WEIGHT * jnp.sum(residue * residue)

def fourier_forward(field_real, field_imaginary):
    spectrum = jnp.fft.fft2(field_real + 1j * field_imaginary, norm='ortho')
    return (jnp.real(spectrum), jnp.imag(spectrum))

def fourier_backward(field_real, field_imaginary):
    spectrum = jnp.fft.ifft2(field_real + 1j * field_imaginary, norm='ortho')
    return (jnp.real(spectrum), jnp.imag(spectrum))

def reference(obj_field, probe, scan_pos, live_count, patterns):
    margin = P_SIZE // 2
    padded = jnp.pad(obj_field, ((0, 0), (0, 0), (margin, margin), (margin, margin)))
    corners = scan_pos.reshape(-1, 2)
    pattern_set = patterns.reshape(-1, P_SIZE, P_SIZE)
    slot_index = jnp.arange(N_ROW * N_COL * SLOTS, dtype=jnp.int32) % SLOTS
    counts = jnp.repeat(live_count.reshape(-1), SLOTS)
    weights = (slot_index < counts).astype(jnp.float32)
    zero = jnp.zeros((), jnp.int32)

    def visit(running, scan_item):
        grad_field, grad_probe = running
        corner, pattern, weight = scan_item
        starts = (zero, zero, (corner[0] + margin).astype(jnp.int32), (corner[1] + margin).astype(jnp.int32))
        window = lax.dynamic_slice(padded, starts, (2, SLICES, P_SIZE, P_SIZE))

        def local_loss(window_in, probe_in):
            return exit_loss(window_in, probe_in, pattern, fourier_forward, fourier_backward)
        loss_value, pullback = jax.vjp(local_loss, window, probe)
        grad_window, grad_of_probe = pullback(jnp.ones_like(loss_value) * weight)
        patch = lax.dynamic_slice(grad_field, starts, (2, SLICES, P_SIZE, P_SIZE))
        grad_field = lax.dynamic_update_slice(grad_field, patch + grad_window, starts)
        return ((grad_field, grad_probe + grad_of_probe), None)
    initial = (jnp.zeros_like(padded), jnp.zeros_like(probe))
    finished, unused = lax.scan(visit, initial, (corners, pattern_set, weights))
    grad_field, grad_probe = finished
    return (grad_field[:, :, margin:margin + NR, margin:margin + NC], grad_probe)
```

```python
import functools
import math

import jax
import jax.numpy as jnp
import ml_dtypes
import numpy as np
from jax import lax
from jax.experimental import pallas as pl
from jax.experimental.pallas import tpu as pltpu
from jax.sharding import Mesh
from jax.sharding import PartitionSpec as P

PHASE_COEF = 20.0
LOSS_WEIGHT = 0.125
ROW = ("y", "zh", "core")
COL = ("x", "zl")
VMEM_LIMIT = 48 * 1024 * 1024


def split_bf16(table):
    high = table.astype(np.float32).astype(ml_dtypes.bfloat16)
    low = (table - high.astype(np.float64)).astype(np.float32).astype(ml_dtypes.bfloat16)
    return high, low


def tables(side):
    counter = np.arange(side)
    phase = 2.0 * math.pi / side * (counter[:, None] * counter[None, :] % side)
    fourier = np.exp(-1j * phase) / math.sqrt(side)
    spatial = ((counter + side // 2) % side - side // 2) / side
    factor = np.exp(-1j * PHASE_COEF * spatial * spatial)
    propagate = np.conj(fourier) @ (factor[:, None] * fourier)
    propagate = 0.5 * (propagate + propagate.T)
    parts = []
    for matrix in (propagate, fourier):
        real, imaginary = matrix.real, matrix.imag
        right = np.block([[real, imaginary], [-imaginary, real]])
        left = np.block([[real, -imaginary], [imaginary, real]])
        parts += [*split_bf16(right), *split_bf16(left)]
    return np.stack(parts)


def split(value):
    high = value.astype(jnp.bfloat16)
    low = (value - high.astype(jnp.float32)).astype(jnp.bfloat16)
    return high, low


def product(left, right):
    (left_high, left_low), (right_high, right_low) = left, right
    dot = functools.partial(jnp.dot, preferred_element_type=jnp.float32)
    return dot(left_high, right_high) + (dot(left_low, right_high) + dot(left_high, right_low))


def two_sided(real, imaginary, right, left):
    side = real[0].shape[0]
    modes = len(real)
    stacked = jnp.concatenate(
        [jnp.concatenate([r, i], axis=1) for r, i in zip(real, imaginary)], axis=0
    )
    middle = product(split(stacked), right)
    blocks = [middle[m * side : (m + 1) * side] for m in range(modes)]
    spread = jnp.concatenate(
        [
            jnp.concatenate([b[:, :side] for b in blocks], axis=1),
            jnp.concatenate([b[:, side:] for b in blocks], axis=1),
        ],
        axis=0,
    )
    out = product(left, split(spread))
    return (
        [out[:side, m * side : (m + 1) * side] for m in range(modes)],
        [out[side:, m * side : (m + 1) * side] for m in range(modes)],
    )


def times(ar, ai, br, bi):
    return ar * br - ai * bi, ar * bi + ai * br


def times_conj(ar, ai, br, bi):
    return ar * br + ai * bi, ar * bi - ai * br


def model(window, probe, pattern, weight, tabs):
    (o0r, o1r), (o0i, o1i) = window
    qr, qi = probe
    modes = len(qr)
    prop_right, prop_left, four_right, four_left = [
        (tabs[2 * n], tabs[2 * n + 1]) for n in range(4)
    ]
    e0 = [times(qr[m], qi[m], o0r, o0i) for m in range(modes)]
    a1r, a1i = two_sided([e[0] for e in e0], [e[1] for e in e0], prop_right, prop_left)
    e1 = [times(a1r[m], a1i[m], o1r, o1i) for m in range(modes)]
    gr, gi = two_sided([e[0] for e in e1], [e[1] for e in e1], four_right, four_left)
    intensity = gr[0] * gr[0] + gi[0] * gi[0]
    for m in range(1, modes):
        intensity = intensity + (gr[m] * gr[m] + gi[m] * gi[m])
    residue = (intensity - pattern) * (4.0 * LOSS_WEIGHT * weight)
    br, bi = two_sided(
        [residue * g for g in gr], [residue * g for g in gi], four_left, four_right
    )
    grad1 = [times_conj(a1r[m], a1i[m], br[m], bi[m]) for m in range(modes)]
    back = [times_conj(o1r, o1i, br[m], bi[m]) for m in range(modes)]
    cr, ci = two_sided([b[0] for b in back], [b[1] for b in back], prop_left, prop_right)
    grad0 = [times_conj(qr[m], qi[m], cr[m], ci[m]) for m in range(modes)]
    probe_grad = [times_conj(o0r, o0i, cr[m], ci[m]) for m in range(modes)]

    def over_modes(terms, part):
        return functools.reduce(lambda a, b: a + b, [t[part] for t in terms])

    window_grad = [
        [over_modes(grad0, 0), over_modes(grad1, 0)],
        [over_modes(grad0, 1), over_modes(grad1, 1)],
    ]
    return window_grad, probe_grad


def main_kernel(
    place, own, other, beyond, from_left, from_right, probe, pattern, tabs,
    keep, message_core, message_beyond, own_strip, extended, shifted,
):
    row, col, core, live = place[0], place[1], place[2], place[3]
    side = probe.shape[-1]
    half = side // 2
    rows, cols = own.shape[2], own.shape[3]
    modes = probe.shape[1]
    other_at = pl.multiple_of((1 - core) * 2 * half, 8)
    beyond_at = pl.multiple_of(core * 2 * half, 8)
    for layer in range(2):
        for part in range(2):
            plane = 2 * part + layer
            inner = pl.ds(half, cols)
            extended[plane, half : half + rows, inner] = own[part, layer]
            extended[plane, pl.ds(other_at, rows), inner] = other[part, layer]
            extended[plane, pl.ds(beyond_at, rows), inner] = beyond[part, layer]
            mine = pl.ds(part * half, half)
            extended[plane, :, 0:half] = from_left[layer, :, mine]
            extended[plane, :, half + cols : 2 * half + cols] = from_right[layer, :, mine]

    tall = side + 8
    step = lax.rem(row, 8)
    base_row = pl.multiple_of(row - step, 8)

    def window_of(plane):
        wide = extended[plane, pl.ds(base_row, tall), :]
        narrow = pltpu.roll(wide, lax.rem(wide.shape[1] - col, wide.shape[1]), 1)[:, :side]
        return pltpu.roll(narrow, lax.rem(tall - step, tall), 0)[:side]

    window = [[window_of(2 * part + layer) for layer in range(2)] for part in range(2)]
    fields = [[probe[part, m] for m in range(modes)] for part in range(2)]
    weight = live.astype(jnp.float32)
    window_grad, probe_grad = model(
        window, fields, pattern[0, 0, 0], weight, [tabs[n] for n in range(8)]
    )
    first = core == 0
    for m in range(modes):
        at = pl.ds(m * side, side)
        real, imaginary = probe_grad[m]
        keep[at, :] = jnp.where(first, real, imaginary)
        message_core[at, :] = jnp.where(first, imaginary, real)
    base = modes * side
    shifted[...] = jnp.zeros_like(shifted)
    for part in range(2):
        for layer in range(2):
            plane = 2 * part + layer
            padded = jnp.concatenate(
                [window_grad[part][layer], jnp.zeros((8, side), jnp.float32)], axis=0
            )
            shifted[plane, pl.ds(base_row, tall), :] = pltpu.roll(padded, step, 0)
            message_core[pl.ds(base + plane * rows, rows), :] = shifted[plane, pl.ds(other_at, rows), :]
            message_beyond[pl.ds(plane * rows, rows), :] = shifted[plane, pl.ds(beyond_at, rows), :]
            own_strip[pl.ds(plane * rows, rows), :] = shifted[plane, half : half + rows, :]
    offset = jnp.full((8, side), col.astype(jnp.float32))
    message_core[pl.ds(base + 4 * rows, 8), :] = offset
    message_beyond[pl.ds(4 * rows, 8), :] = offset


def pack_kernel(place, own, other, beyond, to_left, to_right):
    core = place[2]
    half = own.shape[2]
    cols = own.shape[3]
    other_at = pl.multiple_of((1 - core) * 2 * half, 8)
    beyond_at = pl.multiple_of(core * 2 * half, 8)
    for source, at in ((own, half), (other, other_at), (beyond, beyond_at)):
        for layer in range(2):
            for part in range(2):
                mine = pl.ds(part * half, half)
                to_left[layer, pl.ds(at, half), mine] = source[part, layer, :, 0:half]
                to_right[layer, pl.ds(at, half), mine] = source[part, layer, :, cols - half : cols]


def merge_kernel(place, own_strip, from_core, from_beyond, centre, to_left, to_right):
    side = own_strip.shape[1]
    half = side // 2
    rows = centre.shape[2]
    cols = centre.shape[3]
    wide = cols + side
    base = from_core.shape[0] - from_beyond.shape[0]
    core_col = jnp.max(from_core[pl.ds(base + 4 * rows, 8), :]).astype(jnp.int32)
    beyond_col = jnp.max(from_beyond[pl.ds(4 * rows, 8), :]).astype(jnp.int32)
    gap = jnp.zeros((rows, cols), jnp.float32)

    def placed(strip, col):
        return pltpu.roll(jnp.concatenate([strip, gap], axis=1), col, 1)

    for layer in range(2):
        for part in range(2):
            plane = 2 * part + layer
            total = placed(own_strip[pl.ds(plane * rows, rows), :], place[1])
            total = total + placed(from_core[pl.ds(base + plane * rows, rows), :], core_col)
            total = total + placed(from_beyond[pl.ds(plane * rows, rows), :], beyond_col)
            centre[part, layer] = total[:, half : half + cols]
            mine = pl.ds(part * half, half)
            to_left[layer, :, mine] = total[:, :half]
            to_right[layer, :, mine] = total[:, wide - half :]


def finish_kernel(centre, from_left, from_right, out):
    half = centre.shape[2]
    cols = centre.shape[3]
    for layer in range(2):
        for part in range(2):
            mine = pl.ds(part * half, half)
            value = centre[part, layer]
            out[part, layer] = value
            out[part, layer, :, 0:half] = value[:, :half] + from_left[layer, :, mine]
            out[part, layer, :, cols - half : cols] = value[:, cols - half :] + from_right[layer, :, mine]


def call(kernel, out_shape, n_scalars, n_in, scratch=(), cost=None):
    many = isinstance(out_shape, (list, tuple))
    vmem = pl.BlockSpec(memory_space=pltpu.VMEM)
    return pl.pallas_call(
        kernel,
        out_shape=out_shape,
        in_specs=[pl.BlockSpec(memory_space=pltpu.SMEM)] * n_scalars + [vmem] * n_in,
        out_specs=[vmem] * len(out_shape) if many else vmem,
        scratch_shapes=list(scratch),
        compiler_params=pltpu.CompilerParams(vmem_limit_bytes=VMEM_LIMIT),
        cost_estimate=cost,
    )


def chain(n, step):
    return [(i, i + step) for i in range(n) if 0 <= i + step < n]


def body(obj_field, probe, scan_pos, live_count, patterns):
    side = probe.shape[2]
    modes = probe.shape[1]
    half = side // 2
    rows, cols = obj_field.shape[2], obj_field.shape[3]
    n_row, n_col = lax.axis_size(ROW), lax.axis_size(COL)
    f32 = jnp.float32
    core = lax.axis_index("core")
    row = scan_pos[0, 0, 0, 0] - (lax.axis_index(ROW) * rows - half)
    col = scan_pos[0, 0, 0, 1] - (lax.axis_index(COL) * cols - half)
    live = (live_count[0, 0] > 0).astype(jnp.int32)
    place = jnp.stack([row, col, core, live]).astype(jnp.int32)
    swap = [(0, 1), (1, 0)]
    pairs = [(i, i + 1) for i in range(1, n_row - 1, 2)]
    pairs = pairs + [(j, i) for i, j in pairs]

    def shape(*dims):
        return jax.ShapeDtypeStruct(dims, f32)

    beyond = lax.ppermute(obj_field, ROW, pairs)
    other = lax.ppermute(obj_field, "core", swap)
    column = shape(2, 2 * half + rows, side)
    to_left, to_right = call(pack_kernel, [column, column], 1, 3)(place, obj_field, other, beyond)
    from_left = lax.ppermute(to_right, COL, chain(n_col, 1))
    from_right = lax.ppermute(to_left, COL, chain(n_col, -1))

    tabs = jnp.asarray(tables(side))
    strip = 4 * rows
    keep, message_core, message_beyond, own_strip = call(
        main_kernel,
        [
            shape(modes * side, side),
            shape(modes * side + strip + 8, side),
            shape(strip + 8, side),
            shape(strip, side),
        ],
        1,
        8,
        [
            pltpu.VMEM((4, 2 * half + rows, 2 * half + cols), f32),
            pltpu.VMEM((4, 2 * half + rows, side), f32),
        ],
    )(place, obj_field, other, beyond, from_left, from_right, probe, patterns, tabs)

    from_core = lax.ppermute(message_core, "core", swap)
    from_beyond = lax.ppermute(message_beyond, ROW, pairs)

    n_yx = lax.axis_size(("y", "x"))
    n_z = lax.axis_size(("zh", "zl"))
    total = modes * side
    chunk = total // n_yx
    summed = keep + from_core[:total]
    spread = lax.all_to_all(summed.reshape(n_yx, chunk, side), ("y", "x"), 0, 0)

    edge = shape(2, rows, side)
    centre, grad_left, grad_right = call(
        merge_kernel, [shape(2, 2, rows, cols), edge, edge], 1, 3
    )(place, own_strip, from_core, from_beyond)
    got_left = lax.ppermute(grad_right, COL, chain(n_col, 1))
    got_right = lax.ppermute(grad_left, COL, chain(n_col, -1))

    part = jnp.sum(spread, axis=0)
    part = lax.all_to_all(jnp.broadcast_to(part, (n_z, chunk, side)), ("zh", "zl"), 0, 0)
    part = jnp.sum(part, axis=0)
    whole = lax.all_to_all(jnp.broadcast_to(part, (n_yx, chunk, side)), ("y", "x"), 0, 0)
    whole = whole.reshape(modes, side, side)
    facing = lax.ppermute(whole, "core", swap)
    first = core == 0
    probe_grad = jnp.stack([jnp.where(first, whole, facing), jnp.where(first, facing, whole)])

    obj_grad = call(finish_kernel, shape(2, 2, rows, cols), 0, 3)(centre, got_left, got_right)
    return (obj_grad, probe_grad)


def solution(mesh):
    fine = Mesh(
        mesh.devices.reshape(8, 2, 2, 4, 4), ("y", "zh", "core", "x", "zl")
    )
    return jax.shard_map(
        body,
        mesh=fine,
        in_specs=(
            P(None, None, ROW, COL),
            P(),
            P(ROW, COL, None, None),
            P(ROW, COL),
            P(ROW, COL, None, None, None),
        ),
        out_specs=(P(None, None, ROW, COL), P()),
        check_vma=False,
    )
```

```python
import functools
import math

import jax
import jax.numpy as jnp
import ml_dtypes
import numpy as np
from jax import lax
from jax.experimental import pallas as pl
from jax.experimental.pallas import tpu as pltpu
from jax.sharding import Mesh
from jax.sharding import PartitionSpec as P

PHASE_COEF = 20.0
LOSS_WEIGHT = 0.125
ROW = ("y", "zh", "core")
COL = ("x", "zl")
VMEM_LIMIT = 48 * 1024 * 1024


def split_bf16(table):
    high = table.astype(np.float32).astype(ml_dtypes.bfloat16)
    low = (table - high.astype(np.float64)).astype(np.float32).astype(ml_dtypes.bfloat16)
    return high, low


def tables(side):
    counter = np.arange(side)
    phase = 2.0 * math.pi / side * (counter[:, None] * counter[None, :] % side)
    fourier = np.exp(-1j * phase) / math.sqrt(side)
    spatial = ((counter + side // 2) % side - side // 2) / side
    factor = np.exp(-1j * PHASE_COEF * spatial * spatial)
    propagate = np.conj(fourier) @ (factor[:, None] * fourier)
    propagate = 0.5 * (propagate + propagate.T)
    parts = []
    for matrix in (propagate, fourier):
        for block in (matrix.real, matrix.imag, -matrix.imag):
            parts += split_bf16(block)
    return np.stack(parts)


def on_sides(tabs, which):
    def block(n, part):
        return tabs[6 * which + 2 * n + part]

    def square(a, b, c, d, part):
        return jnp.concatenate(
            [
                jnp.concatenate([block(a, part), block(b, part)], axis=1),
                jnp.concatenate([block(c, part), block(d, part)], axis=1),
            ],
            axis=0,
        )

    right = tuple(square(0, 1, 2, 0, part) for part in range(2))
    left = tuple(square(0, 2, 1, 0, part) for part in range(2))
    return right, left


def split(value):
    high = value.astype(jnp.bfloat16)
    low = (value - high.astype(jnp.float32)).astype(jnp.bfloat16)
    return high, low


def product(left, right):
    (left_high, left_low), (right_high, right_low) = left, right
    dot = functools.partial(jnp.dot, preferred_element_type=jnp.float32)
    return dot(left_high, right_high) + (dot(left_low, right_high) + dot(left_high, right_low))


def two_sided(real, imaginary, right, left):
    side = real[0].shape[0]
    modes = len(real)
    stacked = jnp.concatenate(
        [jnp.concatenate([r, i], axis=1) for r, i in zip(real, imaginary)], axis=0
    )
    middle = product(split(stacked), right)
    blocks = [middle[m * side : (m + 1) * side] for m in range(modes)]
    spread = jnp.concatenate(
        [
            jnp.concatenate([b[:, :side] for b in blocks], axis=1),
            jnp.concatenate([b[:, side:] for b in blocks], axis=1),
        ],
        axis=0,
    )
    out = product(left, split(spread))
    return (
        [out[:side, m * side : (m + 1) * side] for m in range(modes)],
        [out[side:, m * side : (m + 1) * side] for m in range(modes)],
    )


def times(ar, ai, br, bi):
    return ar * br - ai * bi, ar * bi + ai * br


def times_conj(ar, ai, br, bi):
    return ar * br + ai * bi, ar * bi - ai * br


def model(window, probe, pattern, weight, tabs):
    (o0r, o1r), (o0i, o1i) = window
    qr, qi = probe
    modes = len(qr)
    prop_right, prop_left = on_sides(tabs, 0)
    four_right, four_left = on_sides(tabs, 1)
    e0 = [times(qr[m], qi[m], o0r, o0i) for m in range(modes)]
    a1r, a1i = two_sided([e[0] for e in e0], [e[1] for e in e0], prop_right, prop_left)
    e1 = [times(a1r[m], a1i[m], o1r, o1i) for m in range(modes)]
    gr, gi = two_sided([e[0] for e in e1], [e[1] for e in e1], four_right, four_left)
    intensity = gr[0] * gr[0] + gi[0] * gi[0]
    for m in range(1, modes):
        intensity = intensity + (gr[m] * gr[m] + gi[m] * gi[m])
    residue = (intensity - pattern) * (4.0 * LOSS_WEIGHT * weight)
    br, bi = two_sided(
        [residue * g for g in gr], [residue * g for g in gi], four_left, four_right
    )
    grad1 = [times_conj(a1r[m], a1i[m], br[m], bi[m]) for m in range(modes)]
    back = [times_conj(o1r, o1i, br[m], bi[m]) for m in range(modes)]
    cr, ci = two_sided([b[0] for b in back], [b[1] for b in back], prop_left, prop_right)
    grad0 = [times_conj(qr[m], qi[m], cr[m], ci[m]) for m in range(modes)]
    probe_grad = [times_conj(o0r, o0i, cr[m], ci[m]) for m in range(modes)]

    def over_modes(terms, part):
        return functools.reduce(lambda a, b: a + b, [t[part] for t in terms])

    window_grad = [
        [over_modes(grad0, 0), over_modes(grad1, 0)],
        [over_modes(grad0, 1), over_modes(grad1, 1)],
    ]
    return window_grad, probe_grad


def main_kernel(
    place, own, other, beyond, from_left, from_right, probe, pattern, tabs,
    keep, message_core, message_beyond, own_strip, extended, shifted,
):
    row, col, core, live = place[0], place[1], place[2], place[3]
    side = probe.shape[-1]
    half = side // 2
    rows, cols = own.shape[2], own.shape[3]
    modes = probe.shape[1]
    other_at = pl.multiple_of((1 - core) * 2 * half, 8)
    beyond_at = pl.multiple_of(core * 2 * half, 8)
    for layer in range(2):
        for part in range(2):
            plane = 2 * part + layer
            inner = pl.ds(half, cols)
            extended[plane, half : half + rows, inner] = own[part, layer]
            extended[plane, pl.ds(other_at, rows), inner] = other[part, layer]
            extended[plane, pl.ds(beyond_at, rows), inner] = beyond[part, layer]
            mine = pl.ds(part * half, half)
            extended[plane, :, 0:half] = from_left[layer, :, mine]
            extended[plane, :, half + cols : 2 * half + cols] = from_right[layer, :, mine]

    tall = side + 8
    step = lax.rem(row, 8)
    base_row = pl.multiple_of(row - step, 8)

    def window_of(plane):
        wide = extended[plane, pl.ds(base_row, tall), :]
        narrow = pltpu.roll(wide, lax.rem(wide.shape[1] - col, wide.shape[1]), 1)[:, :side]
        return pltpu.roll(narrow, lax.rem(tall - step, tall), 0)[:side]

    window = [[window_of(2 * part + layer) for layer in range(2)] for part in range(2)]
    fields = [[probe[part, m] for m in range(modes)] for part in range(2)]
    weight = live.astype(jnp.float32)
    window_grad, probe_grad = model(
        window, fields, pattern[0, 0, 0], weight, tabs
    )
    first = core == 0
    for m in range(modes):
        at = pl.ds(m * side, side)
        real, imaginary = probe_grad[m]
        keep[at, :] = jnp.where(first, real, imaginary)
        message_core[at, :] = jnp.where(first, imaginary, real)
    base = modes * side
    shifted[...] = jnp.zeros_like(shifted)
    for part in range(2):
        for layer in range(2):
            plane = 2 * part + layer
            padded = jnp.concatenate(
                [window_grad[part][layer], jnp.zeros((8, side), jnp.float32)], axis=0
            )
            shifted[plane, pl.ds(base_row, tall), :] = pltpu.roll(padded, step, 0)
            message_core[pl.ds(base + plane * rows, rows), :] = shifted[plane, pl.ds(other_at, rows), :]
            message_beyond[pl.ds(plane * rows, rows), :] = shifted[plane, pl.ds(beyond_at, rows), :]
            own_strip[pl.ds(plane * rows, rows), :] = shifted[plane, half : half + rows, :]
    offset = jnp.full((8, side), col.astype(jnp.float32))
    message_core[pl.ds(base + 4 * rows, 8), :] = offset
    message_beyond[pl.ds(4 * rows, 8), :] = offset


def pack_kernel(place, own, other, beyond, to_left, to_right):
    core = place[2]
    half = own.shape[2]
    cols = own.shape[3]
    other_at = pl.multiple_of((1 - core) * 2 * half, 8)
    beyond_at = pl.multiple_of(core * 2 * half, 8)
    for source, at in ((own, half), (other, other_at), (beyond, beyond_at)):
        for layer in range(2):
            for part in range(2):
                mine = pl.ds(part * half, half)
                to_left[layer, pl.ds(at, half), mine] = source[part, layer, :, 0:half]
                to_right[layer, pl.ds(at, half), mine] = source[part, layer, :, cols - half : cols]


def merge_kernel(place, own_strip, from_core, from_beyond, centre, to_left, to_right):
    side = own_strip.shape[1]
    half = side // 2
    rows = centre.shape[2]
    cols = centre.shape[3]
    wide = cols + side
    base = from_core.shape[0] - from_beyond.shape[0]
    core_col = jnp.max(from_core[pl.ds(base + 4 * rows, 8), :]).astype(jnp.int32)
    beyond_col = jnp.max(from_beyond[pl.ds(4 * rows, 8), :]).astype(jnp.int32)
    gap = jnp.zeros((rows, cols), jnp.float32)

    def placed(strip, col):
        return pltpu.roll(jnp.concatenate([strip, gap], axis=1), col, 1)

    for layer in range(2):
        for part in range(2):
            plane = 2 * part + layer
            total = placed(own_strip[pl.ds(plane * rows, rows), :], place[1])
            total = total + placed(from_core[pl.ds(base + plane * rows, rows), :], core_col)
            total = total + placed(from_beyond[pl.ds(plane * rows, rows), :], beyond_col)
            centre[part, layer] = total[:, half : half + cols]
            mine = pl.ds(part * half, half)
            to_left[layer, :, mine] = total[:, :half]
            to_right[layer, :, mine] = total[:, wide - half :]


def finish_kernel(centre, from_left, from_right, out):
    half = centre.shape[2]
    cols = centre.shape[3]
    for layer in range(2):
        for part in range(2):
            mine = pl.ds(part * half, half)
            value = centre[part, layer]
            out[part, layer] = value
            out[part, layer, :, 0:half] = value[:, :half] + from_left[layer, :, mine]
            out[part, layer, :, cols - half : cols] = value[:, cols - half :] + from_right[layer, :, mine]


def call(kernel, out_shape, n_scalars, n_in, scratch=(), cost=None):
    many = isinstance(out_shape, (list, tuple))
    vmem = pl.BlockSpec(memory_space=pltpu.VMEM)
    return pl.pallas_call(
        kernel,
        out_shape=out_shape,
        in_specs=[pl.BlockSpec(memory_space=pltpu.SMEM)] * n_scalars + [vmem] * n_in,
        out_specs=[vmem] * len(out_shape) if many else vmem,
        scratch_shapes=list(scratch),
        compiler_params=pltpu.CompilerParams(vmem_limit_bytes=VMEM_LIMIT),
        cost_estimate=cost,
    )


def chain(n, step):
    return [(i, i + step) for i in range(n) if 0 <= i + step < n]


def body(obj_field, probe, scan_pos, live_count, patterns):
    side = probe.shape[2]
    modes = probe.shape[1]
    half = side // 2
    rows, cols = obj_field.shape[2], obj_field.shape[3]
    n_row, n_col = lax.axis_size(ROW), lax.axis_size(COL)
    f32 = jnp.float32
    core = lax.axis_index("core")
    row = scan_pos[0, 0, 0, 0] - (lax.axis_index(ROW) * rows - half)
    col = scan_pos[0, 0, 0, 1] - (lax.axis_index(COL) * cols - half)
    live = (live_count[0, 0] > 0).astype(jnp.int32)
    place = jnp.stack([row, col, core, live]).astype(jnp.int32)
    swap = [(0, 1), (1, 0)]
    pairs = [(i, i + 1) for i in range(1, n_row - 1, 2)]
    pairs = pairs + [(j, i) for i, j in pairs]

    def shape(*dims):
        return jax.ShapeDtypeStruct(dims, f32)

    beyond = lax.ppermute(obj_field, ROW, pairs)
    other = lax.ppermute(obj_field, "core", swap)
    column = shape(2, 2 * half + rows, side)
    to_left, to_right = call(pack_kernel, [column, column], 1, 3)(place, obj_field, other, beyond)
    from_left = lax.ppermute(to_right, COL, chain(n_col, 1))
    from_right = lax.ppermute(to_left, COL, chain(n_col, -1))

    tabs = jnp.asarray(tables(side))
    strip = 4 * rows
    keep, message_core, message_beyond, own_strip = call(
        main_kernel,
        [
            shape(modes * side, side),
            shape(modes * side + strip + 8, side),
            shape(strip + 8, side),
            shape(strip, side),
        ],
        1,
        8,
        [
            pltpu.VMEM((4, 2 * half + rows, 2 * half + cols), f32),
            pltpu.VMEM((4, 2 * half + rows, side), f32),
        ],
    )(place, obj_field, other, beyond, from_left, from_right, probe, patterns, tabs)

    from_core = lax.ppermute(message_core, "core", swap)
    from_beyond = lax.ppermute(message_beyond, ROW, pairs)

    n_yx = lax.axis_size(("y", "x"))
    n_z = lax.axis_size(("zh", "zl"))
    total = modes * side
    chunk = total // n_yx
    summed = keep + from_core[:total]
    spread = lax.all_to_all(summed.reshape(n_yx, chunk, side), ("y", "x"), 0, 0)

    edge = shape(2, rows, side)
    centre, grad_left, grad_right = call(
        merge_kernel, [shape(2, 2, rows, cols), edge, edge], 1, 3
    )(place, own_strip, from_core, from_beyond)
    part = jnp.sum(spread, axis=0)
    part, grad_left, grad_right = lax.optimization_barrier((part, grad_left, grad_right))
    got_left = lax.ppermute(grad_right, COL, chain(n_col, 1))
    got_right = lax.ppermute(grad_left, COL, chain(n_col, -1))
    part = lax.all_to_all(jnp.broadcast_to(part, (n_z, chunk, side)), ("zh", "zl"), 0, 0)
    part = jnp.sum(part, axis=0)
    part, got_left, got_right = lax.optimization_barrier((part, got_left, got_right))
    whole = lax.all_to_all(jnp.broadcast_to(part, (n_yx, chunk, side)), ("y", "x"), 0, 0)
    whole = whole.reshape(modes, side, side)
    facing = lax.ppermute(whole, "core", swap)
    first = core == 0
    probe_grad = jnp.stack([jnp.where(first, whole, facing), jnp.where(first, facing, whole)])

    obj_grad = call(finish_kernel, shape(2, 2, rows, cols), 0, 3)(centre, got_left, got_right)
    return (obj_grad, probe_grad)


def solution(mesh):
    fine = Mesh(
        mesh.devices.reshape(8, 2, 2, 4, 4), ("y", "zh", "core", "x", "zl")
    )
    return jax.shard_map(
        body,
        mesh=fine,
        in_specs=(
            P(None, None, ROW, COL),
            P(),
            P(ROW, COL, None, None),
            P(ROW, COL),
            P(ROW, COL, None, None, None),
        ),
        out_specs=(P(None, None, ROW, COL), P()),
        check_vma=False,
    )
```

```python
import functools
import math

import jax
import jax.numpy as jnp
import ml_dtypes
import numpy as np
from jax import lax
from jax.experimental import pallas as pl
from jax.experimental.pallas import tpu as pltpu
from jax.sharding import Mesh
from jax.sharding import PartitionSpec as P

PHASE_COEF = 20.0
LOSS_WEIGHT = 0.125
ROW = ("y", "zh", "core")
COL = ("x", "zl")
VMEM_LIMIT = 48 * 1024 * 1024
TILE_COLS = 256


def split_bf16(table):
    high = table.astype(np.float32).astype(ml_dtypes.bfloat16)
    low = (table - high.astype(np.float64)).astype(np.float32).astype(ml_dtypes.bfloat16)
    return high, low


def tables(side):
    counter = np.arange(side)
    phase = 2.0 * math.pi / side * (counter[:, None] * counter[None, :] % side)
    fourier = np.exp(-1j * phase) / math.sqrt(side)
    spatial = ((counter + side // 2) % side - side // 2) / side
    factor = np.exp(-1j * PHASE_COEF * spatial * spatial)
    propagate = np.conj(fourier) @ (factor[:, None] * fourier)
    propagate = 0.5 * (propagate + propagate.T)
    parts = []
    for matrix in (propagate, fourier):
        for block in (matrix.real, matrix.imag, -matrix.imag):
            parts += split_bf16(block)
    return np.stack(parts)


def on_sides(tabs, which):
    def block(n, part):
        return tabs[6 * which + 2 * n + part]

    def square(a, b, c, d, part):
        return jnp.concatenate(
            [
                jnp.concatenate([block(a, part), block(b, part)], axis=1),
                jnp.concatenate([block(c, part), block(d, part)], axis=1),
            ],
            axis=0,
        )

    right = tuple(square(0, 1, 2, 0, part) for part in range(2))
    left = tuple(square(0, 2, 1, 0, part) for part in range(2))
    return right, left


def split(value):
    high = value.astype(jnp.bfloat16)
    low = (value - high.astype(jnp.float32)).astype(jnp.bfloat16)
    return high, low


def product(left, right):
    (left_high, left_low), (right_high, right_low) = left, right
    dot = functools.partial(jnp.dot, preferred_element_type=jnp.float32)
    return dot(left_high, right_high) + (dot(left_low, right_high) + dot(left_high, right_low))


def two_sided(real, imaginary, right, left):
    side = real[0].shape[0]
    modes = len(real)
    stacked = jnp.concatenate(
        [jnp.concatenate([r, i], axis=1) for r, i in zip(real, imaginary)], axis=0
    )
    middle = product(split(stacked), right)
    blocks = [middle[m * side : (m + 1) * side] for m in range(modes)]
    spread = jnp.concatenate(
        [
            jnp.concatenate([b[:, :side] for b in blocks], axis=1),
            jnp.concatenate([b[:, side:] for b in blocks], axis=1),
        ],
        axis=0,
    )
    out = product(left, split(spread))
    return (
        [out[:side, m * side : (m + 1) * side] for m in range(modes)],
        [out[side:, m * side : (m + 1) * side] for m in range(modes)],
    )


def times(ar, ai, br, bi):
    return ar * br - ai * bi, ar * bi + ai * br


def times_conj(ar, ai, br, bi):
    return ar * br + ai * bi, ar * bi - ai * br


def model(window, probe, pattern, weight, tabs):
    (o0r, o1r), (o0i, o1i) = window
    qr, qi = probe
    modes = len(qr)
    prop_right, prop_left = on_sides(tabs, 0)
    four_right, four_left = on_sides(tabs, 1)
    e0 = [times(qr[m], qi[m], o0r, o0i) for m in range(modes)]
    a1r, a1i = two_sided([e[0] for e in e0], [e[1] for e in e0], prop_right, prop_left)
    e1 = [times(a1r[m], a1i[m], o1r, o1i) for m in range(modes)]
    gr, gi = two_sided([e[0] for e in e1], [e[1] for e in e1], four_right, four_left)
    intensity = gr[0] * gr[0] + gi[0] * gi[0]
    for m in range(1, modes):
        intensity = intensity + (gr[m] * gr[m] + gi[m] * gi[m])
    residue = (intensity - pattern) * (4.0 * LOSS_WEIGHT * weight)
    br, bi = two_sided(
        [residue * g for g in gr], [residue * g for g in gi], four_left, four_right
    )
    grad1 = [times_conj(a1r[m], a1i[m], br[m], bi[m]) for m in range(modes)]
    back = [times_conj(o1r, o1i, br[m], bi[m]) for m in range(modes)]
    cr, ci = two_sided([b[0] for b in back], [b[1] for b in back], prop_left, prop_right)
    grad0 = [times_conj(qr[m], qi[m], cr[m], ci[m]) for m in range(modes)]
    probe_grad = [times_conj(o0r, o0i, cr[m], ci[m]) for m in range(modes)]

    def over_modes(terms, part):
        return functools.reduce(lambda a, b: a + b, [t[part] for t in terms])

    window_grad = [
        [over_modes(grad0, 0), over_modes(grad1, 0)],
        [over_modes(grad0, 1), over_modes(grad1, 1)],
    ]
    return window_grad, probe_grad


def place_of(scan, rows, cols, half):
    row = scan[0] - (lax.axis_index(ROW) * rows - half)
    col = scan[1] - (lax.axis_index(COL) * cols - half)
    return row, col


def strips_at(half):
    core = lax.axis_index("core")
    return pl.multiple_of((1 - core) * 2 * half, 8), pl.multiple_of(core * 2 * half, 8)


def cut(wide, col, side):
    length = wide.shape[1]
    return pltpu.roll(wide, lax.rem(length - col, length), 1)[:, :side]


def edges_kernel(own, to_left, to_right):
    half = own.shape[2]
    cols = own.shape[3]
    for layer in range(2):
        for part in range(2):
            mine = pl.ds(part * half, half)
            to_left[layer, :, mine] = own[part, layer, :, 0:half]
            to_right[layer, :, mine] = own[part, layer, :, cols - half : cols]


def widened(own, from_left, from_right, part, layer):
    half = own.shape[2]
    mine = pl.ds(part * half, half)
    return jnp.concatenate(
        [from_left[layer, :, mine], own[part, layer], from_right[layer, :, mine]], axis=1
    )


def beyond_kernel(scan_beyond, own, from_left, from_right, to_beyond):
    rows, cols = own.shape[2], own.shape[3]
    side = to_beyond.shape[1]
    half = side // 2
    unused, col = place_of(scan_beyond, rows, cols, half)
    col = jnp.clip(col, 0, cols - 1)
    for layer in range(2):
        for part in range(2):
            at = pl.ds((2 * part + layer) * rows, rows)
            wide = widened(own, from_left, from_right, part, layer)
            to_beyond[at, :] = cut(wide, col, side)


def core_kernel(own, from_left, from_right, to_core):
    rows = own.shape[2]
    for layer in range(2):
        for part in range(2):
            at = pl.ds((2 * part + layer) * rows, rows)
            to_core[at, :] = widened(own, from_left, from_right, part, layer)


def near_kernel(scan, own, from_left, from_right, other, probe, pattern, tabs, near):
    rows, cols = own.shape[2], own.shape[3]
    side = near.shape[2]
    half = side // 2
    unused, col = place_of(scan, rows, cols, half)
    for layer in range(2):
        for part in range(2):
            plane = 2 * part + layer
            near[plane, 0:rows, :] = cut(widened(own, from_left, from_right, part, layer), col, side)
            near[plane, rows : 2 * rows, :] = cut(other[pl.ds(plane * rows, rows), :], col, side)


def main_kernel(
    scan, live, near, beyond, probe, pattern, tabs,
    keep, message_core, message_beyond, own_strip, column, shifted,
):
    side = probe.shape[-1]
    half = side // 2
    rows = beyond.shape[0] // 4
    cols = TILE_COLS
    modes = probe.shape[1]
    row, col = place_of(scan, rows, cols, half)
    other_at, beyond_at = strips_at(half)
    for plane in range(4):
        column[plane, half : half + rows, :] = near[plane, 0:rows, :]
        column[plane, pl.ds(other_at, rows), :] = near[plane, rows : 2 * rows, :]
        column[plane, pl.ds(beyond_at, rows), :] = beyond[pl.ds(plane * rows, rows), :]
    tall = side + 8
    step = lax.rem(row, 8)
    base_row = pl.multiple_of(row - step, 8)

    def window_of(plane):
        high = column[plane, pl.ds(base_row, tall), :]
        return pltpu.roll(high, lax.rem(tall - step, tall), 0)[:side]

    window = [[window_of(2 * part + layer) for layer in range(2)] for part in range(2)]
    fields = [[probe[part, m] for m in range(modes)] for part in range(2)]
    weight = (live[0] > 0).astype(jnp.float32)
    window_grad, probe_grad = model(window, fields, pattern[0, 0, 0], weight, tabs)
    first = lax.axis_index("core") == 0
    for m in range(modes):
        at = pl.ds(m * side, side)
        real, imaginary = probe_grad[m]
        keep[at, :] = jnp.where(first, real, imaginary)
        message_core[at, :] = jnp.where(first, imaginary, real)
    base = modes * side
    shifted[...] = jnp.zeros_like(shifted)
    for part in range(2):
        for layer in range(2):
            plane = 2 * part + layer
            padded = jnp.concatenate(
                [window_grad[part][layer], jnp.zeros((8, side), jnp.float32)], axis=0
            )
            shifted[plane, pl.ds(base_row, tall), :] = pltpu.roll(padded, step, 0)
            at = pl.ds(plane * rows, rows)
            message_core[pl.ds(base + plane * rows, rows), :] = shifted[plane, pl.ds(other_at, rows), :]
            message_beyond[at, :] = shifted[plane, pl.ds(beyond_at, rows), :]
            own_strip[at, :] = shifted[plane, half : half + rows, :]
    offset = jnp.full((8, side), col.astype(jnp.float32))
    message_core[pl.ds(base + 4 * rows, 8), :] = offset
    message_beyond[pl.ds(4 * rows, 8), :] = offset


def merge_kernel(scan, own_strip, from_core, from_beyond, centre, to_left, to_right):
    side = own_strip.shape[1]
    half = side // 2
    rows = centre.shape[2]
    cols = centre.shape[3]
    wide = cols + side
    base = from_core.shape[0] - from_beyond.shape[0]
    core_col = jnp.max(from_core[pl.ds(base + 4 * rows, 8), :]).astype(jnp.int32)
    beyond_col = jnp.max(from_beyond[pl.ds(4 * rows, 8), :]).astype(jnp.int32)
    unused, own_col = place_of(scan, rows, cols, half)
    gap = jnp.zeros((rows, cols), jnp.float32)

    def placed(strip, col):
        return pltpu.roll(jnp.concatenate([strip, gap], axis=1), col, 1)

    for layer in range(2):
        for part in range(2):
            plane = 2 * part + layer
            total = placed(own_strip[pl.ds(plane * rows, rows), :], own_col)
            total = total + placed(from_core[pl.ds(base + plane * rows, rows), :], core_col)
            total = total + placed(from_beyond[pl.ds(plane * rows, rows), :], beyond_col)
            centre[part, layer] = total[:, half : half + cols]
            mine = pl.ds(part * half, half)
            to_left[layer, :, mine] = total[:, :half]
            to_right[layer, :, mine] = total[:, wide - half :]


def finish_kernel(centre, from_left, from_right, out):
    half = centre.shape[2]
    cols = centre.shape[3]
    for layer in range(2):
        for part in range(2):
            mine = pl.ds(part * half, half)
            value = centre[part, layer]
            out[part, layer] = value
            out[part, layer, :, 0:half] = value[:, :half] + from_left[layer, :, mine]
            out[part, layer, :, cols - half : cols] = value[:, cols - half :] + from_right[layer, :, mine]


def call(kernel, out_shape, n_scalars, n_in, scratch=(), cost=None):
    many = isinstance(out_shape, (list, tuple))
    vmem = pl.BlockSpec(memory_space=pltpu.VMEM)
    return pl.pallas_call(
        kernel,
        out_shape=out_shape,
        in_specs=[pl.BlockSpec(memory_space=pltpu.SMEM)] * n_scalars + [vmem] * n_in,
        out_specs=[vmem] * len(out_shape) if many else vmem,
        scratch_shapes=list(scratch),
        compiler_params=pltpu.CompilerParams(vmem_limit_bytes=VMEM_LIMIT),
        cost_estimate=cost,
    )


def chain(n, step):
    return [(i, i + step) for i in range(n) if 0 <= i + step < n]


def body(obj_field, probe, scan_pos, live_count, patterns):
    side = probe.shape[2]
    modes = probe.shape[1]
    half = side // 2
    rows, cols = obj_field.shape[2], obj_field.shape[3]
    n_row, n_col = lax.axis_size(ROW), lax.axis_size(COL)
    f32 = jnp.float32
    core = lax.axis_index("core")
    scan = scan_pos.reshape(2)
    live = live_count.reshape(1)
    swap = [(0, 1), (1, 0)]
    pairs = [(i, i + 1) for i in range(1, n_row - 1, 2)]
    pairs = pairs + [(j, i) for i, j in pairs]
    strip = 4 * rows

    def shape(*dims):
        return jax.ShapeDtypeStruct(dims, f32)

    scan_beyond = lax.ppermute(scan, ROW, pairs)
    edge = shape(2, rows, side)
    to_left, to_right = call(edges_kernel, [edge, edge], 0, 1)(obj_field)
    from_left = lax.ppermute(to_right, COL, chain(n_col, 1))
    from_right = lax.ppermute(to_left, COL, chain(n_col, -1))
    to_beyond = call(beyond_kernel, shape(strip, side), 1, 3)(
        scan_beyond, obj_field, from_left, from_right
    )
    beyond = lax.ppermute(to_beyond, ROW, pairs)
    to_beyond_first, own_edge = lax.optimization_barrier((to_beyond, from_left))
    small = pl.CostEstimate(flops=1000, bytes_accessed=1000, transcendentals=0)
    to_core = call(core_kernel, shape(strip, 2 * half + cols), 0, 3, cost=small)(
        obj_field, own_edge, from_right
    )
    other = lax.ppermute(to_core, "core", swap)
    tabs = jnp.asarray(tables(side))
    near = call(near_kernel, shape(4, 2 * rows, side), 1, 7, cost=small)(
        scan, obj_field, from_left, from_right, other, probe, patterns, tabs
    )
    near, beyond = lax.optimization_barrier((near, beyond))
    tall = pltpu.VMEM((4, 2 * half + rows, side), f32)
    keep, message_core, message_beyond, own_strip = call(
        main_kernel,
        [
            shape(modes * side, side),
            shape(modes * side + strip + 8, side),
            shape(strip + 8, side),
            shape(strip, side),
        ],
        2,
        5,
        [tall, tall],
    )(scan, live, near, beyond, probe, patterns, tabs)

    from_core = lax.ppermute(message_core, "core", swap)
    from_beyond = lax.ppermute(message_beyond, ROW, pairs)

    n_yx = lax.axis_size(("y", "x"))
    n_z = lax.axis_size(("zh", "zl"))
    total = modes * side
    chunk = total // n_yx
    summed = keep + from_core[:total]
    spread = lax.all_to_all(summed.reshape(n_yx, chunk, side), ("y", "x"), 0, 0)

    centre, grad_left, grad_right = call(
        merge_kernel, [shape(2, 2, rows, cols), edge, edge], 1, 3
    )(scan, own_strip, from_core, from_beyond)
    part = jnp.sum(spread, axis=0)
    part = lax.all_to_all(jnp.broadcast_to(part, (n_z, chunk, side)), ("zh", "zl"), 0, 0)
    part = jnp.sum(part, axis=0)
    got_left = lax.ppermute(grad_right, COL, chain(n_col, 1))
    part, got_left, grad_left = lax.optimization_barrier((part, got_left, grad_left))
    got_right = lax.ppermute(grad_left, COL, chain(n_col, -1))
    whole = lax.all_to_all(jnp.broadcast_to(part, (n_yx, chunk, side)), ("y", "x"), 0, 0)
    whole, got_right = lax.optimization_barrier((whole, got_right))
    whole = whole.reshape(modes, side, side)
    facing = lax.ppermute(whole, "core", swap)
    first = core == 0
    probe_grad = jnp.stack([jnp.where(first, whole, facing), jnp.where(first, facing, whole)])

    obj_grad = call(finish_kernel, shape(2, 2, rows, cols), 0, 3)(centre, got_left, got_right)
    return (obj_grad, probe_grad)


def solution(mesh):
    fine = Mesh(
        mesh.devices.reshape(8, 2, 2, 4, 4), ("y", "zh", "core", "x", "zl")
    )
    return jax.shard_map(
        body,
        mesh=fine,
        in_specs=(
            P(None, None, ROW, COL),
            P(),
            P(ROW, COL, None, None),
            P(ROW, COL),
            P(ROW, COL, None, None, None),
        ),
        out_specs=(P(None, None, ROW, COL), P()),
        check_vma=False,
    )
```

```python
import functools
import math

import jax
import jax.numpy as jnp
import ml_dtypes
import numpy as np
from jax import lax
from jax.experimental import pallas as pl
from jax.experimental.pallas import tpu as pltpu
from jax.sharding import Mesh
from jax.sharding import PartitionSpec as P

PHASE_COEF = 20.0
LOSS_WEIGHT = 0.125
ROW = ("y", "zh", "core")
COL = ("x", "zl")
VMEM_LIMIT = 48 * 1024 * 1024
TILE_COLS = 256


def split_bf16(table):
    high = table.astype(np.float32).astype(ml_dtypes.bfloat16)
    low = (table - high.astype(np.float64)).astype(np.float32).astype(ml_dtypes.bfloat16)
    return high, low


def tables(side):
    counter = np.arange(side)
    phase = 2.0 * math.pi / side * (counter[:, None] * counter[None, :] % side)
    fourier = np.exp(-1j * phase) / math.sqrt(side)
    spatial = ((counter + side // 2) % side - side // 2) / side
    factor = np.exp(-1j * PHASE_COEF * spatial * spatial)
    propagate = np.conj(fourier) @ (factor[:, None] * fourier)
    propagate = 0.5 * (propagate + propagate.T)
    parts = []
    for matrix in (propagate, fourier):
        for block in (matrix.real, matrix.imag, -matrix.imag):
            parts += split_bf16(block)
    return np.stack(parts)


def on_sides(tabs, which):
    def block(n, part):
        return tabs[6 * which + 2 * n + part]

    def square(a, b, c, d, part):
        return jnp.concatenate(
            [
                jnp.concatenate([block(a, part), block(b, part)], axis=1),
                jnp.concatenate([block(c, part), block(d, part)], axis=1),
            ],
            axis=0,
        )

    right = tuple(square(0, 1, 2, 0, part) for part in range(2))
    left = tuple(square(0, 2, 1, 0, part) for part in range(2))
    return right, left


def split(value):
    high = value.astype(jnp.bfloat16)
    low = (value - high.astype(jnp.float32)).astype(jnp.bfloat16)
    return high, low


def product(left, right):
    (left_high, left_low), (right_high, right_low) = left, right
    dot = functools.partial(jnp.dot, preferred_element_type=jnp.float32)
    return dot(left_high, right_high) + (dot(left_low, right_high) + dot(left_high, right_low))


def two_sided(real, imaginary, right, left):
    side = real[0].shape[0]
    modes = len(real)
    stacked = jnp.concatenate(
        [jnp.concatenate([r, i], axis=1) for r, i in zip(real, imaginary)], axis=0
    )
    middle = product(split(stacked), right)
    blocks = [middle[m * side : (m + 1) * side] for m in range(modes)]
    spread = jnp.concatenate(
        [
            jnp.concatenate([b[:, :side] for b in blocks], axis=1),
            jnp.concatenate([b[:, side:] for b in blocks], axis=1),
        ],
        axis=0,
    )
    out = product(left, split(spread))
    return (
        [out[:side, m * side : (m + 1) * side] for m in range(modes)],
        [out[side:, m * side : (m + 1) * side] for m in range(modes)],
    )


def times(ar, ai, br, bi):
    return ar * br - ai * bi, ar * bi + ai * br


def times_conj(ar, ai, br, bi):
    return ar * br + ai * bi, ar * bi - ai * br


def model(window, probe, pattern, weight, tabs):
    (o0r, o1r), (o0i, o1i) = window
    qr, qi = probe
    modes = len(qr)
    prop_right, prop_left = on_sides(tabs, 0)
    four_right, four_left = on_sides(tabs, 1)
    e0 = [times(qr[m], qi[m], o0r, o0i) for m in range(modes)]
    a1r, a1i = two_sided([e[0] for e in e0], [e[1] for e in e0], prop_right, prop_left)
    e1 = [times(a1r[m], a1i[m], o1r, o1i) for m in range(modes)]
    gr, gi = two_sided([e[0] for e in e1], [e[1] for e in e1], four_right, four_left)
    intensity = gr[0] * gr[0] + gi[0] * gi[0]
    for m in range(1, modes):
        intensity = intensity + (gr[m] * gr[m] + gi[m] * gi[m])
    residue = (intensity - pattern) * (4.0 * LOSS_WEIGHT * weight)
    br, bi = two_sided(
        [residue * g for g in gr], [residue * g for g in gi], four_left, four_right
    )
    grad1 = [times_conj(a1r[m], a1i[m], br[m], bi[m]) for m in range(modes)]
    back = [times_conj(o1r, o1i, br[m], bi[m]) for m in range(modes)]
    cr, ci = two_sided([b[0] for b in back], [b[1] for b in back], prop_left, prop_right)
    grad0 = [times_conj(qr[m], qi[m], cr[m], ci[m]) for m in range(modes)]
    probe_grad = [times_conj(o0r, o0i, cr[m], ci[m]) for m in range(modes)]

    def over_modes(terms, part):
        return functools.reduce(lambda a, b: a + b, [t[part] for t in terms])

    window_grad = [
        [over_modes(grad0, 0), over_modes(grad1, 0)],
        [over_modes(grad0, 1), over_modes(grad1, 1)],
    ]
    return window_grad, probe_grad


def place_of(scan, rows, cols, half):
    row = scan[0] - (lax.axis_index(ROW) * rows - half)
    col = scan[1] - (lax.axis_index(COL) * cols - half)
    return row, col


def strips_at(half):
    core = lax.axis_index("core")
    return pl.multiple_of((1 - core) * 2 * half, 8), pl.multiple_of(core * 2 * half, 8)


def even_col():
    return lax.rem(lax.axis_index(COL), 2) == 0


def fill(frame, own, with_even, with_odd, part, layer):
    side = with_even.shape[2]
    half = side // 2
    cols = own.shape[3]
    plane = 2 * part + layer
    left = jnp.where(even_col(), with_odd[layer], with_even[layer])
    right = jnp.where(even_col(), with_even[layer], with_odd[layer])
    if part:
        left, right = pltpu.roll(left, half, 1), pltpu.roll(right, half, 1)
    frame[plane, :, 0:side] = left
    frame[plane, :, side : side + cols] = own[part, layer]
    frame[plane, :, side + cols :] = right


def cut(frame, plane, at, side):
    step = lax.rem(at, side)
    wide = frame[plane, :, pl.ds(pl.multiple_of(at - step, side), 2 * side)]
    return pltpu.roll(wide, lax.rem(2 * side - step, 2 * side), 1)[:, :side]


def edges_kernel(own, with_even, with_odd):
    rows, cols = own.shape[2], own.shape[3]
    side = with_even.shape[2]
    half = side // 2
    inner = lax.broadcasted_iota(jnp.int32, (rows, side), 1) < half
    for layer in range(2):
        real, imaginary = own[0, layer], own[1, layer]
        left = jnp.where(inner, real[:, :side], pltpu.roll(imaginary[:, :side], half, 1))
        right = jnp.where(inner, pltpu.roll(imaginary[:, cols - side :], half, 1), real[:, cols - side :])
        with_even[layer] = jnp.where(even_col(), right, left)
        with_odd[layer] = jnp.where(even_col(), left, right)


def beyond_kernel(scan_beyond, own, with_even, with_odd, to_beyond, frame):
    rows, cols = own.shape[2], own.shape[3]
    side = to_beyond.shape[1]
    half = side // 2
    unused, col = place_of(scan_beyond, rows, cols, half)
    col = jnp.clip(col, 0, cols - 1)
    for layer in range(2):
        for part in range(2):
            plane = 2 * part + layer
            fill(frame, own, with_even, with_odd, part, layer)
            to_beyond[pl.ds(plane * rows, rows), :] = cut(frame, plane, col + half, side)


def near_kernel(scan, frame, other, probe, pattern, tabs, near):
    rows, cols = frame.shape[1], frame.shape[2] - 2 * near.shape[2]
    side = near.shape[2]
    half = side // 2
    unused, col = place_of(scan, rows, cols, half)
    for plane in range(4):
        near[plane, 0:rows, :] = cut(frame, plane, col + half, side)
        near[plane, rows : 2 * rows, :] = cut(other, plane, col + half, side)


def main_kernel(
    scan, live, near, beyond, probe, pattern, tabs,
    keep, message_core, message_beyond, own_strip, column, shifted,
):
    side = probe.shape[-1]
    half = side // 2
    rows = beyond.shape[0] // 4
    cols = TILE_COLS
    modes = probe.shape[1]
    row, col = place_of(scan, rows, cols, half)
    other_at, beyond_at = strips_at(half)
    for plane in range(4):
        column[plane, half : half + rows, :] = near[plane, 0:rows, :]
        column[plane, pl.ds(other_at, rows), :] = near[plane, rows : 2 * rows, :]
        column[plane, pl.ds(beyond_at, rows), :] = beyond[pl.ds(plane * rows, rows), :]
    tall = side + 8
    step = lax.rem(row, 8)
    base_row = pl.multiple_of(row - step, 8)

    def window_of(plane):
        high = column[plane, pl.ds(base_row, tall), :]
        return pltpu.roll(high, lax.rem(tall - step, tall), 0)[:side]

    window = [[window_of(2 * part + layer) for layer in range(2)] for part in range(2)]
    fields = [[probe[part, m] for m in range(modes)] for part in range(2)]
    weight = (live[0] > 0).astype(jnp.float32)
    window_grad, probe_grad = model(window, fields, pattern[0, 0, 0], weight, tabs)
    first = lax.axis_index("core") == 0
    for m in range(modes):
        at = pl.ds(m * side, side)
        real, imaginary = probe_grad[m]
        keep[at, :] = jnp.where(first, real, imaginary)
        message_core[at, :] = jnp.where(first, imaginary, real)
    base = modes * side
    shifted[...] = jnp.zeros_like(shifted)
    for part in range(2):
        for layer in range(2):
            plane = 2 * part + layer
            padded = jnp.concatenate(
                [window_grad[part][layer], jnp.zeros((8, side), jnp.float32)], axis=0
            )
            shifted[plane, pl.ds(base_row, tall), :] = pltpu.roll(padded, step, 0)
            at = pl.ds(plane * rows, rows)
            message_core[pl.ds(base + plane * rows, rows), :] = shifted[plane, pl.ds(other_at, rows), :]
            message_beyond[at, :] = shifted[plane, pl.ds(beyond_at, rows), :]
            own_strip[at, :] = shifted[plane, half : half + rows, :]
    offset = jnp.full((8, side), col.astype(jnp.float32))
    message_core[pl.ds(base + 4 * rows, 8), :] = offset
    message_beyond[pl.ds(4 * rows, 8), :] = offset


def merge_kernel(scan, own_strip, from_core, from_beyond, centre, with_even, with_odd, frame):
    side = own_strip.shape[1]
    half = side // 2
    rows = centre.shape[2]
    cols = centre.shape[3]
    base = from_core.shape[0] - from_beyond.shape[0]
    core_col = jnp.max(from_core[pl.ds(base + 4 * rows, 8), :]).astype(jnp.int32)
    beyond_col = jnp.max(from_beyond[pl.ds(4 * rows, 8), :]).astype(jnp.int32)
    unused, own_col = place_of(scan, rows, cols, half)
    lane = lax.broadcasted_iota(jnp.int32, (rows, side), 1)
    zero = jnp.zeros((rows, side), jnp.float32)
    frame[...] = jnp.zeros_like(frame)
    for source, first, col in (
        (own_strip, 0, own_col),
        (from_core, base, jnp.clip(core_col, 0, cols - 1)),
        (from_beyond, 0, jnp.clip(beyond_col, 0, cols - 1)),
    ):
        at = col + half
        step = lax.rem(at, side)
        near = pl.multiple_of(at - step, side)
        here, there = pl.ds(near, side), pl.ds(pl.multiple_of(near + side, side), side)
        for plane in range(4):
            strip = pltpu.roll(source[pl.ds(first + plane * rows, rows), :], step, 1)
            frame[plane, :, here] += jnp.where(lane >= step, strip, zero)
            frame[plane, :, there] += jnp.where(lane < step, strip, zero)
    inner = lane < half
    for layer in range(2):
        real, imaginary = layer, 2 + layer
        left = jnp.where(inner, pltpu.roll(frame[imaginary, :, 0:side], half, 1), frame[real, :, 0:side])
        right = jnp.where(inner, frame[real, :, side + cols :], pltpu.roll(frame[imaginary, :, side + cols :], half, 1))
        with_even[layer] = jnp.where(even_col(), right, left)
        with_odd[layer] = jnp.where(even_col(), left, right)
        centre[0, layer] = frame[real, :, side : side + cols]
        centre[1, layer] = frame[imaginary, :, side : side + cols]


def finish_kernel(centre, with_even, with_odd, out):
    rows, cols = centre.shape[2], centre.shape[3]
    side = with_even.shape[2]
    half = side // 2
    inner = lax.broadcasted_iota(jnp.int32, (rows, side), 1) < half
    zero = jnp.zeros((rows, side), jnp.float32)
    for layer in range(2):
        left = jnp.where(even_col(), with_odd[layer], with_even[layer])
        right = jnp.where(even_col(), with_even[layer], with_odd[layer])
        for part in range(2):
            if part:
                left, right = pltpu.roll(left, half, 1), pltpu.roll(right, half, 1)
            value = centre[part, layer]
            out[part, layer, :, 0:side] = value[:, :side] + jnp.where(inner, left, zero)
            out[part, layer, :, cols - side :] = value[:, cols - side :] + jnp.where(inner, zero, right)


def call(kernel, out_shape, n_scalars, n_in, scratch=(), cost=None):
    many = isinstance(out_shape, (list, tuple))
    vmem = pl.BlockSpec(memory_space=pltpu.VMEM)
    return pl.pallas_call(
        kernel,
        out_shape=out_shape,
        in_specs=[pl.BlockSpec(memory_space=pltpu.SMEM)] * n_scalars + [vmem] * n_in,
        out_specs=[vmem] * len(out_shape) if many else vmem,
        scratch_shapes=list(scratch),
        compiler_params=pltpu.CompilerParams(vmem_limit_bytes=VMEM_LIMIT),
        cost_estimate=cost,
    )


def both_ways(pairs):
    return pairs + [(j, i) for i, j in pairs]


def body(obj_field, probe, scan_pos, live_count, patterns):
    side = probe.shape[2]
    modes = probe.shape[1]
    half = side // 2
    rows, cols = obj_field.shape[2], obj_field.shape[3]
    n_row, n_col = lax.axis_size(ROW), lax.axis_size(COL)
    f32 = jnp.float32
    core = lax.axis_index("core")
    scan = scan_pos.reshape(2)
    live = live_count.reshape(1)
    swap = [(0, 1), (1, 0)]
    pairs = both_ways([(i, i + 1) for i in range(1, n_row - 1, 2)])
    even_pairs = both_ways([(i, i + 1) for i in range(0, n_col - 1, 2)])
    odd_pairs = both_ways([(i, i + 1) for i in range(1, n_col - 1, 2)])
    strip = 4 * rows

    def shape(*dims):
        return jax.ShapeDtypeStruct(dims, f32)

    scan_beyond = lax.ppermute(scan, ROW, pairs)
    edge = shape(2, rows, side)
    to_even, to_odd = call(edges_kernel, [edge, edge], 0, 1)(obj_field)
    with_even = lax.ppermute(to_even, COL, even_pairs)
    with_odd = lax.ppermute(to_odd, COL, odd_pairs)
    to_beyond, frame = call(
        beyond_kernel, [shape(strip, side), shape(4, rows, cols + 2 * side)], 1, 3
    )(scan_beyond, obj_field, with_even, with_odd)
    other = lax.ppermute(frame, "core", swap)
    beyond = lax.ppermute(to_beyond, ROW, pairs)
    tabs = jnp.asarray(tables(side))
    small = pl.CostEstimate(flops=1000, bytes_accessed=1000, transcendentals=0)
    near = call(near_kernel, shape(4, 2 * rows, side), 1, 5, cost=small)(
        scan, frame, other, probe, patterns, tabs
    )
    near, beyond = lax.optimization_barrier((near, beyond))
    tall = pltpu.VMEM((4, 2 * half + rows, side), f32)
    keep, message_core, message_beyond, own_strip = call(
        main_kernel,
        [
            shape(modes * side, side),
            shape(modes * side + strip + 8, side),
            shape(strip + 8, side),
            shape(strip, side),
        ],
        2,
        5,
        [tall, tall],
    )(scan, live, near, beyond, probe, patterns, tabs)

    from_core = lax.ppermute(message_core, "core", swap)
    from_beyond = lax.ppermute(message_beyond, ROW, pairs)

    n_yx = lax.axis_size(("y", "x"))
    n_z = lax.axis_size(("zh", "zl"))
    total = modes * side
    chunk = total // n_yx
    summed = keep + from_core[:total]
    spread = lax.all_to_all(summed.reshape(n_yx, chunk, side), ("y", "x"), 0, 0)

    centre, grad_even, grad_odd = call(
        merge_kernel,
        [shape(2, 2, rows, cols), edge, edge],
        1,
        3,
        [pltpu.VMEM((4, rows, cols + 2 * side), f32)],
    )(scan, own_strip, from_core, from_beyond)
    part = jnp.sum(spread, axis=0)
    part = lax.all_to_all(jnp.broadcast_to(part, (n_z, chunk, side)), ("zh", "zl"), 0, 0)
    part = jnp.sum(part, axis=0)
    got_even = lax.ppermute(grad_even, COL, even_pairs)
    part = jnp.broadcast_to(part, (n_yx, chunk, side))
    part, got_even, grad_odd = lax.optimization_barrier((part, got_even, grad_odd))
    got_odd = lax.ppermute(grad_odd, COL, odd_pairs)
    whole = lax.all_to_all(part, ("y", "x"), 0, 0)
    whole, got_odd = lax.optimization_barrier((whole, got_odd))
    whole = whole.reshape(modes, side, side)
    facing = lax.ppermute(whole, "core", swap)
    first = core == 0
    probe_grad = jnp.stack([jnp.where(first, whole, facing), jnp.where(first, facing, whole)])

    obj_grad = call(finish_kernel, shape(2, 2, rows, cols), 0, 3)(centre, got_even, got_odd)
    return (obj_grad, probe_grad)


def solution(mesh):
    fine = Mesh(
        mesh.devices.reshape(8, 2, 2, 4, 4), ("y", "zh", "core", "x", "zl")
    )
    return jax.shard_map(
        body,
        mesh=fine,
        in_specs=(
            P(None, None, ROW, COL),
            P(),
            P(ROW, COL, None, None),
            P(ROW, COL),
            P(ROW, COL, None, None, None),
        ),
        out_specs=(P(None, None, ROW, COL), P()),
        check_vma=False,
    )
```

```python
import functools
import math

import jax
import jax.numpy as jnp
import ml_dtypes
import numpy as np
from jax import lax
from jax.experimental import pallas as pl
from jax.experimental.pallas import tpu as pltpu
from jax.sharding import Mesh
from jax.sharding import PartitionSpec as P

PHASE_COEF = 20.0
LOSS_WEIGHT = 0.125
ROW = ("y", "zh", "core")
COL = ("x", "zl")
VMEM_LIMIT = 48 * 1024 * 1024
TILE_COLS = 256


def split_bf16(table):
    high = table.astype(np.float32).astype(ml_dtypes.bfloat16)
    low = (table - high.astype(np.float64)).astype(np.float32).astype(ml_dtypes.bfloat16)
    return high, low


def tables(side):
    counter = np.arange(side)
    phase = 2.0 * math.pi / side * (counter[:, None] * counter[None, :] % side)
    fourier = np.exp(-1j * phase) / math.sqrt(side)
    spatial = ((counter + side // 2) % side - side // 2) / side
    factor = np.exp(-1j * PHASE_COEF * spatial * spatial)
    propagate = np.conj(fourier) @ (factor[:, None] * fourier)
    propagate = 0.5 * (propagate + propagate.T)
    parts = []
    for matrix in (propagate, fourier):
        for block in (matrix.real, matrix.imag, -matrix.imag):
            parts += split_bf16(block)
    return np.stack(parts)


def on_sides(tabs, which):
    def block(n, part):
        return tabs[6 * which + 2 * n + part]

    def square(a, b, c, d, part):
        return jnp.concatenate(
            [
                jnp.concatenate([block(a, part), block(b, part)], axis=1),
                jnp.concatenate([block(c, part), block(d, part)], axis=1),
            ],
            axis=0,
        )

    right = tuple(square(0, 1, 2, 0, part) for part in range(2))
    left = tuple(square(0, 2, 1, 0, part) for part in range(2))
    return right, left


def split(value):
    high = value.astype(jnp.bfloat16)
    low = (value - high.astype(jnp.float32)).astype(jnp.bfloat16)
    return high, low


def product(left, right):
    (left_high, left_low), (right_high, right_low) = left, right
    dot = functools.partial(jnp.dot, preferred_element_type=jnp.float32)
    return dot(left_high, right_high) + (dot(left_low, right_high) + dot(left_high, right_low))


def two_sided(real, imaginary, right, left):
    side = real[0].shape[0]
    modes = len(real)
    stacked = jnp.concatenate(
        [jnp.concatenate([r, i], axis=1) for r, i in zip(real, imaginary)], axis=0
    )
    middle = product(split(stacked), right)
    blocks = [middle[m * side : (m + 1) * side] for m in range(modes)]
    spread = jnp.concatenate(
        [
            jnp.concatenate([b[:, :side] for b in blocks], axis=1),
            jnp.concatenate([b[:, side:] for b in blocks], axis=1),
        ],
        axis=0,
    )
    out = product(left, split(spread))
    return (
        [out[:side, m * side : (m + 1) * side] for m in range(modes)],
        [out[side:, m * side : (m + 1) * side] for m in range(modes)],
    )


def times(ar, ai, br, bi):
    return ar * br - ai * bi, ar * bi + ai * br


def times_conj(ar, ai, br, bi):
    return ar * br + ai * bi, ar * bi - ai * br


def model(window, probe, pattern, weight, tabs):
    (o0r, o1r), (o0i, o1i) = window
    qr, qi = probe
    modes = len(qr)
    prop_right, prop_left = on_sides(tabs, 0)
    four_right, four_left = on_sides(tabs, 1)
    e0 = [times(qr[m], qi[m], o0r, o0i) for m in range(modes)]
    a1r, a1i = two_sided([e[0] for e in e0], [e[1] for e in e0], prop_right, prop_left)
    e1 = [times(a1r[m], a1i[m], o1r, o1i) for m in range(modes)]
    gr, gi = two_sided([e[0] for e in e1], [e[1] for e in e1], four_right, four_left)
    intensity = gr[0] * gr[0] + gi[0] * gi[0]
    for m in range(1, modes):
        intensity = intensity + (gr[m] * gr[m] + gi[m] * gi[m])
    residue = (intensity - pattern) * (4.0 * LOSS_WEIGHT * weight)
    br, bi = two_sided(
        [residue * g for g in gr], [residue * g for g in gi], four_left, four_right
    )
    grad1 = [times_conj(a1r[m], a1i[m], br[m], bi[m]) for m in range(modes)]
    back = [times_conj(o1r, o1i, br[m], bi[m]) for m in range(modes)]
    cr, ci = two_sided([b[0] for b in back], [b[1] for b in back], prop_left, prop_right)
    grad0 = [times_conj(qr[m], qi[m], cr[m], ci[m]) for m in range(modes)]
    probe_grad = [times_conj(o0r, o0i, cr[m], ci[m]) for m in range(modes)]

    def over_modes(terms, part):
        return functools.reduce(lambda a, b: a + b, [t[part] for t in terms])

    window_grad = [
        [over_modes(grad0, 0), over_modes(grad1, 0)],
        [over_modes(grad0, 1), over_modes(grad1, 1)],
    ]
    return window_grad, probe_grad


def place_of(scan, rows, cols, half):
    row = scan[0] - (lax.axis_index(ROW) * rows - half)
    col = scan[1] - (lax.axis_index(COL) * cols - half)
    return row, col


def strips_at(half):
    core = lax.axis_index("core")
    return pl.multiple_of((1 - core) * 2 * half, 8), pl.multiple_of(core * 2 * half, 8)


def even_col():
    return lax.rem(lax.axis_index(COL), 2) == 0


def pack(source, with_even, with_odd, at):
    rows, cols = source.shape[2], source.shape[3]
    side = with_even.shape[2]
    half = side // 2
    inner = lax.broadcasted_iota(jnp.int32, (rows, side), 1) < half
    for layer in range(2):
        real, imaginary = source[0, layer], source[1, layer]
        left = jnp.where(inner, real[:, :side], pltpu.roll(imaginary[:, :side], half, 1))
        right = jnp.where(inner, pltpu.roll(imaginary[:, cols - side :], half, 1), real[:, cols - side :])
        with_even[layer, at, :] = jnp.where(even_col(), right, left)
        with_odd[layer, at, :] = jnp.where(even_col(), left, right)


def pack_near_kernel(own, other, with_even, with_odd):
    rows = own.shape[2]
    pack(own, with_even, with_odd, pl.ds(0, rows))
    pack(other, with_even, with_odd, pl.ds(rows, rows))


def pack_kernel(beyond, near_even, near_odd, with_even, with_odd):
    rows = beyond.shape[2]
    other_at, beyond_at = strips_at(rows)
    pack(beyond, with_even, with_odd, pl.ds(beyond_at, rows))
    for packed, out in ((near_even, with_even), (near_odd, with_odd)):
        for layer in range(2):
            out[layer, rows : 2 * rows, :] = packed[layer, 0:rows, :]
            out[layer, pl.ds(other_at, rows), :] = packed[layer, rows : 2 * rows, :]


def tile_and_step(col, side):
    at = col + side // 2
    step = lax.rem(at, side)
    return (at - step) // side, step


def near_kernel(scan, own, other, beyond, after, probe, pattern, tabs, near):
    rows, cols = own.shape[2], own.shape[3]
    side = near.shape[2]
    half = side // 2
    unused, col = place_of(scan, rows, cols, half)
    tile, step = tile_and_step(col, side)
    other_at, beyond_at = strips_at(half)
    lane = lax.broadcasted_iota(jnp.int32, (rows, side), 1)
    back = lax.rem(side - step, side)
    zero = jnp.zeros((rows, side), jnp.float32)
    for source, first in ((own, half), (other, other_at), (beyond, beyond_at)):
        for layer in range(2):
            for part in range(2):
                a, b = source[part, layer, :, 0:side], source[part, layer, :, side:]
                early = jnp.where(tile == 0, zero, jnp.where(tile == 1, a, b))
                late = jnp.where(tile == 0, a, jnp.where(tile == 1, b, zero))
                near[2 * part + layer, pl.ds(first, rows), :] = jnp.where(
                    lane < side - step, pltpu.roll(early, back, 1), pltpu.roll(late, back, 1)
                )


def main_kernel(
    scan, live, near, with_even, with_odd, probe, pattern, tabs,
    keep, message_core, message_beyond, own_strip, column, shifted,
):
    side = probe.shape[-1]
    half = side // 2
    rows = own_strip.shape[0] // 4
    cols = TILE_COLS
    modes = probe.shape[1]
    row, col = place_of(scan, rows, cols, half)
    other_at, beyond_at = strips_at(half)
    tile, tile_step = tile_and_step(col, side)
    use_even = (tile == 0) != even_col()
    lane = lax.broadcasted_iota(jnp.int32, column.shape[1:], 1)
    from_left = jnp.logical_and(tile == 0, lane < side - tile_step)
    from_right = jnp.logical_and(tile == 2, lane >= side - tile_step)
    margin_lanes = jnp.logical_or(from_left, from_right)
    for layer in range(2):
        margin = jnp.where(use_even, with_even[layer], with_odd[layer])
        for part in range(2):
            plane = 2 * part + layer
            moved = pltpu.roll(margin, lax.rem(side - tile_step + part * half, side), 1)
            column[plane] = jnp.where(margin_lanes, moved, near[plane])
    tall = side + 8
    step = lax.rem(row, 8)
    base_row = pl.multiple_of(row - step, 8)

    def window_of(plane):
        high = column[plane, pl.ds(base_row, tall), :]
        return pltpu.roll(high, lax.rem(tall - step, tall), 0)[:side]

    window = [[window_of(2 * part + layer) for layer in range(2)] for part in range(2)]
    fields = [[probe[part, m] for m in range(modes)] for part in range(2)]
    weight = (live[0] > 0).astype(jnp.float32)
    window_grad, probe_grad = model(window, fields, pattern[0, 0, 0], weight, tabs)
    first = lax.axis_index("core") == 0
    for m in range(modes):
        at = pl.ds(m * side, side)
        real, imaginary = probe_grad[m]
        keep[at, :] = jnp.where(first, real, imaginary)
        message_core[at, :] = jnp.where(first, imaginary, real)
    base = modes * side
    shifted[...] = jnp.zeros_like(shifted)
    for part in range(2):
        for layer in range(2):
            plane = 2 * part + layer
            padded = jnp.concatenate(
                [window_grad[part][layer], jnp.zeros((8, side), jnp.float32)], axis=0
            )
            shifted[plane, pl.ds(base_row, tall), :] = pltpu.roll(padded, step, 0)
            at = pl.ds(plane * rows, rows)
            message_core[pl.ds(base + plane * rows, rows), :] = shifted[plane, pl.ds(other_at, rows), :]
            message_beyond[at, :] = shifted[plane, pl.ds(beyond_at, rows), :]
            own_strip[at, :] = shifted[plane, half : half + rows, :]
    offset = jnp.full((8, side), col.astype(jnp.float32))
    message_core[pl.ds(base + 4 * rows, 8), :] = offset
    message_beyond[pl.ds(4 * rows, 8), :] = offset


def merge_kernel(scan, own_strip, from_core, from_beyond, centre, with_even, with_odd, frame):
    side = own_strip.shape[1]
    half = side // 2
    rows = centre.shape[2]
    cols = centre.shape[3]
    base = from_core.shape[0] - from_beyond.shape[0]
    core_col = jnp.max(from_core[pl.ds(base + 4 * rows, 8), :]).astype(jnp.int32)
    beyond_col = jnp.max(from_beyond[pl.ds(4 * rows, 8), :]).astype(jnp.int32)
    unused, own_col = place_of(scan, rows, cols, half)
    lane = lax.broadcasted_iota(jnp.int32, (rows, side), 1)
    zero = jnp.zeros((rows, side), jnp.float32)
    frame[...] = jnp.zeros_like(frame)
    for source, first, col in (
        (own_strip, 0, own_col),
        (from_core, base, jnp.clip(core_col, 0, cols - 1)),
        (from_beyond, 0, jnp.clip(beyond_col, 0, cols - 1)),
    ):
        at = col + half
        step = lax.rem(at, side)
        near = pl.multiple_of(at - step, side)
        here, there = pl.ds(near, side), pl.ds(pl.multiple_of(near + side, side), side)
        for plane in range(4):
            strip = pltpu.roll(source[pl.ds(first + plane * rows, rows), :], step, 1)
            frame[plane, :, here] += jnp.where(lane >= step, strip, zero)
            frame[plane, :, there] += jnp.where(lane < step, strip, zero)
    inner = lane < half
    for layer in range(2):
        real, imaginary = layer, 2 + layer
        left = jnp.where(inner, pltpu.roll(frame[imaginary, :, 0:side], half, 1), frame[real, :, 0:side])
        right = jnp.where(inner, frame[real, :, side + cols :], pltpu.roll(frame[imaginary, :, side + cols :], half, 1))
        with_even[layer] = jnp.where(even_col(), right, left)
        with_odd[layer] = jnp.where(even_col(), left, right)
        centre[0, layer] = frame[real, :, side : side + cols]
        centre[1, layer] = frame[imaginary, :, side : side + cols]


def finish_kernel(centre, with_even, with_odd, out):
    rows, cols = centre.shape[2], centre.shape[3]
    side = with_even.shape[2]
    half = side // 2
    inner = lax.broadcasted_iota(jnp.int32, (rows, side), 1) < half
    zero = jnp.zeros((rows, side), jnp.float32)
    for layer in range(2):
        left = jnp.where(even_col(), with_odd[layer], with_even[layer])
        right = jnp.where(even_col(), with_even[layer], with_odd[layer])
        for part in range(2):
            if part:
                left, right = pltpu.roll(left, half, 1), pltpu.roll(right, half, 1)
            value = centre[part, layer]
            out[part, layer, :, 0:side] = value[:, :side] + jnp.where(inner, left, zero)
            out[part, layer, :, cols - side :] = value[:, cols - side :] + jnp.where(inner, zero, right)


def call(kernel, out_shape, n_scalars, n_in, scratch=(), cost=None):
    many = isinstance(out_shape, (list, tuple))
    vmem = pl.BlockSpec(memory_space=pltpu.VMEM)
    return pl.pallas_call(
        kernel,
        out_shape=out_shape,
        in_specs=[pl.BlockSpec(memory_space=pltpu.SMEM)] * n_scalars + [vmem] * n_in,
        out_specs=[vmem] * len(out_shape) if many else vmem,
        scratch_shapes=list(scratch),
        compiler_params=pltpu.CompilerParams(vmem_limit_bytes=VMEM_LIMIT),
        cost_estimate=cost,
    )


def both_ways(pairs):
    return pairs + [(j, i) for i, j in pairs]


def body(obj_field, probe, scan_pos, live_count, patterns):
    side = probe.shape[2]
    modes = probe.shape[1]
    half = side // 2
    rows, cols = obj_field.shape[2], obj_field.shape[3]
    n_row, n_col = lax.axis_size(ROW), lax.axis_size(COL)
    f32 = jnp.float32
    core = lax.axis_index("core")
    scan = scan_pos.reshape(2)
    live = live_count.reshape(1)
    swap = [(0, 1), (1, 0)]
    pairs = both_ways([(i, i + 1) for i in range(1, n_row - 1, 2)])
    even_pairs = both_ways([(i, i + 1) for i in range(0, n_col - 1, 2)])
    odd_pairs = both_ways([(i, i + 1) for i in range(1, n_col - 1, 2)])
    strip = 4 * rows

    def shape(*dims):
        return jax.ShapeDtypeStruct(dims, f32)

    beyond = lax.ppermute(obj_field, ROW, pairs)
    other = lax.ppermute(obj_field, "core", swap)
    edge = shape(2, rows, side)
    tall_edge = shape(2, 2 * half + rows, side)
    near_edge = shape(2, 2 * rows, side)
    near_even, near_odd = call(pack_near_kernel, [near_edge, near_edge], 0, 2)(obj_field, other)
    to_even, to_odd = call(pack_kernel, [tall_edge, tall_edge], 0, 3)(beyond, near_even, near_odd)
    with_even = lax.ppermute(to_even, COL, even_pairs)
    with_odd = lax.ppermute(to_odd, COL, odd_pairs)
    tabs = jnp.asarray(tables(side))
    near = call(near_kernel, shape(4, 2 * half + rows, side), 1, 7)(
        scan, obj_field, other, beyond, to_even, probe, patterns, tabs
    )
    tall = pltpu.VMEM((4, 2 * half + rows, side), f32)
    keep, message_core, message_beyond, own_strip = call(
        main_kernel,
        [
            shape(modes * side, side),
            shape(modes * side + strip + 8, side),
            shape(strip + 8, side),
            shape(strip, side),
        ],
        2,
        6,
        [tall, tall],
    )(scan, live, near, with_even, with_odd, probe, patterns, tabs)

    from_core = lax.ppermute(message_core, "core", swap)
    from_beyond = lax.ppermute(message_beyond, ROW, pairs)

    n_yx = lax.axis_size(("y", "x"))
    n_z = lax.axis_size(("zh", "zl"))
    total = modes * side
    chunk = total // n_yx
    summed = keep + from_core[:total]
    spread = lax.all_to_all(summed.reshape(n_yx, chunk, side), ("y", "x"), 0, 0)

    centre, grad_even, grad_odd = call(
        merge_kernel,
        [shape(2, 2, rows, cols), edge, edge],
        1,
        3,
        [pltpu.VMEM((4, rows, cols + 2 * side), f32)],
    )(scan, own_strip, from_core, from_beyond)
    part = jnp.sum(spread, axis=0)
    part = lax.all_to_all(jnp.broadcast_to(part, (n_z, chunk, side)), ("zh", "zl"), 0, 0)
    part = jnp.sum(part, axis=0)
    got_even = lax.ppermute(grad_even, COL, even_pairs)
    part = jnp.broadcast_to(part, (n_yx, chunk, side))
    part, got_even, grad_odd = lax.optimization_barrier((part, got_even, grad_odd))
    got_odd = lax.ppermute(grad_odd, COL, odd_pairs)
    whole = lax.all_to_all(part, ("y", "x"), 0, 0)
    whole, got_odd = lax.optimization_barrier((whole, got_odd))
    whole = whole.reshape(modes, side, side)
    facing = lax.ppermute(whole, "core", swap)
    first = core == 0
    probe_grad = jnp.stack([jnp.where(first, whole, facing), jnp.where(first, facing, whole)])

    obj_grad = call(finish_kernel, shape(2, 2, rows, cols), 0, 3)(centre, got_even, got_odd)
    return (obj_grad, probe_grad)


def solution(mesh):
    fine = Mesh(
        mesh.devices.reshape(8, 2, 2, 4, 4), ("y", "zh", "core", "x", "zl")
    )
    return jax.shard_map(
        body,
        mesh=fine,
        in_specs=(
            P(None, None, ROW, COL),
            P(),
            P(ROW, COL, None, None),
            P(ROW, COL),
            P(ROW, COL, None, None, None),
        ),
        out_specs=(P(None, None, ROW, COL), P()),
        check_vma=False,
    )
```

```python
import functools
import math

import jax
import jax.numpy as jnp
import ml_dtypes
import numpy as np
from jax import lax
from jax.experimental import pallas as pl
from jax.experimental.pallas import tpu as pltpu
from jax.sharding import Mesh
from jax.sharding import PartitionSpec as P

PHASE_COEF = 20.0
LOSS_WEIGHT = 0.125
ROW = ("y", "zh", "core")
COL = ("x", "zl")
VMEM_LIMIT = 48 * 1024 * 1024
TILE_COLS = 256


def split_bf16(table):
    high = table.astype(np.float32).astype(ml_dtypes.bfloat16)
    low = (table - high.astype(np.float64)).astype(np.float32).astype(ml_dtypes.bfloat16)
    return high, low


def tables(side):
    counter = np.arange(side)
    phase = 2.0 * math.pi / side * (counter[:, None] * counter[None, :] % side)
    fourier = np.exp(-1j * phase) / math.sqrt(side)
    spatial = ((counter + side // 2) % side - side // 2) / side
    factor = np.exp(-1j * PHASE_COEF * spatial * spatial)
    propagate = np.conj(fourier) @ (factor[:, None] * fourier)
    propagate = 0.5 * (propagate + propagate.T)
    parts = []
    for matrix in (propagate, fourier):
        for block in (matrix.real, matrix.imag, -matrix.imag):
            parts += split_bf16(block)
    return np.stack(parts)


def on_sides(tabs, which):
    def block(n, part):
        return tabs[6 * which + 2 * n + part]

    def square(a, b, c, d, part):
        return jnp.concatenate(
            [
                jnp.concatenate([block(a, part), block(b, part)], axis=1),
                jnp.concatenate([block(c, part), block(d, part)], axis=1),
            ],
            axis=0,
        )

    right = tuple(square(0, 1, 2, 0, part) for part in range(2))
    left = tuple(square(0, 2, 1, 0, part) for part in range(2))
    return right, left


def split(value):
    high = value.astype(jnp.bfloat16)
    low = (value - high.astype(jnp.float32)).astype(jnp.bfloat16)
    return high, low


def product(left, right):
    (left_high, left_low), (right_high, right_low) = left, right
    dot = functools.partial(jnp.dot, preferred_element_type=jnp.float32)
    return dot(left_high, right_high) + (dot(left_low, right_high) + dot(left_high, right_low))


def two_sided(real, imaginary, right, left):
    side = real[0].shape[0]
    modes = len(real)
    stacked = jnp.concatenate(
        [jnp.concatenate([r, i], axis=1) for r, i in zip(real, imaginary)], axis=0
    )
    middle = product(split(stacked), right)
    blocks = [middle[m * side : (m + 1) * side] for m in range(modes)]
    spread = jnp.concatenate(
        [
            jnp.concatenate([b[:, :side] for b in blocks], axis=1),
            jnp.concatenate([b[:, side:] for b in blocks], axis=1),
        ],
        axis=0,
    )
    out = product(left, split(spread))
    return (
        [out[:side, m * side : (m + 1) * side] for m in range(modes)],
        [out[side:, m * side : (m + 1) * side] for m in range(modes)],
    )


def times(ar, ai, br, bi):
    return ar * br - ai * bi, ar * bi + ai * br


def times_conj(ar, ai, br, bi):
    return ar * br + ai * bi, ar * bi - ai * br


def model(window, probe, pattern, weight, tabs):
    (o0r, o1r), (o0i, o1i) = window
    qr, qi = probe
    modes = len(qr)
    prop_right, prop_left = on_sides(tabs, 0)
    four_right, four_left = on_sides(tabs, 1)
    e0 = [times(qr[m], qi[m], o0r, o0i) for m in range(modes)]
    a1r, a1i = two_sided([e[0] for e in e0], [e[1] for e in e0], prop_right, prop_left)
    e1 = [times(a1r[m], a1i[m], o1r, o1i) for m in range(modes)]
    gr, gi = two_sided([e[0] for e in e1], [e[1] for e in e1], four_right, four_left)
    intensity = gr[0] * gr[0] + gi[0] * gi[0]
    for m in range(1, modes):
        intensity = intensity + (gr[m] * gr[m] + gi[m] * gi[m])
    residue = (intensity - pattern) * (4.0 * LOSS_WEIGHT * weight)
    br, bi = two_sided(
        [residue * g for g in gr], [residue * g for g in gi], four_left, four_right
    )
    grad1 = [times_conj(a1r[m], a1i[m], br[m], bi[m]) for m in range(modes)]
    back = [times_conj(o1r, o1i, br[m], bi[m]) for m in range(modes)]
    cr, ci = two_sided([b[0] for b in back], [b[1] for b in back], prop_left, prop_right)
    grad0 = [times_conj(qr[m], qi[m], cr[m], ci[m]) for m in range(modes)]
    probe_grad = [times_conj(o0r, o0i, cr[m], ci[m]) for m in range(modes)]

    def over_modes(terms, part):
        return functools.reduce(lambda a, b: a + b, [t[part] for t in terms])

    window_grad = [
        [over_modes(grad0, 0), over_modes(grad1, 0)],
        [over_modes(grad0, 1), over_modes(grad1, 1)],
    ]
    return window_grad, probe_grad


def place_of(scan, rows, cols, half):
    row = scan[0] - (lax.axis_index(ROW) * rows - half)
    col = scan[1] - (lax.axis_index(COL) * cols - half)
    return row, col


def strips_at(half):
    core = lax.axis_index("core")
    return pl.multiple_of((1 - core) * 2 * half, 8), pl.multiple_of(core * 2 * half, 8)


def even_col():
    return lax.rem(lax.axis_index(COL), 2) == 0


def fill(frame, own, with_even, with_odd, part, layer):
    side = with_even.shape[2]
    half = side // 2
    cols = own.shape[3]
    plane = 2 * part + layer
    left = jnp.where(even_col(), with_odd[layer], with_even[layer])
    right = jnp.where(even_col(), with_even[layer], with_odd[layer])
    if part:
        left, right = pltpu.roll(left, half, 1), pltpu.roll(right, half, 1)
    frame[plane, :, 0:side] = left
    frame[plane, :, side : side + cols] = own[part, layer]
    frame[plane, :, side + cols :] = right


def cut(frame, plane, at, side):
    step = lax.rem(at, side)
    wide = frame[plane, :, pl.ds(pl.multiple_of(at - step, side), 2 * side)]
    return pltpu.roll(wide, lax.rem(2 * side - step, 2 * side), 1)[:, :side]


def edges_kernel(scan, own, with_even, with_odd, column, column_near):
    rows, cols = own.shape[2], own.shape[3]
    side = with_even.shape[2]
    half = side // 2
    inner = lax.broadcasted_iota(jnp.int32, (rows, side), 1) < half
    for layer in range(2):
        real, imaginary = own[0, layer], own[1, layer]
        left = jnp.where(inner, real[:, :side], pltpu.roll(imaginary[:, :side], half, 1))
        right = jnp.where(inner, pltpu.roll(imaginary[:, cols - side :], half, 1), real[:, cols - side :])
        with_even[layer] = jnp.where(even_col(), right, left)
        with_odd[layer] = jnp.where(even_col(), left, right)
    unused, col = place_of(scan, rows, cols, half)
    column[...] = jnp.full(column.shape, col.astype(jnp.float32))
    column_near[...] = jnp.full(column_near.shape, col.astype(jnp.float32))


def partner_column(column, cols):
    return jnp.clip(jnp.max(column[0:8, :]).astype(jnp.int32), 0, cols - 1)


def beyond_kernel(column, own, with_even, with_odd, to_beyond, frame):
    rows, cols = own.shape[2], own.shape[3]
    side = to_beyond.shape[1]
    col = partner_column(column, cols)
    for layer in range(2):
        for part in range(2):
            plane = 2 * part + layer
            fill(frame, own, with_even, with_odd, part, layer)
            to_beyond[pl.ds(plane * rows, rows), :] = cut(frame, plane, col + side // 2, side)
    to_beyond[pl.ds(4 * rows, 8), :] = jnp.zeros((8, side), jnp.float32)


def core_kernel(column, frame, to_core):
    side = to_core.shape[1]
    rows, cols = frame.shape[1], frame.shape[2] - 2 * side
    col = partner_column(column, cols)
    for plane in range(4):
        to_core[pl.ds(plane * rows, rows), :] = cut(frame, plane, col + side // 2, side)


def near_kernel(scan, frame, probe, pattern, tabs, near):
    rows, cols = frame.shape[1], frame.shape[2] - 2 * near.shape[1]
    side = near.shape[1]
    half = side // 2
    unused, col = place_of(scan, rows, cols, half)
    for plane in range(4):
        near[pl.ds(plane * rows, rows), :] = cut(frame, plane, col + half, side)


def main_kernel(
    scan, live, near, other, beyond, probe, pattern, tabs,
    keep, message_core, message_beyond, own_strip, column, shifted,
):
    side = probe.shape[-1]
    half = side // 2
    rows = own_strip.shape[0] // 4
    cols = TILE_COLS
    modes = probe.shape[1]
    row, col = place_of(scan, rows, cols, half)
    other_at, beyond_at = strips_at(half)
    for plane in range(4):
        at = pl.ds(plane * rows, rows)
        column[plane, half : half + rows, :] = near[at, :]
        column[plane, pl.ds(other_at, rows), :] = other[at, :]
        column[plane, pl.ds(beyond_at, rows), :] = beyond[at, :]
    tall = side + 8
    step = lax.rem(row, 8)
    base_row = pl.multiple_of(row - step, 8)

    def window_of(plane):
        high = column[plane, pl.ds(base_row, tall), :]
        return pltpu.roll(high, lax.rem(tall - step, tall), 0)[:side]

    window = [[window_of(2 * part + layer) for layer in range(2)] for part in range(2)]
    fields = [[probe[part, m] for m in range(modes)] for part in range(2)]
    weight = (live[0] > 0).astype(jnp.float32)
    window_grad, probe_grad = model(window, fields, pattern[0, 0, 0], weight, tabs)
    first = lax.axis_index("core") == 0
    for m in range(modes):
        at = pl.ds(m * side, side)
        real, imaginary = probe_grad[m]
        keep[at, :] = jnp.where(first, real, imaginary)
        message_core[at, :] = jnp.where(first, imaginary, real)
    base = modes * side
    shifted[...] = jnp.zeros_like(shifted)
    for part in range(2):
        for layer in range(2):
            plane = 2 * part + layer
            padded = jnp.concatenate(
                [window_grad[part][layer], jnp.zeros((8, side), jnp.float32)], axis=0
            )
            shifted[plane, pl.ds(base_row, tall), :] = pltpu.roll(padded, step, 0)
            at = pl.ds(plane * rows, rows)
            message_core[pl.ds(base + plane * rows, rows), :] = shifted[plane, pl.ds(other_at, rows), :]
            message_beyond[at, :] = shifted[plane, pl.ds(beyond_at, rows), :]
            own_strip[at, :] = shifted[plane, half : half + rows, :]
    offset = jnp.full((8, side), col.astype(jnp.float32))
    message_core[pl.ds(base + 4 * rows, 8), :] = offset
    message_beyond[pl.ds(4 * rows, 8), :] = offset


def merge_kernel(scan, own_strip, from_core, from_beyond, centre, with_even, with_odd, frame):
    side = own_strip.shape[1]
    half = side // 2
    rows = centre.shape[2]
    cols = centre.shape[3]
    base = from_core.shape[0] - from_beyond.shape[0]
    core_col = jnp.max(from_core[pl.ds(base + 4 * rows, 8), :]).astype(jnp.int32)
    beyond_col = jnp.max(from_beyond[pl.ds(4 * rows, 8), :]).astype(jnp.int32)
    unused, own_col = place_of(scan, rows, cols, half)
    lane = lax.broadcasted_iota(jnp.int32, (rows, side), 1)
    zero = jnp.zeros((rows, side), jnp.float32)
    frame[...] = jnp.zeros_like(frame)
    for source, first, col in (
        (own_strip, 0, own_col),
        (from_core, base, jnp.clip(core_col, 0, cols - 1)),
        (from_beyond, 0, jnp.clip(beyond_col, 0, cols - 1)),
    ):
        at = col + half
        step = lax.rem(at, side)
        near = pl.multiple_of(at - step, side)
        here, there = pl.ds(near, side), pl.ds(pl.multiple_of(near + side, side), side)
        for plane in range(4):
            strip = pltpu.roll(source[pl.ds(first + plane * rows, rows), :], step, 1)
            frame[plane, :, here] += jnp.where(lane >= step, strip, zero)
            frame[plane, :, there] += jnp.where(lane < step, strip, zero)
    inner = lane < half
    for layer in range(2):
        real, imaginary = layer, 2 + layer
        left = jnp.where(inner, pltpu.roll(frame[imaginary, :, 0:side], half, 1), frame[real, :, 0:side])
        right = jnp.where(inner, frame[real, :, side + cols :], pltpu.roll(frame[imaginary, :, side + cols :], half, 1))
        with_even[layer] = jnp.where(even_col(), right, left)
        with_odd[layer] = jnp.where(even_col(), left, right)
        centre[0, layer] = frame[real, :, side : side + cols]
        centre[1, layer] = frame[imaginary, :, side : side + cols]


def finish_kernel(centre, with_even, with_odd, out):
    rows, cols = centre.shape[2], centre.shape[3]
    side = with_even.shape[2]
    half = side // 2
    inner = lax.broadcasted_iota(jnp.int32, (rows, side), 1) < half
    zero = jnp.zeros((rows, side), jnp.float32)
    for layer in range(2):
        left = jnp.where(even_col(), with_odd[layer], with_even[layer])
        right = jnp.where(even_col(), with_even[layer], with_odd[layer])
        for part in range(2):
            if part:
                left, right = pltpu.roll(left, half, 1), pltpu.roll(right, half, 1)
            value = centre[part, layer]
            out[part, layer, :, 0:side] = value[:, :side] + jnp.where(inner, left, zero)
            out[part, layer, :, cols - side :] = value[:, cols - side :] + jnp.where(inner, zero, right)


def call(kernel, out_shape, n_scalars, n_in, scratch=(), cost=None):
    many = isinstance(out_shape, (list, tuple))
    vmem = pl.BlockSpec(memory_space=pltpu.VMEM)
    return pl.pallas_call(
        kernel,
        out_shape=out_shape,
        in_specs=[pl.BlockSpec(memory_space=pltpu.SMEM)] * n_scalars + [vmem] * n_in,
        out_specs=[vmem] * len(out_shape) if many else vmem,
        scratch_shapes=list(scratch),
        compiler_params=pltpu.CompilerParams(vmem_limit_bytes=VMEM_LIMIT),
        cost_estimate=cost,
    )


def both_ways(pairs):
    return pairs + [(j, i) for i, j in pairs]


def body(obj_field, probe, scan_pos, live_count, patterns):
    side = probe.shape[2]
    modes = probe.shape[1]
    half = side // 2
    rows, cols = obj_field.shape[2], obj_field.shape[3]
    n_row, n_col = lax.axis_size(ROW), lax.axis_size(COL)
    f32 = jnp.float32
    core = lax.axis_index("core")
    scan = scan_pos.reshape(2)
    live = live_count.reshape(1)
    swap = [(0, 1), (1, 0)]
    pairs = both_ways([(i, i + 1) for i in range(1, n_row - 1, 2)])
    even_pairs = both_ways([(i, i + 1) for i in range(0, n_col - 1, 2)])
    odd_pairs = both_ways([(i, i + 1) for i in range(1, n_col - 1, 2)])
    strip = 4 * rows

    def shape(*dims):
        return jax.ShapeDtypeStruct(dims, f32)

    edge = shape(2, rows, side)
    to_even, to_odd, column, column_near = call(
        edges_kernel, [edge, edge, shape(136, side), shape(8, side)], 1, 1
    )(scan, obj_field)
    column = lax.ppermute(column, ROW, pairs)
    with_even = lax.ppermute(to_even, COL, even_pairs)
    with_odd = lax.ppermute(to_odd, COL, odd_pairs)
    column_near = lax.ppermute(column_near, "core", swap)
    to_beyond, frame = call(
        beyond_kernel, [shape(strip + 8, side), shape(4, rows, cols + 2 * side)], 0, 4
    )(column, obj_field, with_even, with_odd)
    beyond = lax.ppermute(to_beyond, ROW, pairs)
    to_core = call(core_kernel, shape(strip, side), 0, 2)(column_near, frame)
    other = lax.ppermute(to_core, "core", swap)
    tabs = jnp.asarray(tables(side))
    small = pl.CostEstimate(flops=1000, bytes_accessed=1000, transcendentals=0)
    near = call(near_kernel, shape(strip, side), 1, 4, cost=small)(
        scan, frame, probe, patterns, tabs
    )
    near, other, beyond = lax.optimization_barrier((near, other, beyond))
    tall = pltpu.VMEM((4, 2 * half + rows, side), f32)
    keep, message_core, message_beyond, own_strip = call(
        main_kernel,
        [
            shape(modes * side, side),
            shape(modes * side + strip + 8, side),
            shape(strip + 8, side),
            shape(strip, side),
        ],
        2,
        6,
        [tall, tall],
    )(scan, live, near, other, beyond, probe, patterns, tabs)

    from_core = lax.ppermute(message_core, "core", swap)
    from_beyond = lax.ppermute(message_beyond, ROW, pairs)

    n_yx = lax.axis_size(("y", "x"))
    n_z = lax.axis_size(("zh", "zl"))
    total = modes * side
    chunk = total // n_yx
    summed = keep + from_core[:total]
    spread = lax.all_to_all(summed.reshape(n_yx, chunk, side), ("y", "x"), 0, 0)

    centre, grad_even, grad_odd = call(
        merge_kernel,
        [shape(2, 2, rows, cols), edge, edge],
        1,
        3,
        [pltpu.VMEM((4, rows, cols + 2 * side), f32)],
    )(scan, own_strip, from_core, from_beyond)
    part = jnp.sum(spread, axis=0)
    part = lax.all_to_all(jnp.broadcast_to(part, (n_z, chunk, side)), ("zh", "zl"), 0, 0)
    part = jnp.sum(part, axis=0)
    got_even = lax.ppermute(grad_even, COL, even_pairs)
    part = jnp.broadcast_to(part, (n_yx, chunk, side))
    part, got_even, grad_odd = lax.optimization_barrier((part, got_even, grad_odd))
    got_odd = lax.ppermute(grad_odd, COL, odd_pairs)
    whole = lax.all_to_all(part, ("y", "x"), 0, 0)
    whole, got_odd = lax.optimization_barrier((whole, got_odd))
    whole = whole.reshape(modes, side, side)
    facing = lax.ppermute(whole, "core", swap)
    first = core == 0
    probe_grad = jnp.stack([jnp.where(first, whole, facing), jnp.where(first, facing, whole)])

    obj_grad = call(finish_kernel, shape(2, 2, rows, cols), 0, 3)(centre, got_even, got_odd)
    return (obj_grad, probe_grad)


def solution(mesh):
    fine = Mesh(
        mesh.devices.reshape(8, 2, 2, 4, 4), ("y", "zh", "core", "x", "zl")
    )
    return jax.shard_map(
        body,
        mesh=fine,
        in_specs=(
            P(None, None, ROW, COL),
            P(),
            P(ROW, COL, None, None),
            P(ROW, COL),
            P(ROW, COL, None, None, None),
        ),
        out_specs=(P(None, None, ROW, COL), P()),
        check_vma=False,
    )
```

```python
import functools
import math

import jax
import jax.numpy as jnp
import ml_dtypes
import numpy as np
from jax import lax
from jax.experimental import pallas as pl
from jax.experimental.pallas import tpu as pltpu
from jax.sharding import Mesh
from jax.sharding import PartitionSpec as P

PHASE_COEF = 20.0
LOSS_WEIGHT = 0.125
ROW = ("y", "zh", "core")
COL = ("x", "zl")
VMEM_LIMIT = 48 * 1024 * 1024
TILE_COLS = 256


def split_bf16(table):
    high = table.astype(np.float32).astype(ml_dtypes.bfloat16)
    low = (table - high.astype(np.float64)).astype(np.float32).astype(ml_dtypes.bfloat16)
    return high, low


def tables(side):
    counter = np.arange(side)
    phase = 2.0 * math.pi / side * (counter[:, None] * counter[None, :] % side)
    fourier = np.exp(-1j * phase) / math.sqrt(side)
    spatial = ((counter + side // 2) % side - side // 2) / side
    factor = np.exp(-1j * PHASE_COEF * spatial * spatial)
    propagate = np.conj(fourier) @ (factor[:, None] * fourier)
    propagate = 0.5 * (propagate + propagate.T)
    parts = []
    for matrix in (propagate, fourier):
        for block in (matrix.real, matrix.imag, -matrix.imag):
            parts += split_bf16(block)
    return np.stack(parts)


def on_sides(tabs, which):
    def block(n, part):
        return tabs[6 * which + 2 * n + part]

    def square(a, b, c, d, part):
        return jnp.concatenate(
            [
                jnp.concatenate([block(a, part), block(b, part)], axis=1),
                jnp.concatenate([block(c, part), block(d, part)], axis=1),
            ],
            axis=0,
        )

    right = tuple(square(0, 1, 2, 0, part) for part in range(2))
    left = tuple(square(0, 2, 1, 0, part) for part in range(2))
    return right, left


def split(value):
    high = value.astype(jnp.bfloat16)
    low = (value - high.astype(jnp.float32)).astype(jnp.bfloat16)
    return high, low


def product(left, right):
    (left_high, left_low), (right_high, right_low) = left, right
    dot = functools.partial(jnp.dot, preferred_element_type=jnp.float32)
    return dot(left_high, right_high) + (dot(left_low, right_high) + dot(left_high, right_low))


def two_sided(real, imaginary, right, left, group=2):
    side = real[0].shape[0]
    middles = []
    for n in range(0, len(real), group):
        pairs = zip(real[n : n + group], imaginary[n : n + group])
        stacked = jnp.concatenate([jnp.concatenate(pair, axis=1) for pair in pairs], axis=0)
        middles.append(product(split(stacked), right))
    out_real, out_imaginary = [], []
    for middle in middles:
        blocks = [middle[m * side : (m + 1) * side] for m in range(group)]
        spread = jnp.concatenate(
            [
                jnp.concatenate([block[:, :side] for block in blocks], axis=1),
                jnp.concatenate([block[:, side:] for block in blocks], axis=1),
            ],
            axis=0,
        )
        out = product(left, split(spread))
        out_real += [out[:side, m * side : (m + 1) * side] for m in range(group)]
        out_imaginary += [out[side:, m * side : (m + 1) * side] for m in range(group)]
    return out_real, out_imaginary


def times(ar, ai, br, bi):
    return ar * br - ai * bi, ar * bi + ai * br


def times_conj(ar, ai, br, bi):
    return ar * br + ai * bi, ar * bi - ai * br


def model(window, probe, pattern, weight, tabs):
    (o0r, o1r), (o0i, o1i) = window
    qr, qi = probe
    modes = len(qr)
    prop_right, prop_left = on_sides(tabs, 0)
    four_right, four_left = on_sides(tabs, 1)
    e0 = [times(qr[m], qi[m], o0r, o0i) for m in range(modes)]
    a1r, a1i = two_sided([e[0] for e in e0], [e[1] for e in e0], prop_right, prop_left)
    e1 = [times(a1r[m], a1i[m], o1r, o1i) for m in range(modes)]
    gr, gi = two_sided([e[0] for e in e1], [e[1] for e in e1], four_right, four_left)
    intensity = gr[0] * gr[0] + gi[0] * gi[0]
    for m in range(1, modes):
        intensity = intensity + (gr[m] * gr[m] + gi[m] * gi[m])
    residue = (intensity - pattern) * (4.0 * LOSS_WEIGHT * weight)
    br, bi = two_sided(
        [residue * g for g in gr], [residue * g for g in gi], four_left, four_right
    )
    grad1 = [times_conj(a1r[m], a1i[m], br[m], bi[m]) for m in range(modes)]
    back = [times_conj(o1r, o1i, br[m], bi[m]) for m in range(modes)]
    cr, ci = two_sided([b[0] for b in back], [b[1] for b in back], prop_left, prop_right)
    grad0 = [times_conj(qr[m], qi[m], cr[m], ci[m]) for m in range(modes)]
    probe_grad = [times_conj(o0r, o0i, cr[m], ci[m]) for m in range(modes)]

    def over_modes(terms, part):
        return functools.reduce(lambda a, b: a + b, [t[part] for t in terms])

    window_grad = [
        [over_modes(grad0, 0), over_modes(grad1, 0)],
        [over_modes(grad0, 1), over_modes(grad1, 1)],
    ]
    return window_grad, probe_grad


def place_of(scan, rows, cols, half):
    row = scan[0] - (lax.axis_index(ROW) * rows - half)
    col = scan[1] - (lax.axis_index(COL) * cols - half)
    return row, col


def strips_at(half):
    core = lax.axis_index("core")
    return pl.multiple_of((1 - core) * 2 * half, 8), pl.multiple_of(core * 2 * half, 8)


def even_col():
    return lax.rem(lax.axis_index(COL), 2) == 0


def fill(frame, own, with_even, with_odd, part, layer):
    side = with_even.shape[2]
    half = side // 2
    cols = own.shape[3]
    plane = 2 * part + layer
    left = jnp.where(even_col(), with_odd[layer], with_even[layer])
    right = jnp.where(even_col(), with_even[layer], with_odd[layer])
    if part:
        left, right = pltpu.roll(left, half, 1), pltpu.roll(right, half, 1)
    frame[plane, :, 0:side] = left
    frame[plane, :, side : side + cols] = own[part, layer]
    frame[plane, :, side + cols :] = right


def cut(frame, plane, at, side):
    step = lax.rem(at, side)
    wide = frame[plane, :, pl.ds(pl.multiple_of(at - step, side), 2 * side)]
    return pltpu.roll(wide, lax.rem(2 * side - step, 2 * side), 1)[:, :side]


def edges_kernel(scan, own, with_even, with_odd, column, column_near):
    rows, cols = own.shape[2], own.shape[3]
    side = with_even.shape[2]
    half = side // 2
    inner = lax.broadcasted_iota(jnp.int32, (rows, side), 1) < half
    for layer in range(2):
        real, imaginary = own[0, layer], own[1, layer]
        left = jnp.where(inner, real[:, :side], pltpu.roll(imaginary[:, :side], half, 1))
        right = jnp.where(inner, pltpu.roll(imaginary[:, cols - side :], half, 1), real[:, cols - side :])
        with_even[layer] = jnp.where(even_col(), right, left)
        with_odd[layer] = jnp.where(even_col(), left, right)
    col = (scan[:, 1:2] - (lax.axis_index(COL) * cols - half)).astype(jnp.float32)
    column[...] = jnp.broadcast_to(col, column.shape)
    column_near[...] = jnp.broadcast_to(col, column_near.shape)


def partner_column(column, cols):
    return jnp.clip(jnp.max(column[0:8, :]).astype(jnp.int32), 0, cols - 1)


def beyond_kernel(column, own, with_even, with_odd, to_beyond, frame):
    rows, cols = own.shape[2], own.shape[3]
    side = to_beyond.shape[1]
    col = partner_column(column, cols)
    for layer in range(2):
        for part in range(2):
            plane = 2 * part + layer
            fill(frame, own, with_even, with_odd, part, layer)
            to_beyond[pl.ds(plane * rows, rows), :] = cut(frame, plane, col + side // 2, side)
    to_beyond[pl.ds(4 * rows, 8), :] = jnp.zeros((8, side), jnp.float32)


def core_kernel(column, frame, to_core):
    side = to_core.shape[1]
    rows, cols = frame.shape[1], frame.shape[2] - 2 * side
    col = partner_column(column, cols)
    for plane in range(4):
        to_core[pl.ds(plane * rows, rows), :] = cut(frame, plane, col + side // 2, side)


def near_kernel(scan, frame, probe, pattern, tabs, near):
    rows, cols = frame.shape[1], frame.shape[2] - 2 * near.shape[1]
    side = near.shape[1]
    half = side // 2
    unused, col = place_of(scan, rows, cols, half)
    for plane in range(4):
        near[pl.ds(plane * rows, rows), :] = cut(frame, plane, col + half, side)


def main_kernel(
    scan, live, near, other, beyond, probe, pattern, tabs,
    keep, message_core, message_beyond, own_strip, column, shifted,
):
    side = probe.shape[-1]
    half = side // 2
    rows = own_strip.shape[0] // 4
    cols = TILE_COLS
    modes = probe.shape[1]
    row, col = place_of(scan, rows, cols, half)
    other_at, beyond_at = strips_at(half)
    for plane in range(4):
        at = pl.ds(plane * rows, rows)
        column[plane, half : half + rows, :] = near[at, :]
        column[plane, pl.ds(other_at, rows), :] = other[at, :]
        column[plane, pl.ds(beyond_at, rows), :] = beyond[at, :]
    tall = side + 8
    step = lax.rem(row, 8)
    base_row = pl.multiple_of(row - step, 8)

    def window_of(plane):
        high = column[plane, pl.ds(base_row, tall), :]
        return pltpu.roll(high, lax.rem(tall - step, tall), 0)[:side]

    window = [[window_of(2 * part + layer) for layer in range(2)] for part in range(2)]
    fields = [[probe[part, m] for m in range(modes)] for part in range(2)]
    weight = (live[0] > 0).astype(jnp.float32)
    window_grad, probe_grad = model(window, fields, pattern[0, 0, 0], weight, tabs)
    first = lax.axis_index("core") == 0
    for m in range(modes):
        at = pl.ds(m * side, side)
        real, imaginary = probe_grad[m]
        keep[at, :] = jnp.where(first, real, imaginary)
        message_core[at, :] = jnp.where(first, imaginary, real)
    base = modes * side
    shifted[...] = jnp.zeros_like(shifted)
    for part in range(2):
        for layer in range(2):
            plane = 2 * part + layer
            padded = jnp.concatenate(
                [window_grad[part][layer], jnp.zeros((8, side), jnp.float32)], axis=0
            )
            shifted[plane, pl.ds(base_row, tall), :] = pltpu.roll(padded, step, 0)
            at = pl.ds(plane * rows, rows)
            message_core[pl.ds(base + plane * rows, rows), :] = shifted[plane, pl.ds(other_at, rows), :]
            message_beyond[at, :] = shifted[plane, pl.ds(beyond_at, rows), :]
            own_strip[at, :] = shifted[plane, half : half + rows, :]
    offset = jnp.full((8, side), col.astype(jnp.float32))
    message_core[pl.ds(base + 4 * rows, 8), :] = offset
    message_beyond[pl.ds(4 * rows, 8), :] = offset


def merge_kernel(scan, own_strip, from_core, from_beyond, centre, with_even, with_odd, frame):
    side = own_strip.shape[1]
    half = side // 2
    rows = centre.shape[2]
    cols = centre.shape[3]
    base = from_core.shape[0] - from_beyond.shape[0]
    core_col = jnp.max(from_core[pl.ds(base + 4 * rows, 8), :]).astype(jnp.int32)
    beyond_col = jnp.max(from_beyond[pl.ds(4 * rows, 8), :]).astype(jnp.int32)
    unused, own_col = place_of(scan, rows, cols, half)
    lane = lax.broadcasted_iota(jnp.int32, (rows, side), 1)
    zero = jnp.zeros((rows, side), jnp.float32)
    frame[...] = jnp.zeros_like(frame)
    for source, first, col in (
        (own_strip, 0, own_col),
        (from_core, base, jnp.clip(core_col, 0, cols - 1)),
        (from_beyond, 0, jnp.clip(beyond_col, 0, cols - 1)),
    ):
        at = col + half
        step = lax.rem(at, side)
        near = pl.multiple_of(at - step, side)
        here, there = pl.ds(near, side), pl.ds(pl.multiple_of(near + side, side), side)
        for plane in range(4):
            strip = pltpu.roll(source[pl.ds(first + plane * rows, rows), :], step, 1)
            frame[plane, :, here] += jnp.where(lane >= step, strip, zero)
            frame[plane, :, there] += jnp.where(lane < step, strip, zero)
    inner = lane < half
    for layer in range(2):
        real, imaginary = layer, 2 + layer
        left = jnp.where(inner, pltpu.roll(frame[imaginary, :, 0:side], half, 1), frame[real, :, 0:side])
        right = jnp.where(inner, frame[real, :, side + cols :], pltpu.roll(frame[imaginary, :, side + cols :], half, 1))
        with_even[layer] = jnp.where(even_col(), right, left)
        with_odd[layer] = jnp.where(even_col(), left, right)
        centre[0, layer] = frame[real, :, side : side + cols]
        centre[1, layer] = frame[imaginary, :, side : side + cols]


def add_kernel(keep, message, out):
    out[...] = keep[...] + message[0 : keep.shape[0], :]


def sum_kernel(parts, copies):
    total = parts[0]
    for n in range(1, parts.shape[0]):
        total = total + parts[n]
    for n in range(copies.shape[0]):
        copies[n] = total


def finish_kernel(centre, with_even, with_odd, whole, out, probe_grad, total, sem, out_sem):
    copy = pltpu.make_async_copy(whole, probe_grad.at[lax.axis_index("core")], sem)
    copy.start()
    rows, cols = centre.shape[2], centre.shape[3]
    side = with_even.shape[2]
    half = side // 2
    inner = lax.broadcasted_iota(jnp.int32, (rows, side), 1) < half
    zero = jnp.zeros((rows, side), jnp.float32)
    for layer in range(2):
        left = jnp.where(even_col(), with_odd[layer], with_even[layer])
        right = jnp.where(even_col(), with_even[layer], with_odd[layer])
        for part in range(2):
            if part:
                left, right = pltpu.roll(left, half, 1), pltpu.roll(right, half, 1)
            value = centre[part, layer]
            total[part, layer, :, 0:side] = value[:, :side] + jnp.where(inner, left, zero)
            total[part, layer, :, cols - side :] = value[:, cols - side :] + jnp.where(inner, zero, right)
    out_copy = pltpu.make_async_copy(total, out, out_sem)
    out_copy.start()
    copy.wait()
    out_copy.wait()


def other_half_kernel(facing, half_done, probe_grad, sem):
    copy = pltpu.make_async_copy(facing, probe_grad.at[1 - lax.axis_index("core")], sem)
    copy.start()
    copy.wait()


def call(kernel, out_shape, n_scalars, n_in, scratch=(), cost=None, n_far=0, out_far=(), aliases=None):
    many = isinstance(out_shape, (list, tuple))
    vmem = pl.BlockSpec(memory_space=pltpu.VMEM)
    far = pl.BlockSpec(memory_space=pltpu.HBM)
    return pl.pallas_call(
        kernel,
        out_shape=out_shape,
        in_specs=[pl.BlockSpec(memory_space=pltpu.SMEM)] * n_scalars + [vmem] * n_in + [far] * n_far,
        out_specs=[far if n in out_far else vmem for n in range(len(out_shape))] if many else vmem,
        input_output_aliases=aliases or {},
        scratch_shapes=list(scratch),
        compiler_params=pltpu.CompilerParams(vmem_limit_bytes=VMEM_LIMIT),
        cost_estimate=cost,
    )


def both_ways(pairs):
    return pairs + [(j, i) for i, j in pairs]


def body(obj_field, probe, scan_pos, live_count, patterns):
    side = probe.shape[2]
    modes = probe.shape[1]
    half = side // 2
    rows, cols = obj_field.shape[2], obj_field.shape[3]
    n_row, n_col = lax.axis_size(ROW), lax.axis_size(COL)
    f32 = jnp.float32
    scan = scan_pos.reshape(2)
    live = live_count.reshape(1)
    swap = [(0, 1), (1, 0)]
    pairs = both_ways([(i, i + 1) for i in range(1, n_row - 1, 2)])
    even_pairs = both_ways([(i, i + 1) for i in range(0, n_col - 1, 2)])
    odd_pairs = both_ways([(i, i + 1) for i in range(1, n_col - 1, 2)])
    strip = 4 * rows

    def shape(*dims):
        return jax.ShapeDtypeStruct(dims, f32)

    edge = shape(2, rows, side)
    to_even, to_odd, column, column_near = call(
        edges_kernel, [edge, edge, shape(136, side), shape(8, side)], 0, 2
    )(scan.reshape(1, 2), obj_field)
    column = lax.ppermute(column, ROW, pairs)
    with_even = lax.ppermute(to_even, COL, even_pairs)
    with_odd = lax.ppermute(to_odd, COL, odd_pairs)
    column_near = lax.ppermute(column_near, "core", swap)
    to_beyond, frame = call(
        beyond_kernel, [shape(strip + 8, side), shape(4, rows, cols + 2 * side)], 0, 4
    )(column, obj_field, with_even, with_odd)
    beyond = lax.ppermute(to_beyond, ROW, pairs)
    to_core = call(core_kernel, shape(strip, side), 0, 2)(column_near, frame)
    other = lax.ppermute(to_core, "core", swap)
    tabs = jnp.asarray(tables(side))
    small = pl.CostEstimate(flops=1000, bytes_accessed=1000, transcendentals=0)
    near = call(near_kernel, shape(strip, side), 1, 4, cost=small)(
        scan, frame, probe, patterns, tabs
    )
    near, other, beyond = lax.optimization_barrier((near, other, beyond))
    tall = pltpu.VMEM((4, 2 * half + rows, side), f32)
    keep, message_core, message_beyond, own_strip = call(
        main_kernel,
        [
            shape(modes * side, side),
            shape(modes * side + strip + 8, side),
            shape(strip + 8, side),
            shape(strip, side),
        ],
        2,
        6,
        [tall, tall],
    )(scan, live, near, other, beyond, probe, patterns, tabs)

    from_core = lax.ppermute(message_core, "core", swap)
    from_beyond = lax.ppermute(message_beyond, ROW, pairs)

    n_yx = lax.axis_size(("y", "x"))
    n_z = lax.axis_size(("zh", "zl"))
    total = modes * side
    chunk = total // n_yx
    summed = call(add_kernel, shape(total, side), 0, 2)(keep, from_core)
    spread = lax.all_to_all(summed.reshape(n_yx, chunk, side), ("y", "x"), 0, 0)

    centre, grad_even, grad_odd = call(
        merge_kernel,
        [shape(2, 2, rows, cols), edge, edge],
        1,
        3,
        [pltpu.VMEM((4, rows, cols + 2 * side), f32)],
    )(scan, own_strip, from_core, from_beyond)
    part = call(sum_kernel, shape(n_z, chunk, side), 0, 1)(spread)
    part = lax.all_to_all(part, ("zh", "zl"), 0, 0)
    part = call(sum_kernel, shape(n_yx, chunk, side), 0, 1)(part)
    part, grad_even, grad_odd = lax.optimization_barrier((part, grad_even, grad_odd))
    got_even = lax.ppermute(grad_even, COL, even_pairs)
    got_odd = lax.ppermute(grad_odd, COL, odd_pairs)
    whole = lax.all_to_all(part, ("y", "x"), 0, 0)
    whole, got_even, got_odd = lax.optimization_barrier((whole, got_even, got_odd))
    whole = whole.reshape(modes, side, side)
    facing = lax.ppermute(whole, "core", swap)
    obj_grad, probe_grad = call(
        finish_kernel,
        [shape(2, 2, rows, cols), shape(2, modes, side, side)],
        0,
        4,
        [pltpu.VMEM((2, 2, rows, cols), f32), pltpu.SemaphoreType.DMA, pltpu.SemaphoreType.DMA],
        out_far=(0, 1),
    )(centre, got_even, got_odd, whole)
    (probe_grad,) = call(
        other_half_kernel,
        [shape(2, modes, side, side)],
        0,
        1,
        [pltpu.SemaphoreType.DMA],
        n_far=1,
        out_far=(0,),
        aliases={1: 0},
    )(facing, probe_grad)
    return (obj_grad, probe_grad)


def solution(mesh):
    fine = Mesh(
        mesh.devices.reshape(8, 2, 2, 4, 4), ("y", "zh", "core", "x", "zl")
    )
    return jax.shard_map(
        body,
        mesh=fine,
        in_specs=(
            P(None, None, ROW, COL),
            P(),
            P(ROW, COL, None, None),
            P(ROW, COL),
            P(ROW, COL, None, None, None),
        ),
        out_specs=(P(None, None, ROW, COL), P()),
        check_vma=False,
    )
```

```python
import functools
import math

import jax
import jax.numpy as jnp
import ml_dtypes
import numpy as np
from jax import lax
from jax.experimental import pallas as pl
from jax.experimental.pallas import tpu as pltpu
from jax.sharding import Mesh
from jax.sharding import PartitionSpec as P

PHASE_COEF = 20.0
LOSS_WEIGHT = 0.125
ROW = ("y", "zh", "core")
COL = ("x", "zl")
VMEM_LIMIT = 48 * 1024 * 1024
TILE_COLS = 256


def split_bf16(table):
    high = table.astype(np.float32).astype(ml_dtypes.bfloat16)
    low = (table - high.astype(np.float64)).astype(np.float32).astype(ml_dtypes.bfloat16)
    return high, low


def tables(side):
    counter = np.arange(side)
    phase = 2.0 * math.pi / side * (counter[:, None] * counter[None, :] % side)
    fourier = np.exp(-1j * phase) / math.sqrt(side)
    spatial = ((counter + side // 2) % side - side // 2) / side
    factor = np.exp(-1j * PHASE_COEF * spatial * spatial)
    propagate = np.conj(fourier) @ (factor[:, None] * fourier)
    propagate = 0.5 * (propagate + propagate.T)
    parts = []
    for matrix in (propagate, fourier):
        for block in (matrix.real, matrix.imag, -matrix.imag):
            parts += split_bf16(block)
    return np.stack(parts)


def on_sides(tabs, which):
    def block(n, part):
        return tabs[6 * which + 2 * n + part]

    def square(a, b, c, d, part):
        return jnp.concatenate(
            [
                jnp.concatenate([block(a, part), block(b, part)], axis=1),
                jnp.concatenate([block(c, part), block(d, part)], axis=1),
            ],
            axis=0,
        )

    right = tuple(square(0, 1, 2, 0, part) for part in range(2))
    left = tuple(square(0, 2, 1, 0, part) for part in range(2))
    return right, left


def split(value):
    high = value.astype(jnp.bfloat16)
    low = (value - high.astype(jnp.float32)).astype(jnp.bfloat16)
    return high, low


def product(left, right):
    (left_high, left_low), (right_high, right_low) = left, right
    dot = functools.partial(jnp.dot, preferred_element_type=jnp.float32)
    return dot(left_high, right_high) + (dot(left_low, right_high) + dot(left_high, right_low))


def two_sided(real, imaginary, right, left, group=2):
    side = real[0].shape[0]
    middles = []
    for n in range(0, len(real), group):
        pairs = zip(real[n : n + group], imaginary[n : n + group])
        stacked = jnp.concatenate([jnp.concatenate(pair, axis=1) for pair in pairs], axis=0)
        middles.append(product(split(stacked), right))
    out_real, out_imaginary = [], []
    for middle in middles:
        blocks = [middle[m * side : (m + 1) * side] for m in range(group)]
        spread = jnp.concatenate(
            [
                jnp.concatenate([block[:, :side] for block in blocks], axis=1),
                jnp.concatenate([block[:, side:] for block in blocks], axis=1),
            ],
            axis=0,
        )
        out = product(left, split(spread))
        out_real += [out[:side, m * side : (m + 1) * side] for m in range(group)]
        out_imaginary += [out[side:, m * side : (m + 1) * side] for m in range(group)]
    return out_real, out_imaginary


def times(ar, ai, br, bi):
    return ar * br - ai * bi, ar * bi + ai * br


def times_conj(ar, ai, br, bi):
    return ar * br + ai * bi, ar * bi - ai * br


def model(window, probe, pattern, weight, tabs):
    (o0r, o1r), (o0i, o1i) = window
    qr, qi = probe
    modes = len(qr)
    prop_right, prop_left = on_sides(tabs, 0)
    four_right, four_left = on_sides(tabs, 1)
    e0 = [times(qr[m], qi[m], o0r, o0i) for m in range(modes)]
    a1r, a1i = two_sided([e[0] for e in e0], [e[1] for e in e0], prop_right, prop_left)
    e1 = [times(a1r[m], a1i[m], o1r, o1i) for m in range(modes)]
    gr, gi = two_sided([e[0] for e in e1], [e[1] for e in e1], four_right, four_left)
    intensity = gr[0] * gr[0] + gi[0] * gi[0]
    for m in range(1, modes):
        intensity = intensity + (gr[m] * gr[m] + gi[m] * gi[m])
    residue = (intensity - pattern) * (4.0 * LOSS_WEIGHT * weight)
    br, bi = two_sided(
        [residue * g for g in gr], [residue * g for g in gi], four_left, four_right
    )
    grad1 = [times_conj(a1r[m], a1i[m], br[m], bi[m]) for m in range(modes)]
    back = [times_conj(o1r, o1i, br[m], bi[m]) for m in range(modes)]
    cr, ci = two_sided([b[0] for b in back], [b[1] for b in back], prop_left, prop_right)
    grad0 = [times_conj(qr[m], qi[m], cr[m], ci[m]) for m in range(modes)]
    probe_grad = [times_conj(o0r, o0i, cr[m], ci[m]) for m in range(modes)]

    def over_modes(terms, part):
        return functools.reduce(lambda a, b: a + b, [t[part] for t in terms])

    window_grad = [
        [over_modes(grad0, 0), over_modes(grad1, 0)],
        [over_modes(grad0, 1), over_modes(grad1, 1)],
    ]
    return window_grad, probe_grad


def place_of(scan, rows, cols, half):
    row = scan[0] - (lax.axis_index(ROW) * rows - half)
    col = scan[1] - (lax.axis_index(COL) * cols - half)
    return row, col


def strips_at(half):
    core = lax.axis_index("core")
    return pl.multiple_of((1 - core) * 2 * half, 8), pl.multiple_of(core * 2 * half, 8)


def even_col():
    return lax.rem(lax.axis_index(COL), 2) == 0


def fill(frame, own, with_even, with_odd, part, layer):
    side = with_even.shape[2]
    half = side // 2
    cols = own.shape[3]
    plane = 2 * part + layer
    left = jnp.where(even_col(), with_odd[layer], with_even[layer])
    right = jnp.where(even_col(), with_even[layer], with_odd[layer])
    if part:
        left, right = pltpu.roll(left, half, 1), pltpu.roll(right, half, 1)
    frame[plane, :, 0:side] = left
    frame[plane, :, side : side + cols] = own[part, layer]
    frame[plane, :, side + cols :] = right


def cut(frame, plane, at, side):
    step = lax.rem(at, side)
    wide = frame[plane, :, pl.ds(pl.multiple_of(at - step, side), 2 * side)]
    return pltpu.roll(wide, lax.rem(2 * side - step, 2 * side), 1)[:, :side]


def column_kernel(scan, column, column_near):
    half = column.shape[1] // 2
    col = (scan[:, 1:2] - (lax.axis_index(COL) * TILE_COLS - half)).astype(jnp.float32)
    column[...] = jnp.broadcast_to(col, column.shape)
    column_near[...] = jnp.broadcast_to(col, column_near.shape)


def edges_kernel(own, with_even, with_odd):
    rows, cols = own.shape[2], own.shape[3]
    side = with_even.shape[2]
    half = side // 2
    inner = lax.broadcasted_iota(jnp.int32, (rows, side), 1) < half
    for layer in range(2):
        real, imaginary = own[0, layer], own[1, layer]
        left = jnp.where(inner, real[:, :side], pltpu.roll(imaginary[:, :side], half, 1))
        right = jnp.where(inner, pltpu.roll(imaginary[:, cols - side :], half, 1), real[:, cols - side :])
        with_even[layer] = jnp.where(even_col(), right, left)
        with_odd[layer] = jnp.where(even_col(), left, right)


def partner_column(column, cols):
    return jnp.clip(jnp.max(column[0:8, :]).astype(jnp.int32), 0, cols - 1)


def beyond_kernel(column, own, with_even, with_odd, to_beyond, frame):
    rows, cols = own.shape[2], own.shape[3]
    side = to_beyond.shape[1]
    col = partner_column(column, cols)
    for layer in range(2):
        for part in range(2):
            plane = 2 * part + layer
            fill(frame, own, with_even, with_odd, part, layer)
            to_beyond[pl.ds(plane * rows, rows), :] = cut(frame, plane, col + side // 2, side)
    to_beyond[pl.ds(4 * rows, 8), :] = jnp.zeros((8, side), jnp.float32)


def core_kernel(column, frame, to_core):
    side = to_core.shape[1]
    rows, cols = frame.shape[1], frame.shape[2] - 2 * side
    col = partner_column(column, cols)
    for plane in range(4):
        to_core[pl.ds(plane * rows, rows), :] = cut(frame, plane, col + side // 2, side)


def near_kernel(scan, frame, probe, pattern, tabs, near):
    rows, cols = frame.shape[1], frame.shape[2] - 2 * near.shape[1]
    side = near.shape[1]
    half = side // 2
    unused, col = place_of(scan, rows, cols, half)
    for plane in range(4):
        near[pl.ds(plane * rows, rows), :] = cut(frame, plane, col + half, side)


def main_kernel(
    scan, live, near, other, beyond, probe, pattern, tabs,
    keep, message_core, message_beyond, own_strip, column, shifted,
):
    side = probe.shape[-1]
    half = side // 2
    rows = own_strip.shape[0] // 4
    cols = TILE_COLS
    modes = probe.shape[1]
    row, col = place_of(scan, rows, cols, half)
    other_at, beyond_at = strips_at(half)
    for plane in range(4):
        at = pl.ds(plane * rows, rows)
        column[plane, half : half + rows, :] = near[at, :]
        column[plane, pl.ds(other_at, rows), :] = other[at, :]
        column[plane, pl.ds(beyond_at, rows), :] = beyond[at, :]
    tall = side + 8
    step = lax.rem(row, 8)
    base_row = pl.multiple_of(row - step, 8)

    def window_of(plane):
        high = column[plane, pl.ds(base_row, tall), :]
        return pltpu.roll(high, lax.rem(tall - step, tall), 0)[:side]

    window = [[window_of(2 * part + layer) for layer in range(2)] for part in range(2)]
    fields = [[probe[part, m] for m in range(modes)] for part in range(2)]
    weight = (live[0] > 0).astype(jnp.float32)
    window_grad, probe_grad = model(window, fields, pattern[0, 0, 0], weight, tabs)
    first = lax.axis_index("core") == 0
    for m in range(modes):
        at = pl.ds(m * side, side)
        real, imaginary = probe_grad[m]
        keep[at, :] = jnp.where(first, real, imaginary)
        message_core[at, :] = jnp.where(first, imaginary, real)
    base = modes * side
    shifted[...] = jnp.zeros_like(shifted)
    for part in range(2):
        for layer in range(2):
            plane = 2 * part + layer
            padded = jnp.concatenate(
                [window_grad[part][layer], jnp.zeros((8, side), jnp.float32)], axis=0
            )
            shifted[plane, pl.ds(base_row, tall), :] = pltpu.roll(padded, step, 0)
            at = pl.ds(plane * rows, rows)
            message_core[pl.ds(base + plane * rows, rows), :] = shifted[plane, pl.ds(other_at, rows), :]
            message_beyond[at, :] = shifted[plane, pl.ds(beyond_at, rows), :]
            own_strip[at, :] = shifted[plane, half : half + rows, :]
    offset = jnp.full((8, side), col.astype(jnp.float32))
    message_core[pl.ds(base + 4 * rows, 8), :] = offset
    message_beyond[pl.ds(4 * rows, 8), :] = offset


def merge_kernel(scan, own_strip, from_core, from_beyond, centre, with_even, with_odd, frame):
    side = own_strip.shape[1]
    half = side // 2
    rows = centre.shape[2]
    cols = centre.shape[3]
    base = from_core.shape[0] - from_beyond.shape[0]
    core_col = jnp.max(from_core[pl.ds(base + 4 * rows, 8), :]).astype(jnp.int32)
    beyond_col = jnp.max(from_beyond[pl.ds(4 * rows, 8), :]).astype(jnp.int32)
    unused, own_col = place_of(scan, rows, cols, half)
    lane = lax.broadcasted_iota(jnp.int32, (rows, side), 1)
    zero = jnp.zeros((rows, side), jnp.float32)
    frame[...] = jnp.zeros_like(frame)
    for source, first, col in (
        (own_strip, 0, own_col),
        (from_core, base, jnp.clip(core_col, 0, cols - 1)),
        (from_beyond, 0, jnp.clip(beyond_col, 0, cols - 1)),
    ):
        at = col + half
        step = lax.rem(at, side)
        near = pl.multiple_of(at - step, side)
        here, there = pl.ds(near, side), pl.ds(pl.multiple_of(near + side, side), side)
        for plane in range(4):
            strip = pltpu.roll(source[pl.ds(first + plane * rows, rows), :], step, 1)
            frame[plane, :, here] += jnp.where(lane >= step, strip, zero)
            frame[plane, :, there] += jnp.where(lane < step, strip, zero)
    inner = lane < half
    for layer in range(2):
        real, imaginary = layer, 2 + layer
        left = jnp.where(inner, pltpu.roll(frame[imaginary, :, 0:side], half, 1), frame[real, :, 0:side])
        right = jnp.where(inner, frame[real, :, side + cols :], pltpu.roll(frame[imaginary, :, side + cols :], half, 1))
        with_even[layer] = jnp.where(even_col(), right, left)
        with_odd[layer] = jnp.where(even_col(), left, right)
        centre[0, layer] = frame[real, :, side : side + cols]
        centre[1, layer] = frame[imaginary, :, side : side + cols]


def add_kernel(keep, message, out):
    out[...] = keep[...] + message[0 : keep.shape[0], :]


def sum_kernel(parts, copies):
    total = parts[0]
    for n in range(1, parts.shape[0]):
        total = total + parts[n]
    for n in range(copies.shape[0]):
        copies[n] = total


def finish_kernel(centre, with_even, with_odd, whole, out, probe_grad, total, sem, out_sem):
    copy = pltpu.make_async_copy(whole, probe_grad.at[lax.axis_index("core")], sem)
    copy.start()
    rows, cols = centre.shape[2], centre.shape[3]
    side = with_even.shape[2]
    half = side // 2
    inner = lax.broadcasted_iota(jnp.int32, (rows, side), 1) < half
    zero = jnp.zeros((rows, side), jnp.float32)
    for layer in range(2):
        left = jnp.where(even_col(), with_odd[layer], with_even[layer])
        right = jnp.where(even_col(), with_even[layer], with_odd[layer])
        for part in range(2):
            if part:
                left, right = pltpu.roll(left, half, 1), pltpu.roll(right, half, 1)
            value = centre[part, layer]
            total[part, layer, :, 0:side] = value[:, :side] + jnp.where(inner, left, zero)
            total[part, layer, :, cols - side :] = value[:, cols - side :] + jnp.where(inner, zero, right)
    out_copy = pltpu.make_async_copy(total, out, out_sem)
    out_copy.start()
    copy.wait()
    out_copy.wait()


def other_half_kernel(facing, half_done, probe_grad, sem):
    copy = pltpu.make_async_copy(facing, probe_grad.at[1 - lax.axis_index("core")], sem)
    copy.start()
    copy.wait()


def call(kernel, out_shape, n_scalars, n_in, scratch=(), cost=None, n_far=0, out_far=(), aliases=None):
    many = isinstance(out_shape, (list, tuple))
    vmem = pl.BlockSpec(memory_space=pltpu.VMEM)
    far = pl.BlockSpec(memory_space=pltpu.HBM)
    return pl.pallas_call(
        kernel,
        out_shape=out_shape,
        in_specs=[pl.BlockSpec(memory_space=pltpu.SMEM)] * n_scalars + [vmem] * n_in + [far] * n_far,
        out_specs=[far if n in out_far else vmem for n in range(len(out_shape))] if many else vmem,
        input_output_aliases=aliases or {},
        scratch_shapes=list(scratch),
        compiler_params=pltpu.CompilerParams(vmem_limit_bytes=VMEM_LIMIT),
        cost_estimate=cost,
    )


def both_ways(pairs):
    return pairs + [(j, i) for i, j in pairs]


def body(obj_field, probe, scan_pos, live_count, patterns):
    side = probe.shape[2]
    modes = probe.shape[1]
    half = side // 2
    rows, cols = obj_field.shape[2], obj_field.shape[3]
    n_row, n_col = lax.axis_size(ROW), lax.axis_size(COL)
    f32 = jnp.float32
    scan = scan_pos.reshape(2)
    live = live_count.reshape(1)
    swap = [(0, 1), (1, 0)]
    pairs = both_ways([(i, i + 1) for i in range(1, n_row - 1, 2)])
    even_pairs = both_ways([(i, i + 1) for i in range(0, n_col - 1, 2)])
    odd_pairs = both_ways([(i, i + 1) for i in range(1, n_col - 1, 2)])
    strip = 4 * rows

    def shape(*dims):
        return jax.ShapeDtypeStruct(dims, f32)

    edge = shape(2, rows, side)
    column, column_near = call(column_kernel, [shape(136, side), shape(8, side)], 0, 1)(
        scan.reshape(1, 2)
    )
    to_even, to_odd = call(edges_kernel, [edge, edge], 0, 1)(obj_field)
    column = lax.ppermute(column, ROW, pairs)
    with_even = lax.ppermute(to_even, COL, even_pairs)
    with_odd = lax.ppermute(to_odd, COL, odd_pairs)
    column_near = lax.ppermute(column_near, "core", swap)
    to_beyond, frame = call(
        beyond_kernel, [shape(strip + 8, side), shape(4, rows, cols + 2 * side)], 0, 4
    )(column, obj_field, with_even, with_odd)
    beyond = lax.ppermute(to_beyond, ROW, pairs)
    to_core = call(core_kernel, shape(strip, side), 0, 2)(column_near, frame)
    other = lax.ppermute(to_core, "core", swap)
    tabs = jnp.asarray(tables(side))
    small = pl.CostEstimate(flops=1000, bytes_accessed=1000, transcendentals=0)
    near = call(near_kernel, shape(strip, side), 1, 4, cost=small)(
        scan, frame, probe, patterns, tabs
    )
    near, other, beyond = lax.optimization_barrier((near, other, beyond))
    tall = pltpu.VMEM((4, 2 * half + rows, side), f32)
    keep, message_core, message_beyond, own_strip = call(
        main_kernel,
        [
            shape(modes * side, side),
            shape(modes * side + strip + 8, side),
            shape(strip + 8, side),
            shape(strip, side),
        ],
        2,
        6,
        [tall, tall],
    )(scan, live, near, other, beyond, probe, patterns, tabs)

    from_core = lax.ppermute(message_core, "core", swap)
    from_beyond = lax.ppermute(message_beyond, ROW, pairs)

    n_yx = lax.axis_size(("y", "x"))
    n_z = lax.axis_size(("zh", "zl"))
    total = modes * side
    chunk = total // n_yx
    summed = call(add_kernel, shape(total, side), 0, 2)(keep, from_core)
    spread = lax.all_to_all(summed.reshape(n_yx, chunk, side), ("y", "x"), 0, 0)

    centre, grad_even, grad_odd = call(
        merge_kernel,
        [shape(2, 2, rows, cols), edge, edge],
        1,
        3,
        [pltpu.VMEM((4, rows, cols + 2 * side), f32)],
    )(scan, own_strip, from_core, from_beyond)
    part = call(sum_kernel, shape(n_z, chunk, side), 0, 1)(spread)
    part = lax.all_to_all(part, ("zh", "zl"), 0, 0)
    part = call(sum_kernel, shape(n_yx, chunk, side), 0, 1)(part)
    got_even = lax.ppermute(grad_even, COL, even_pairs)
    part, got_even, grad_odd = lax.optimization_barrier((part, got_even, grad_odd))
    got_odd = lax.ppermute(grad_odd, COL, odd_pairs)
    whole = lax.all_to_all(part, ("y", "x"), 0, 0)
    whole, got_even, got_odd = lax.optimization_barrier((whole, got_even, got_odd))
    whole = whole.reshape(modes, side, side)
    facing = lax.ppermute(whole, "core", swap)
    obj_grad, probe_grad = call(
        finish_kernel,
        [shape(2, 2, rows, cols), shape(2, modes, side, side)],
        0,
        4,
        [pltpu.VMEM((2, 2, rows, cols), f32), pltpu.SemaphoreType.DMA, pltpu.SemaphoreType.DMA],
        out_far=(0, 1),
    )(centre, got_even, got_odd, whole)
    (probe_grad,) = call(
        other_half_kernel,
        [shape(2, modes, side, side)],
        0,
        1,
        [pltpu.SemaphoreType.DMA],
        n_far=1,
        out_far=(0,),
        aliases={1: 0},
    )(facing, probe_grad)
    return (obj_grad, probe_grad)


def solution(mesh):
    fine = Mesh(
        mesh.devices.reshape(8, 2, 2, 4, 4), ("y", "zh", "core", "x", "zl")
    )
    return jax.shard_map(
        body,
        mesh=fine,
        in_specs=(
            P(None, None, ROW, COL),
            P(),
            P(ROW, COL, None, None),
            P(ROW, COL),
            P(ROW, COL, None, None, None),
        ),
        out_specs=(P(None, None, ROW, COL), P()),
        check_vma=False,
    )
```

```python
import functools
import math

import jax
import jax.numpy as jnp
import ml_dtypes
import numpy as np
from jax import lax
from jax.experimental import pallas as pl
from jax.experimental.pallas import tpu as pltpu
from jax.sharding import Mesh
from jax.sharding import PartitionSpec as P

PHASE_COEF = 20.0
LOSS_WEIGHT = 0.125
ROW = ("y", "zh", "core")
COL = ("x", "zl")
VMEM_LIMIT = 48 * 1024 * 1024
TILE_COLS = 256


def split_bf16(table):
    high = table.astype(np.float32).astype(ml_dtypes.bfloat16)
    low = (table - high.astype(np.float64)).astype(np.float32).astype(ml_dtypes.bfloat16)
    return high, low


def tables(side):
    counter = np.arange(side)
    phase = 2.0 * math.pi / side * (counter[:, None] * counter[None, :] % side)
    fourier = np.exp(-1j * phase) / math.sqrt(side)
    spatial = ((counter + side // 2) % side - side // 2) / side
    factor = np.exp(-1j * PHASE_COEF * spatial * spatial)
    propagate = np.conj(fourier) @ (factor[:, None] * fourier)
    propagate = 0.5 * (propagate + propagate.T)
    parts = []
    for matrix in (propagate, fourier):
        for block in (matrix.real, matrix.imag, -matrix.imag):
            parts += split_bf16(block)
    return np.stack(parts)


def on_sides(tabs, which):
    def block(n, part):
        return tabs[6 * which + 2 * n + part]

    def square(a, b, c, d, part):
        return jnp.concatenate(
            [
                jnp.concatenate([block(a, part), block(b, part)], axis=1),
                jnp.concatenate([block(c, part), block(d, part)], axis=1),
            ],
            axis=0,
        )

    right = tuple(square(0, 1, 2, 0, part) for part in range(2))
    left = tuple(square(0, 2, 1, 0, part) for part in range(2))
    return right, left


def split(value):
    high = value.astype(jnp.bfloat16)
    low = (value - high.astype(jnp.float32)).astype(jnp.bfloat16)
    return high, low


def product(left, right):
    (left_high, left_low), (right_high, right_low) = left, right
    dot = functools.partial(jnp.dot, preferred_element_type=jnp.float32)
    return dot(left_high, right_high) + (dot(left_low, right_high) + dot(left_high, right_low))


def two_sided(real, imaginary, right, left, group=2):
    side = real[0].shape[0]
    middles = []
    for n in range(0, len(real), group):
        pairs = zip(real[n : n + group], imaginary[n : n + group])
        stacked = jnp.concatenate([jnp.concatenate(pair, axis=1) for pair in pairs], axis=0)
        middles.append(product(split(stacked), right))
    out_real, out_imaginary = [], []
    for middle in middles:
        blocks = [middle[m * side : (m + 1) * side] for m in range(group)]
        spread = jnp.concatenate(
            [
                jnp.concatenate([block[:, :side] for block in blocks], axis=1),
                jnp.concatenate([block[:, side:] for block in blocks], axis=1),
            ],
            axis=0,
        )
        out = product(left, split(spread))
        out_real += [out[:side, m * side : (m + 1) * side] for m in range(group)]
        out_imaginary += [out[side:, m * side : (m + 1) * side] for m in range(group)]
    return out_real, out_imaginary


def times(ar, ai, br, bi):
    return ar * br - ai * bi, ar * bi + ai * br


def times_conj(ar, ai, br, bi):
    return ar * br + ai * bi, ar * bi - ai * br


def model(window, probe, pattern, weight, tabs):
    (o0r, o1r), (o0i, o1i) = window
    qr, qi = probe
    modes = len(qr)
    prop_right, prop_left = on_sides(tabs, 0)
    four_right, four_left = on_sides(tabs, 1)
    e0 = [times(qr[m], qi[m], o0r, o0i) for m in range(modes)]
    a1r, a1i = two_sided([e[0] for e in e0], [e[1] for e in e0], prop_right, prop_left)
    e1 = [times(a1r[m], a1i[m], o1r, o1i) for m in range(modes)]
    gr, gi = two_sided([e[0] for e in e1], [e[1] for e in e1], four_right, four_left)
    intensity = gr[0] * gr[0] + gi[0] * gi[0]
    for m in range(1, modes):
        intensity = intensity + (gr[m] * gr[m] + gi[m] * gi[m])
    residue = (intensity - pattern) * (4.0 * LOSS_WEIGHT * weight)
    br, bi = two_sided(
        [residue * g for g in gr], [residue * g for g in gi], four_left, four_right
    )
    grad1 = [times_conj(a1r[m], a1i[m], br[m], bi[m]) for m in range(modes)]
    back = [times_conj(o1r, o1i, br[m], bi[m]) for m in range(modes)]
    cr, ci = two_sided([b[0] for b in back], [b[1] for b in back], prop_left, prop_right)
    grad0 = [times_conj(qr[m], qi[m], cr[m], ci[m]) for m in range(modes)]
    probe_grad = [times_conj(o0r, o0i, cr[m], ci[m]) for m in range(modes)]

    def over_modes(terms, part):
        return functools.reduce(lambda a, b: a + b, [t[part] for t in terms])

    window_grad = [
        [over_modes(grad0, 0), over_modes(grad1, 0)],
        [over_modes(grad0, 1), over_modes(grad1, 1)],
    ]
    return window_grad, probe_grad


def place_of(scan, rows, cols, half):
    row = scan[0] - (lax.axis_index(ROW) * rows - half)
    col = scan[1] - (lax.axis_index(COL) * cols - half)
    return row, col


def strips_at(half):
    core = lax.axis_index("core")
    return pl.multiple_of((1 - core) * 2 * half, 8), pl.multiple_of(core * 2 * half, 8)


def even_col():
    return lax.rem(lax.axis_index(COL), 2) == 0


def fill(frame, own, with_even, with_odd, part, layer):
    side = with_even.shape[2]
    half = side // 2
    cols = own.shape[3]
    plane = 2 * part + layer
    left = jnp.where(even_col(), with_odd[layer], with_even[layer])
    right = jnp.where(even_col(), with_even[layer], with_odd[layer])
    if part:
        left, right = pltpu.roll(left, half, 1), pltpu.roll(right, half, 1)
    frame[plane, :, 0:side] = left
    frame[plane, :, side : side + cols] = own[part, layer]
    frame[plane, :, side + cols :] = right


def cut(frame, plane, at, side):
    step = lax.rem(at, side)
    wide = frame[plane, :, pl.ds(pl.multiple_of(at - step, side), 2 * side)]
    return pltpu.roll(wide, lax.rem(2 * side - step, 2 * side), 1)[:, :side]


def column_kernel(scan, column, column_near):
    half = column.shape[1] // 2
    col = (scan[:, 1:2] - (lax.axis_index(COL) * TILE_COLS - half)).astype(jnp.float32)
    column[...] = jnp.broadcast_to(col, column.shape)
    column_near[...] = jnp.broadcast_to(col, column_near.shape)


def edges_kernel(own, with_even, with_odd):
    rows, cols = own.shape[2], own.shape[3]
    side = with_even.shape[2]
    half = side // 2
    inner = lax.broadcasted_iota(jnp.int32, (rows, side), 1) < half
    for layer in range(2):
        real, imaginary = own[0, layer], own[1, layer]
        left = jnp.where(inner, real[:, :side], pltpu.roll(imaginary[:, :side], half, 1))
        right = jnp.where(inner, pltpu.roll(imaginary[:, cols - side :], half, 1), real[:, cols - side :])
        with_even[layer] = jnp.where(even_col(), right, left)
        with_odd[layer] = jnp.where(even_col(), left, right)


def partner_column(column, cols):
    return jnp.clip(jnp.max(column[0:8, :]).astype(jnp.int32), 0, cols - 1)


def beyond_kernel(column, own, with_even, with_odd, to_beyond, frame):
    rows, cols = own.shape[2], own.shape[3]
    side = to_beyond.shape[1]
    col = partner_column(column, cols)
    for layer in range(2):
        for part in range(2):
            plane = 2 * part + layer
            fill(frame, own, with_even, with_odd, part, layer)
            to_beyond[pl.ds(plane * rows, rows), :] = cut(frame, plane, col + side // 2, side)
    to_beyond[pl.ds(4 * rows, 8), :] = jnp.zeros((8, side), jnp.float32)


def core_kernel(column, frame, to_core):
    side = to_core.shape[1]
    rows, cols = frame.shape[1], frame.shape[2] - 2 * side
    col = partner_column(column, cols)
    for plane in range(4):
        to_core[pl.ds(plane * rows, rows), :] = cut(frame, plane, col + side // 2, side)


def near_kernel(scan, frame, probe, pattern, tabs, near):
    rows, cols = frame.shape[1], frame.shape[2] - 2 * near.shape[1]
    side = near.shape[1]
    half = side // 2
    unused, col = place_of(scan, rows, cols, half)
    for plane in range(4):
        near[pl.ds(plane * rows, rows), :] = cut(frame, plane, col + half, side)


def main_kernel(
    scan, live, near, other, beyond, probe, pattern, tabs,
    keep, message_core, message_beyond, own_strip, column, shifted,
):
    side = probe.shape[-1]
    half = side // 2
    rows = own_strip.shape[0] // 4
    cols = TILE_COLS
    modes = probe.shape[1]
    row, col = place_of(scan, rows, cols, half)
    other_at, beyond_at = strips_at(half)
    for plane in range(4):
        at = pl.ds(plane * rows, rows)
        column[plane, half : half + rows, :] = near[at, :]
        column[plane, pl.ds(other_at, rows), :] = other[at, :]
        column[plane, pl.ds(beyond_at, rows), :] = beyond[at, :]
    tall = side + 8
    step = lax.rem(row, 8)
    base_row = pl.multiple_of(row - step, 8)

    def window_of(plane):
        high = column[plane, pl.ds(base_row, tall), :]
        return pltpu.roll(high, lax.rem(tall - step, tall), 0)[:side]

    window = [[window_of(2 * part + layer) for layer in range(2)] for part in range(2)]
    fields = [[probe[part, m] for m in range(modes)] for part in range(2)]
    weight = (live[0] > 0).astype(jnp.float32)
    window_grad, probe_grad = model(window, fields, pattern[0, 0, 0], weight, tabs)
    first = lax.axis_index("core") == 0
    for m in range(modes):
        at = pl.ds(m * side, side)
        real, imaginary = probe_grad[m]
        keep[at, :] = jnp.where(first, real, imaginary)
        message_core[at, :] = jnp.where(first, imaginary, real)
    base = modes * side
    shifted[...] = jnp.zeros_like(shifted)
    for part in range(2):
        for layer in range(2):
            plane = 2 * part + layer
            padded = jnp.concatenate(
                [window_grad[part][layer], jnp.zeros((8, side), jnp.float32)], axis=0
            )
            shifted[plane, pl.ds(base_row, tall), :] = pltpu.roll(padded, step, 0)
            at = pl.ds(plane * rows, rows)
            message_core[pl.ds(base + plane * rows, rows), :] = shifted[plane, pl.ds(other_at, rows), :]
            message_beyond[at, :] = shifted[plane, pl.ds(beyond_at, rows), :]
            own_strip[at, :] = shifted[plane, half : half + rows, :]
    offset = jnp.full((8, side), col.astype(jnp.float32))
    message_core[pl.ds(base + 4 * rows, 8), :] = offset
    message_beyond[pl.ds(4 * rows, 8), :] = offset


def merge_kernel(scan, own_strip, from_core, from_beyond, centre, with_even, with_odd, frame):
    side = own_strip.shape[1]
    half = side // 2
    rows = centre.shape[2]
    cols = centre.shape[3]
    base = from_core.shape[0] - from_beyond.shape[0]
    core_col = jnp.max(from_core[pl.ds(base + 4 * rows, 8), :]).astype(jnp.int32)
    beyond_col = jnp.max(from_beyond[pl.ds(4 * rows, 8), :]).astype(jnp.int32)
    unused, own_col = place_of(scan, rows, cols, half)
    lane = lax.broadcasted_iota(jnp.int32, (rows, side), 1)
    zero = jnp.zeros((rows, side), jnp.float32)
    frame[...] = jnp.zeros_like(frame)
    for source, first, col in (
        (own_strip, 0, own_col),
        (from_core, base, jnp.clip(core_col, 0, cols - 1)),
        (from_beyond, 0, jnp.clip(beyond_col, 0, cols - 1)),
    ):
        at = col + half
        step = lax.rem(at, side)
        near = pl.multiple_of(at - step, side)
        here, there = pl.ds(near, side), pl.ds(pl.multiple_of(near + side, side), side)
        for plane in range(4):
            strip = pltpu.roll(source[pl.ds(first + plane * rows, rows), :], step, 1)
            frame[plane, :, here] += jnp.where(lane >= step, strip, zero)
            frame[plane, :, there] += jnp.where(lane < step, strip, zero)
    inner = lane < half
    for layer in range(2):
        real, imaginary = layer, 2 + layer
        left = jnp.where(inner, pltpu.roll(frame[imaginary, :, 0:side], half, 1), frame[real, :, 0:side])
        right = jnp.where(inner, frame[real, :, side + cols :], pltpu.roll(frame[imaginary, :, side + cols :], half, 1))
        with_even[layer] = jnp.where(even_col(), right, left)
        with_odd[layer] = jnp.where(even_col(), left, right)
        centre[0, layer] = frame[real, :, side : side + cols]
        centre[1, layer] = frame[imaginary, :, side : side + cols]


def add_kernel(keep, message, out):
    out[...] = keep[...] + message[0 : keep.shape[0], :]


def sum_kernel(parts, copies):
    total = parts[0]
    for n in range(1, parts.shape[0]):
        total = total + parts[n]
    for n in range(copies.shape[0]):
        copies[n] = total


def finish_kernel(centre, with_even, with_odd, whole, out, probe_grad, total, sem, out_sem):
    copy = pltpu.make_async_copy(whole, probe_grad.at[lax.axis_index("core")], sem)
    copy.start()
    rows, cols = centre.shape[2], centre.shape[3]
    side = with_even.shape[2]
    half = side // 2
    inner = lax.broadcasted_iota(jnp.int32, (rows, side), 1) < half
    zero = jnp.zeros((rows, side), jnp.float32)
    for layer in range(2):
        left = jnp.where(even_col(), with_odd[layer], with_even[layer])
        right = jnp.where(even_col(), with_even[layer], with_odd[layer])
        for part in range(2):
            if part:
                left, right = pltpu.roll(left, half, 1), pltpu.roll(right, half, 1)
            value = centre[part, layer]
            total[part, layer, :, 0:side] = value[:, :side] + jnp.where(inner, left, zero)
            total[part, layer, :, cols - side :] = value[:, cols - side :] + jnp.where(inner, zero, right)
    out_copy = pltpu.make_async_copy(total, out, out_sem)
    out_copy.start()
    copy.wait()
    out_copy.wait()


def other_half_kernel(facing, half_done, probe_grad, sem):
    copy = pltpu.make_async_copy(facing, probe_grad.at[1 - lax.axis_index("core")], sem)
    copy.start()
    copy.wait()


def call(kernel, out_shape, n_scalars, n_in, scratch=(), cost=None, n_far=0, out_far=(), aliases=None):
    many = isinstance(out_shape, (list, tuple))
    vmem = pl.BlockSpec(memory_space=pltpu.VMEM)
    far = pl.BlockSpec(memory_space=pltpu.HBM)
    return pl.pallas_call(
        kernel,
        out_shape=out_shape,
        in_specs=[pl.BlockSpec(memory_space=pltpu.SMEM)] * n_scalars + [vmem] * n_in + [far] * n_far,
        out_specs=[far if n in out_far else vmem for n in range(len(out_shape))] if many else vmem,
        input_output_aliases=aliases or {},
        scratch_shapes=list(scratch),
        compiler_params=pltpu.CompilerParams(vmem_limit_bytes=VMEM_LIMIT),
        cost_estimate=cost,
    )


def both_ways(pairs):
    return pairs + [(j, i) for i, j in pairs]


def body(obj_field, probe, scan_pos, live_count, patterns):
    side = probe.shape[2]
    modes = probe.shape[1]
    half = side // 2
    rows, cols = obj_field.shape[2], obj_field.shape[3]
    n_row, n_col = lax.axis_size(ROW), lax.axis_size(COL)
    f32 = jnp.float32
    scan = scan_pos.reshape(2)
    live = live_count.reshape(1)
    swap = [(0, 1), (1, 0)]
    pairs = both_ways([(i, i + 1) for i in range(1, n_row - 1, 2)])
    even_pairs = both_ways([(i, i + 1) for i in range(0, n_col - 1, 2)])
    odd_pairs = both_ways([(i, i + 1) for i in range(1, n_col - 1, 2)])
    strip = 4 * rows

    def shape(*dims):
        return jax.ShapeDtypeStruct(dims, f32)

    edge = shape(2, rows, side)
    large = pl.CostEstimate(flops=4_000_000_000, bytes_accessed=0, transcendentals=0)
    column, column_near = call(
        column_kernel, [shape(136, side), shape(8, side)], 0, 1, cost=large
    )(scan.reshape(1, 2))
    to_even, to_odd = call(edges_kernel, [edge, edge], 0, 1)(obj_field)
    column = lax.ppermute(column, ROW, pairs)
    with_even = lax.ppermute(to_even, COL, even_pairs)
    with_odd = lax.ppermute(to_odd, COL, odd_pairs)
    column_near = lax.ppermute(column_near, "core", swap)
    to_beyond, frame = call(
        beyond_kernel, [shape(strip + 8, side), shape(4, rows, cols + 2 * side)], 0, 4
    )(column, obj_field, with_even, with_odd)
    beyond = lax.ppermute(to_beyond, ROW, pairs)
    to_core = call(core_kernel, shape(strip, side), 0, 2)(column_near, frame)
    other = lax.ppermute(to_core, "core", swap)
    tabs = jnp.asarray(tables(side))
    small = pl.CostEstimate(flops=1000, bytes_accessed=1000, transcendentals=0)
    near = call(near_kernel, shape(strip, side), 1, 4, cost=small)(
        scan, frame, probe, patterns, tabs
    )
    near, other, beyond = lax.optimization_barrier((near, other, beyond))
    tall = pltpu.VMEM((4, 2 * half + rows, side), f32)
    keep, message_core, message_beyond, own_strip = call(
        main_kernel,
        [
            shape(modes * side, side),
            shape(modes * side + strip + 8, side),
            shape(strip + 8, side),
            shape(strip, side),
        ],
        2,
        6,
        [tall, tall],
    )(scan, live, near, other, beyond, probe, patterns, tabs)

    from_core = lax.ppermute(message_core, "core", swap)
    from_beyond = lax.ppermute(message_beyond, ROW, pairs)

    n_yx = lax.axis_size(("y", "x"))
    n_z = lax.axis_size(("zh", "zl"))
    total = modes * side
    chunk = total // n_yx
    summed = call(add_kernel, shape(total, side), 0, 2)(keep, from_core)
    spread = lax.all_to_all(summed.reshape(n_yx, chunk, side), ("y", "x"), 0, 0)

    centre, grad_even, grad_odd = call(
        merge_kernel,
        [shape(2, 2, rows, cols), edge, edge],
        1,
        3,
        [pltpu.VMEM((4, rows, cols + 2 * side), f32)],
    )(scan, own_strip, from_core, from_beyond)
    part = call(sum_kernel, shape(n_z, chunk, side), 0, 1)(spread)
    part = lax.all_to_all(part, ("zh", "zl"), 0, 0)
    part = call(sum_kernel, shape(n_yx, chunk, side), 0, 1)(part)
    got_even = lax.ppermute(grad_even, COL, even_pairs)
    part, got_even, grad_odd = lax.optimization_barrier((part, got_even, grad_odd))
    got_odd = lax.ppermute(grad_odd, COL, odd_pairs)
    whole = lax.all_to_all(part, ("y", "x"), 0, 0)
    whole, got_even, got_odd = lax.optimization_barrier((whole, got_even, got_odd))
    whole = whole.reshape(modes, side, side)
    facing = lax.ppermute(whole, "core", swap)
    obj_grad, probe_grad = call(
        finish_kernel,
        [shape(2, 2, rows, cols), shape(2, modes, side, side)],
        0,
        4,
        [pltpu.VMEM((2, 2, rows, cols), f32), pltpu.SemaphoreType.DMA, pltpu.SemaphoreType.DMA],
        out_far=(0, 1),
    )(centre, got_even, got_odd, whole)
    (probe_grad,) = call(
        other_half_kernel,
        [shape(2, modes, side, side)],
        0,
        1,
        [pltpu.SemaphoreType.DMA],
        n_far=1,
        out_far=(0,),
        aliases={1: 0},
    )(facing, probe_grad)
    return (obj_grad, probe_grad)


def solution(mesh):
    fine = Mesh(
        mesh.devices.reshape(8, 2, 2, 4, 4), ("y", "zh", "core", "x", "zl")
    )
    return jax.shard_map(
        body,
        mesh=fine,
        in_specs=(
            P(None, None, ROW, COL),
            P(),
            P(ROW, COL, None, None),
            P(ROW, COL),
            P(ROW, COL, None, None, None),
        ),
        out_specs=(P(None, None, ROW, COL), P()),
        check_vma=False,
    )
```

```python
import functools
import math

import jax
import jax.numpy as jnp
import ml_dtypes
import numpy as np
from jax import lax
from jax.experimental import pallas as pl
from jax.experimental.pallas import tpu as pltpu
from jax.sharding import Mesh
from jax.sharding import PartitionSpec as P

PHASE_COEF = 20.0
LOSS_WEIGHT = 0.125
ROW = ("y", "zh", "core")
COL = ("x", "zl")
VMEM_LIMIT = 48 * 1024 * 1024
TILE_COLS = 256


def split_bf16(table):
    high = table.astype(np.float32).astype(ml_dtypes.bfloat16)
    low = (table - high.astype(np.float64)).astype(np.float32).astype(ml_dtypes.bfloat16)
    return high, low


def tables(side):
    counter = np.arange(side)
    phase = 2.0 * math.pi / side * (counter[:, None] * counter[None, :] % side)
    fourier = np.exp(-1j * phase) / math.sqrt(side)
    spatial = ((counter + side // 2) % side - side // 2) / side
    factor = np.exp(-1j * PHASE_COEF * spatial * spatial)
    propagate = np.conj(fourier) @ (factor[:, None] * fourier)
    propagate = 0.5 * (propagate + propagate.T)
    parts = []
    for matrix in (propagate, fourier):
        for block in (matrix.real, matrix.imag, -matrix.imag):
            parts += split_bf16(block)
    return np.stack(parts)


def on_sides(tabs, which):
    def block(n, part):
        return tabs[6 * which + 2 * n + part]

    def square(a, b, c, d, part):
        return jnp.concatenate(
            [
                jnp.concatenate([block(a, part), block(b, part)], axis=1),
                jnp.concatenate([block(c, part), block(d, part)], axis=1),
            ],
            axis=0,
        )

    right = tuple(square(0, 1, 2, 0, part) for part in range(2))
    left = tuple(square(0, 2, 1, 0, part) for part in range(2))
    return right, left


def split(value):
    high = value.astype(jnp.bfloat16)
    low = (value - high.astype(jnp.float32)).astype(jnp.bfloat16)
    return high, low


def product(left, right):
    (left_high, left_low), (right_high, right_low) = left, right
    dot = functools.partial(jnp.dot, preferred_element_type=jnp.float32)
    return dot(left_high, right_high) + (dot(left_low, right_high) + dot(left_high, right_low))


def two_sided(real, imaginary, right, left, group=2):
    side = real[0].shape[0]
    middles = []
    for n in range(0, len(real), group):
        pairs = zip(real[n : n + group], imaginary[n : n + group])
        stacked = jnp.concatenate([jnp.concatenate(pair, axis=1) for pair in pairs], axis=0)
        middles.append(product(split(stacked), right))
    out_real, out_imaginary = [], []
    for middle in middles:
        blocks = [middle[m * side : (m + 1) * side] for m in range(group)]
        spread = jnp.concatenate(
            [
                jnp.concatenate([block[:, :side] for block in blocks], axis=1),
                jnp.concatenate([block[:, side:] for block in blocks], axis=1),
            ],
            axis=0,
        )
        out = product(left, split(spread))
        out_real += [out[:side, m * side : (m + 1) * side] for m in range(group)]
        out_imaginary += [out[side:, m * side : (m + 1) * side] for m in range(group)]
    return out_real, out_imaginary


def times(ar, ai, br, bi):
    return ar * br - ai * bi, ar * bi + ai * br


def times_conj(ar, ai, br, bi):
    return ar * br + ai * bi, ar * bi - ai * br


def model(window, probe, pattern, weight, tabs):
    (o0r, o1r), (o0i, o1i) = window
    qr, qi = probe
    modes = len(qr)
    prop_right, prop_left = on_sides(tabs, 0)
    four_right, four_left = on_sides(tabs, 1)
    e0 = [times(qr[m], qi[m], o0r, o0i) for m in range(modes)]
    a1r, a1i = two_sided([e[0] for e in e0], [e[1] for e in e0], prop_right, prop_left)
    e1 = [times(a1r[m], a1i[m], o1r, o1i) for m in range(modes)]
    gr, gi = two_sided([e[0] for e in e1], [e[1] for e in e1], four_right, four_left)
    intensity = gr[0] * gr[0] + gi[0] * gi[0]
    for m in range(1, modes):
        intensity = intensity + (gr[m] * gr[m] + gi[m] * gi[m])
    residue = (intensity - pattern) * (4.0 * LOSS_WEIGHT * weight)
    br, bi = two_sided(
        [residue * g for g in gr], [residue * g for g in gi], four_left, four_right
    )
    grad1 = [times_conj(a1r[m], a1i[m], br[m], bi[m]) for m in range(modes)]
    back = [times_conj(o1r, o1i, br[m], bi[m]) for m in range(modes)]
    cr, ci = two_sided([b[0] for b in back], [b[1] for b in back], prop_left, prop_right)
    grad0 = [times_conj(qr[m], qi[m], cr[m], ci[m]) for m in range(modes)]
    probe_grad = [times_conj(o0r, o0i, cr[m], ci[m]) for m in range(modes)]

    def over_modes(terms, part):
        return functools.reduce(lambda a, b: a + b, [t[part] for t in terms])

    window_grad = [
        [over_modes(grad0, 0), over_modes(grad1, 0)],
        [over_modes(grad0, 1), over_modes(grad1, 1)],
    ]
    return window_grad, probe_grad


def place_of(scan, rows, cols, half):
    row = scan[0] - (lax.axis_index(ROW) * rows - half)
    col = scan[1] - (lax.axis_index(COL) * cols - half)
    return row, col


def strips_at(half):
    core = lax.axis_index("core")
    return pl.multiple_of((1 - core) * 2 * half, 8), pl.multiple_of(core * 2 * half, 8)


def even_col():
    return lax.rem(lax.axis_index(COL), 2) == 0


def fill(frame, own, with_even, with_odd, part, layer):
    side = with_even.shape[2]
    half = side // 2
    cols = own.shape[3]
    plane = 2 * part + layer
    left = jnp.where(even_col(), with_odd[layer], with_even[layer])
    right = jnp.where(even_col(), with_even[layer], with_odd[layer])
    if part:
        left, right = pltpu.roll(left, half, 1), pltpu.roll(right, half, 1)
    frame[plane, :, 0:side] = left
    frame[plane, :, side : side + cols] = own[part, layer]
    frame[plane, :, side + cols :] = right


def cut(frame, plane, at, side):
    step = lax.rem(at, side)
    wide = frame[plane, :, pl.ds(pl.multiple_of(at - step, side), 2 * side)]
    return pltpu.roll(wide, lax.rem(2 * side - step, 2 * side), 1)[:, :side]


def column_kernel(scan, column, column_near):
    half = column.shape[1] // 2
    col = (scan[:, 1:2] - (lax.axis_index(COL) * TILE_COLS - half)).astype(jnp.float32)
    column[...] = jnp.broadcast_to(col, column.shape)
    column_near[...] = jnp.broadcast_to(col, column_near.shape)


def edges_kernel(own, with_even, with_odd):
    rows, cols = own.shape[2], own.shape[3]
    side = with_even.shape[2]
    half = side // 2
    inner = lax.broadcasted_iota(jnp.int32, (rows, side), 1) < half
    for layer in range(2):
        real, imaginary = own[0, layer], own[1, layer]
        left = jnp.where(inner, real[:, :side], pltpu.roll(imaginary[:, :side], half, 1))
        right = jnp.where(inner, pltpu.roll(imaginary[:, cols - side :], half, 1), real[:, cols - side :])
        with_even[layer] = jnp.where(even_col(), right, left)
        with_odd[layer] = jnp.where(even_col(), left, right)


def partner_column(column, cols):
    return jnp.clip(jnp.max(column[0:8, :]).astype(jnp.int32), 0, cols - 1)


def beyond_kernel(column, own, with_even, with_odd, to_beyond, frame):
    rows, cols = own.shape[2], own.shape[3]
    side = to_beyond.shape[1]
    col = partner_column(column, cols)
    for layer in range(2):
        for part in range(2):
            plane = 2 * part + layer
            fill(frame, own, with_even, with_odd, part, layer)
            to_beyond[pl.ds(plane * rows, rows), :] = cut(frame, plane, col + side // 2, side)
    to_beyond[pl.ds(4 * rows, 8), :] = jnp.zeros((8, side), jnp.float32)


def core_kernel(column, frame, to_core):
    side = to_core.shape[1]
    rows, cols = frame.shape[1], frame.shape[2] - 2 * side
    col = partner_column(column, cols)
    for plane in range(4):
        to_core[pl.ds(plane * rows, rows), :] = cut(frame, plane, col + side // 2, side)


def near_kernel(scan, frame, probe, pattern, tabs, near):
    rows, cols = frame.shape[1], frame.shape[2] - 2 * near.shape[1]
    side = near.shape[1]
    half = side // 2
    unused, col = place_of(scan, rows, cols, half)
    for plane in range(4):
        near[pl.ds(plane * rows, rows), :] = cut(frame, plane, col + half, side)


def main_kernel(
    scan, live, near, other, beyond, probe, pattern, tabs,
    keep, message_core, message_beyond, own_strip, column, shifted,
):
    side = probe.shape[-1]
    half = side // 2
    rows = own_strip.shape[0] // 4
    cols = TILE_COLS
    modes = probe.shape[1]
    row, col = place_of(scan, rows, cols, half)
    other_at, beyond_at = strips_at(half)
    for plane in range(4):
        at = pl.ds(plane * rows, rows)
        column[plane, half : half + rows, :] = near[at, :]
        column[plane, pl.ds(other_at, rows), :] = other[at, :]
        column[plane, pl.ds(beyond_at, rows), :] = beyond[at, :]
    tall = side + 8
    step = lax.rem(row, 8)
    base_row = pl.multiple_of(row - step, 8)

    def window_of(plane):
        high = column[plane, pl.ds(base_row, tall), :]
        return pltpu.roll(high, lax.rem(tall - step, tall), 0)[:side]

    window = [[window_of(2 * part + layer) for layer in range(2)] for part in range(2)]
    fields = [[probe[part, m] for m in range(modes)] for part in range(2)]
    weight = (live[0] > 0).astype(jnp.float32)
    window_grad, probe_grad = model(window, fields, pattern[0, 0, 0], weight, tabs)
    first = lax.axis_index("core") == 0
    for m in range(modes):
        at = pl.ds(m * side, side)
        real, imaginary = probe_grad[m]
        keep[at, :] = jnp.where(first, real, imaginary)
        message_core[at, :] = jnp.where(first, imaginary, real)
    base = modes * side
    shifted[...] = jnp.zeros_like(shifted)
    for part in range(2):
        for layer in range(2):
            plane = 2 * part + layer
            padded = jnp.concatenate(
                [window_grad[part][layer], jnp.zeros((8, side), jnp.float32)], axis=0
            )
            shifted[plane, pl.ds(base_row, tall), :] = pltpu.roll(padded, step, 0)
            at = pl.ds(plane * rows, rows)
            message_core[pl.ds(base + plane * rows, rows), :] = shifted[plane, pl.ds(other_at, rows), :]
            message_beyond[at, :] = shifted[plane, pl.ds(beyond_at, rows), :]
            own_strip[at, :] = shifted[plane, half : half + rows, :]
    offset = jnp.full((8, side), col.astype(jnp.float32))
    message_core[pl.ds(base + 4 * rows, 8), :] = offset
    message_beyond[pl.ds(4 * rows, 8), :] = offset


def merge_kernel(scan, own_strip, from_core, from_beyond, centre, with_even, with_odd, frame):
    side = own_strip.shape[1]
    half = side // 2
    rows = centre.shape[2]
    cols = centre.shape[3]
    base = from_core.shape[0] - from_beyond.shape[0]
    core_col = jnp.max(from_core[pl.ds(base + 4 * rows, 8), :]).astype(jnp.int32)
    beyond_col = jnp.max(from_beyond[pl.ds(4 * rows, 8), :]).astype(jnp.int32)
    unused, own_col = place_of(scan, rows, cols, half)
    lane = lax.broadcasted_iota(jnp.int32, (rows, side), 1)
    zero = jnp.zeros((rows, side), jnp.float32)
    frame[...] = jnp.zeros_like(frame)
    for source, first, col in (
        (own_strip, 0, own_col),
        (from_core, base, jnp.clip(core_col, 0, cols - 1)),
        (from_beyond, 0, jnp.clip(beyond_col, 0, cols - 1)),
    ):
        at = col + half
        step = lax.rem(at, side)
        near = pl.multiple_of(at - step, side)
        here, there = pl.ds(near, side), pl.ds(pl.multiple_of(near + side, side), side)
        for plane in range(4):
            strip = pltpu.roll(source[pl.ds(first + plane * rows, rows), :], step, 1)
            frame[plane, :, here] += jnp.where(lane >= step, strip, zero)
            frame[plane, :, there] += jnp.where(lane < step, strip, zero)
    inner = lane < half
    for layer in range(2):
        real, imaginary = layer, 2 + layer
        left = jnp.where(inner, pltpu.roll(frame[imaginary, :, 0:side], half, 1), frame[real, :, 0:side])
        right = jnp.where(inner, frame[real, :, side + cols :], pltpu.roll(frame[imaginary, :, side + cols :], half, 1))
        with_even[layer] = jnp.where(even_col(), right, left)
        with_odd[layer] = jnp.where(even_col(), left, right)
        centre[0, layer] = frame[real, :, side : side + cols]
        centre[1, layer] = frame[imaginary, :, side : side + cols]


def add_kernel(keep, message, out):
    out[...] = keep[...] + message[0 : keep.shape[0], :]


def sum_kernel(parts, copies):
    total = parts[0]
    for n in range(1, parts.shape[0]):
        total = total + parts[n]
    for n in range(copies.shape[0]):
        copies[n] = total


def finish_kernel(centre, with_even, with_odd, whole, out, probe_grad, total, sem, out_sem):
    copy = pltpu.make_async_copy(whole, probe_grad.at[lax.axis_index("core")], sem)
    copy.start()
    rows, cols = centre.shape[2], centre.shape[3]
    side = with_even.shape[2]
    half = side // 2
    inner = lax.broadcasted_iota(jnp.int32, (rows, side), 1) < half
    zero = jnp.zeros((rows, side), jnp.float32)
    for layer in range(2):
        left = jnp.where(even_col(), with_odd[layer], with_even[layer])
        right = jnp.where(even_col(), with_even[layer], with_odd[layer])
        for part in range(2):
            if part:
                left, right = pltpu.roll(left, half, 1), pltpu.roll(right, half, 1)
            value = centre[part, layer]
            total[part, layer, :, 0:side] = value[:, :side] + jnp.where(inner, left, zero)
            total[part, layer, :, cols - side :] = value[:, cols - side :] + jnp.where(inner, zero, right)
    out_copy = pltpu.make_async_copy(total, out, out_sem)
    out_copy.start()
    copy.wait()
    out_copy.wait()


def other_half_kernel(facing, half_done, probe_grad, sem):
    copy = pltpu.make_async_copy(facing, probe_grad.at[1 - lax.axis_index("core")], sem)
    copy.start()
    copy.wait()


def call(kernel, out_shape, n_scalars, n_in, scratch=(), cost=None, n_far=0, out_far=(), aliases=None):
    many = isinstance(out_shape, (list, tuple))
    vmem = pl.BlockSpec(memory_space=pltpu.VMEM)
    far = pl.BlockSpec(memory_space=pltpu.HBM)
    return pl.pallas_call(
        kernel,
        out_shape=out_shape,
        in_specs=[pl.BlockSpec(memory_space=pltpu.SMEM)] * n_scalars + [vmem] * n_in + [far] * n_far,
        out_specs=[far if n in out_far else vmem for n in range(len(out_shape))] if many else vmem,
        input_output_aliases=aliases or {},
        scratch_shapes=list(scratch),
        compiler_params=pltpu.CompilerParams(vmem_limit_bytes=VMEM_LIMIT),
        cost_estimate=cost,
    )


def both_ways(pairs):
    return pairs + [(j, i) for i, j in pairs]


def body(obj_field, probe, scan_pos, live_count, patterns):
    side = probe.shape[2]
    modes = probe.shape[1]
    half = side // 2
    rows, cols = obj_field.shape[2], obj_field.shape[3]
    n_row, n_col = lax.axis_size(ROW), lax.axis_size(COL)
    f32 = jnp.float32
    scan = scan_pos.reshape(2)
    live = live_count.reshape(1)
    swap = [(0, 1), (1, 0)]
    pairs = both_ways([(i, i + 1) for i in range(1, n_row - 1, 2)])
    even_pairs = both_ways([(i, i + 1) for i in range(0, n_col - 1, 2)])
    odd_pairs = both_ways([(i, i + 1) for i in range(1, n_col - 1, 2)])
    strip = 4 * rows

    def shape(*dims):
        return jax.ShapeDtypeStruct(dims, f32)

    edge = shape(2, rows, side)
    large = pl.CostEstimate(flops=4_000_000_000, bytes_accessed=0, transcendentals=0)
    column, column_near = call(
        column_kernel, [shape(136, side), shape(8, side)], 0, 1, cost=large
    )(scan.reshape(1, 2))
    to_even, to_odd = call(edges_kernel, [edge, edge], 0, 1)(obj_field)
    column = lax.ppermute(column, ROW, pairs)
    with_even = lax.ppermute(to_even, COL, even_pairs)
    with_odd = lax.ppermute(to_odd, COL, odd_pairs)
    column_near = lax.ppermute(column_near, "core", swap)
    to_beyond, frame = call(
        beyond_kernel, [shape(strip + 8, side), shape(4, rows, cols + 2 * side)], 0, 4
    )(column, obj_field, with_even, with_odd)
    beyond = lax.ppermute(to_beyond, ROW, pairs)
    to_core = call(core_kernel, shape(strip, side), 0, 2)(column_near, frame)
    other = lax.ppermute(to_core, "core", swap)
    tabs = jnp.asarray(tables(side))
    small = pl.CostEstimate(flops=1000, bytes_accessed=1000, transcendentals=0)
    near = call(near_kernel, shape(strip, side), 1, 4, cost=small)(
        scan, frame, probe, patterns, tabs
    )
    near, other, beyond = lax.optimization_barrier((near, other, beyond))
    tall = pltpu.VMEM((4, 2 * half + rows, side), f32)
    keep, message_core, message_beyond, own_strip = call(
        main_kernel,
        [
            shape(modes * side, side),
            shape(modes * side + strip + 8, side),
            shape(strip + 8, side),
            shape(strip, side),
        ],
        2,
        6,
        [tall, tall],
    )(scan, live, near, other, beyond, probe, patterns, tabs)

    from_core = lax.ppermute(message_core, "core", swap)
    from_beyond = lax.ppermute(message_beyond, ROW, pairs)

    n_yx = lax.axis_size(("x", "y"))
    n_z = lax.axis_size(("zh", "zl"))
    total = modes * side
    chunk = total // n_yx
    summed = call(add_kernel, shape(total, side), 0, 2)(keep, from_core)
    spread = lax.all_to_all(summed.reshape(n_yx, chunk, side), ("x", "y"), 0, 0)

    centre, grad_even, grad_odd = call(
        merge_kernel,
        [shape(2, 2, rows, cols), edge, edge],
        1,
        3,
        [pltpu.VMEM((4, rows, cols + 2 * side), f32)],
    )(scan, own_strip, from_core, from_beyond)
    part = call(sum_kernel, shape(n_z, chunk, side), 0, 1)(spread)
    part = lax.all_to_all(part, ("zh", "zl"), 0, 0)
    part = call(sum_kernel, shape(n_yx, chunk, side), 0, 1)(part)
    got_even = lax.ppermute(grad_even, COL, even_pairs)
    part, got_even, grad_odd = lax.optimization_barrier((part, got_even, grad_odd))
    got_odd = lax.ppermute(grad_odd, COL, odd_pairs)
    whole = lax.all_to_all(part, ("x", "y"), 0, 0)
    whole, got_even, got_odd = lax.optimization_barrier((whole, got_even, got_odd))
    whole = whole.reshape(modes, side, side)
    facing = lax.ppermute(whole, "core", swap)
    obj_grad, probe_grad = call(
        finish_kernel,
        [shape(2, 2, rows, cols), shape(2, modes, side, side)],
        0,
        4,
        [pltpu.VMEM((2, 2, rows, cols), f32), pltpu.SemaphoreType.DMA, pltpu.SemaphoreType.DMA],
        out_far=(0, 1),
    )(centre, got_even, got_odd, whole)
    (probe_grad,) = call(
        other_half_kernel,
        [shape(2, modes, side, side)],
        0,
        1,
        [pltpu.SemaphoreType.DMA],
        n_far=1,
        out_far=(0,),
        aliases={1: 0},
    )(facing, probe_grad)
    return (obj_grad, probe_grad)


def solution(mesh):
    fine = Mesh(
        mesh.devices.reshape(8, 2, 2, 4, 4), ("y", "zh", "core", "x", "zl")
    )
    return jax.shard_map(
        body,
        mesh=fine,
        in_specs=(
            P(None, None, ROW, COL),
            P(),
            P(ROW, COL, None, None),
            P(ROW, COL),
            P(ROW, COL, None, None, None),
        ),
        out_specs=(P(None, None, ROW, COL), P()),
        check_vma=False,
    )
```

```python
import functools
import math

import jax
import jax.numpy as jnp
import ml_dtypes
import numpy as np
from jax import lax
from jax.experimental import pallas as pl
from jax.experimental.pallas import tpu as pltpu
from jax.sharding import Mesh
from jax.sharding import PartitionSpec as P

PHASE_COEF = 20.0
LOSS_WEIGHT = 0.125
ROW = ("y", "zh", "core")
COL = ("x", "zl")
EVERY = ("y", "zh", "core", "x", "zl")
VMEM_LIMIT = 48 * 1024 * 1024
TILE_COLS = 256


def split_bf16(table):
    high = table.astype(np.float32).astype(ml_dtypes.bfloat16)
    low = (table - high.astype(np.float64)).astype(np.float32).astype(ml_dtypes.bfloat16)
    return high, low


def tables(side):
    counter = np.arange(side)
    phase = 2.0 * math.pi / side * (counter[:, None] * counter[None, :] % side)
    fourier = np.exp(-1j * phase) / math.sqrt(side)
    spatial = ((counter + side // 2) % side - side // 2) / side
    factor = np.exp(-1j * PHASE_COEF * spatial * spatial)
    propagate = np.conj(fourier) @ (factor[:, None] * fourier)
    propagate = 0.5 * (propagate + propagate.T)
    parts = []
    for matrix in (propagate, fourier):
        for block in (matrix.real, matrix.imag, -matrix.imag):
            parts += split_bf16(block)
    return np.stack(parts)


def on_sides(tabs, which):
    def block(n, part):
        return tabs[6 * which + 2 * n + part]

    def square(a, b, c, d, part):
        return jnp.concatenate(
            [
                jnp.concatenate([block(a, part), block(b, part)], axis=1),
                jnp.concatenate([block(c, part), block(d, part)], axis=1),
            ],
            axis=0,
        )

    right = tuple(square(0, 1, 2, 0, part) for part in range(2))
    left = tuple(square(0, 2, 1, 0, part) for part in range(2))
    return right, left


def split(value):
    high = value.astype(jnp.bfloat16)
    low = (value - high.astype(jnp.float32)).astype(jnp.bfloat16)
    return high, low


def product(left, right):
    (left_high, left_low), (right_high, right_low) = left, right
    dot = functools.partial(jnp.dot, preferred_element_type=jnp.float32)
    return dot(left_high, right_high) + (dot(left_low, right_high) + dot(left_high, right_low))


def two_sided(real, imaginary, right, left, group=2):
    side = real[0].shape[0]
    middles = []
    for n in range(0, len(real), group):
        pairs = zip(real[n : n + group], imaginary[n : n + group])
        stacked = jnp.concatenate([jnp.concatenate(pair, axis=1) for pair in pairs], axis=0)
        middles.append(product(split(stacked), right))
    out_real, out_imaginary = [], []
    for middle in middles:
        blocks = [middle[m * side : (m + 1) * side] for m in range(group)]
        spread = jnp.concatenate(
            [
                jnp.concatenate([block[:, :side] for block in blocks], axis=1),
                jnp.concatenate([block[:, side:] for block in blocks], axis=1),
            ],
            axis=0,
        )
        out = product(left, split(spread))
        out_real += [out[:side, m * side : (m + 1) * side] for m in range(group)]
        out_imaginary += [out[side:, m * side : (m + 1) * side] for m in range(group)]
    return out_real, out_imaginary


def times(ar, ai, br, bi):
    return ar * br - ai * bi, ar * bi + ai * br


def times_conj(ar, ai, br, bi):
    return ar * br + ai * bi, ar * bi - ai * br


def model(window, probe, pattern, weight, tabs):
    (o0r, o1r), (o0i, o1i) = window
    qr, qi = probe
    modes = len(qr)
    prop_right, prop_left = on_sides(tabs, 0)
    four_right, four_left = on_sides(tabs, 1)
    e0 = [times(qr[m], qi[m], o0r, o0i) for m in range(modes)]
    a1r, a1i = two_sided([e[0] for e in e0], [e[1] for e in e0], prop_right, prop_left)
    e1 = [times(a1r[m], a1i[m], o1r, o1i) for m in range(modes)]
    gr, gi = two_sided([e[0] for e in e1], [e[1] for e in e1], four_right, four_left)
    intensity = gr[0] * gr[0] + gi[0] * gi[0]
    for m in range(1, modes):
        intensity = intensity + (gr[m] * gr[m] + gi[m] * gi[m])
    residue = (intensity - pattern) * (4.0 * LOSS_WEIGHT * weight)
    br, bi = two_sided(
        [residue * g for g in gr], [residue * g for g in gi], four_left, four_right
    )
    grad1 = [times_conj(a1r[m], a1i[m], br[m], bi[m]) for m in range(modes)]
    back = [times_conj(o1r, o1i, br[m], bi[m]) for m in range(modes)]
    cr, ci = two_sided([b[0] for b in back], [b[1] for b in back], prop_left, prop_right)
    grad0 = [times_conj(qr[m], qi[m], cr[m], ci[m]) for m in range(modes)]
    probe_grad = [times_conj(o0r, o0i, cr[m], ci[m]) for m in range(modes)]

    def over_modes(terms, part):
        return functools.reduce(lambda a, b: a + b, [t[part] for t in terms])

    window_grad = [
        [over_modes(grad0, 0), over_modes(grad1, 0)],
        [over_modes(grad0, 1), over_modes(grad1, 1)],
    ]
    return window_grad, probe_grad


def place_of(scan, rows, cols, half):
    row = scan[0] - (lax.axis_index(ROW) * rows - half)
    col = scan[1] - (lax.axis_index(COL) * cols - half)
    return row, col


def strips_at(half):
    core = lax.axis_index("core")
    return pl.multiple_of((1 - core) * 2 * half, 8), pl.multiple_of(core * 2 * half, 8)


def even_col():
    return lax.rem(lax.axis_index(COL), 2) == 0


def fill(frame, own, with_even, with_odd, part, layer):
    side = with_even.shape[2]
    half = side // 2
    cols = own.shape[3]
    plane = 2 * part + layer
    left = jnp.where(even_col(), with_odd[layer], with_even[layer])
    right = jnp.where(even_col(), with_even[layer], with_odd[layer])
    if part:
        left, right = pltpu.roll(left, half, 1), pltpu.roll(right, half, 1)
    frame[plane, :, 0:side] = left
    frame[plane, :, side : side + cols] = own[part, layer]
    frame[plane, :, side + cols :] = right


def cut(frame, plane, at, side):
    step = lax.rem(at, side)
    wide = frame[plane, :, pl.ds(pl.multiple_of(at - step, side), 2 * side)]
    return pltpu.roll(wide, lax.rem(2 * side - step, 2 * side), 1)[:, :side]


def column_kernel(scan, column, column_near):
    half = column.shape[1] // 2
    col = (scan[:, 1:2] - (lax.axis_index(COL) * TILE_COLS - half)).astype(jnp.float32)
    column[...] = jnp.broadcast_to(col, column.shape)
    column_near[...] = jnp.broadcast_to(col, column_near.shape)


def edges_kernel(own, with_even, with_odd):
    rows, cols = own.shape[2], own.shape[3]
    side = with_even.shape[2]
    half = side // 2
    inner = lax.broadcasted_iota(jnp.int32, (rows, side), 1) < half
    for layer in range(2):
        real, imaginary = own[0, layer], own[1, layer]
        left = jnp.where(inner, real[:, :side], pltpu.roll(imaginary[:, :side], half, 1))
        right = jnp.where(inner, pltpu.roll(imaginary[:, cols - side :], half, 1), real[:, cols - side :])
        with_even[layer] = jnp.where(even_col(), right, left)
        with_odd[layer] = jnp.where(even_col(), left, right)


def partner_column(column, cols):
    return jnp.clip(jnp.max(column[0:8, :]).astype(jnp.int32), 0, cols - 1)


def beyond_kernel(column, own, with_even, with_odd, to_beyond, frame):
    rows, cols = own.shape[2], own.shape[3]
    side = to_beyond.shape[1]
    col = partner_column(column, cols)
    for layer in range(2):
        for part in range(2):
            plane = 2 * part + layer
            fill(frame, own, with_even, with_odd, part, layer)
            to_beyond[pl.ds(plane * rows, rows), :] = cut(frame, plane, col + side // 2, side)
    to_beyond[pl.ds(4 * rows, 8), :] = jnp.zeros((8, side), jnp.float32)


def core_kernel(column, frame, to_core):
    side = to_core.shape[1]
    rows, cols = frame.shape[1], frame.shape[2] - 2 * side
    col = partner_column(column, cols)
    for plane in range(4):
        to_core[pl.ds(plane * rows, rows), :] = cut(frame, plane, col + side // 2, side)


def near_kernel(scan, frame, probe, pattern, tabs, near):
    rows, cols = frame.shape[1], frame.shape[2] - 2 * near.shape[1]
    side = near.shape[1]
    half = side // 2
    unused, col = place_of(scan, rows, cols, half)
    for plane in range(4):
        near[pl.ds(plane * rows, rows), :] = cut(frame, plane, col + half, side)


def main_kernel(
    scan, live, near, other, beyond, probe, pattern, tabs,
    keep, message_core, message_beyond, own_strip, column, shifted,
):
    side = probe.shape[-1]
    half = side // 2
    rows = own_strip.shape[0] // 4
    cols = TILE_COLS
    modes = probe.shape[1]
    row, col = place_of(scan, rows, cols, half)
    other_at, beyond_at = strips_at(half)
    for plane in range(4):
        at = pl.ds(plane * rows, rows)
        column[plane, half : half + rows, :] = near[at, :]
        column[plane, pl.ds(other_at, rows), :] = other[at, :]
        column[plane, pl.ds(beyond_at, rows), :] = beyond[at, :]
    tall = side + 8
    step = lax.rem(row, 8)
    base_row = pl.multiple_of(row - step, 8)

    def window_of(plane):
        high = column[plane, pl.ds(base_row, tall), :]
        return pltpu.roll(high, lax.rem(tall - step, tall), 0)[:side]

    window = [[window_of(2 * part + layer) for layer in range(2)] for part in range(2)]
    fields = [[probe[part, m] for m in range(modes)] for part in range(2)]
    weight = (live[0] > 0).astype(jnp.float32)
    window_grad, probe_grad = model(window, fields, pattern[0, 0, 0], weight, tabs)
    first = lax.axis_index("core") == 0
    for m in range(modes):
        at = pl.ds(m * side, side)
        real, imaginary = probe_grad[m]
        keep[at, :] = jnp.where(first, real, imaginary)
        message_core[at, :] = jnp.where(first, imaginary, real)
    base = modes * side
    shifted[...] = jnp.zeros_like(shifted)
    for part in range(2):
        for layer in range(2):
            plane = 2 * part + layer
            padded = jnp.concatenate(
                [window_grad[part][layer], jnp.zeros((8, side), jnp.float32)], axis=0
            )
            shifted[plane, pl.ds(base_row, tall), :] = pltpu.roll(padded, step, 0)
            at = pl.ds(plane * rows, rows)
            message_core[pl.ds(base + plane * rows, rows), :] = shifted[plane, pl.ds(other_at, rows), :]
            message_beyond[at, :] = shifted[plane, pl.ds(beyond_at, rows), :]
            own_strip[at, :] = shifted[plane, half : half + rows, :]
    offset = jnp.full((8, side), col.astype(jnp.float32))
    message_core[pl.ds(base + 4 * rows, 8), :] = offset
    message_beyond[pl.ds(4 * rows, 8), :] = offset


def merge_kernel(scan, own_strip, from_core, from_beyond, centre, with_even, with_odd, frame):
    side = own_strip.shape[1]
    half = side // 2
    rows = centre.shape[2]
    cols = centre.shape[3]
    base = from_core.shape[0] - from_beyond.shape[0]
    core_col = jnp.max(from_core[pl.ds(base + 4 * rows, 8), :]).astype(jnp.int32)
    beyond_col = jnp.max(from_beyond[pl.ds(4 * rows, 8), :]).astype(jnp.int32)
    unused, own_col = place_of(scan, rows, cols, half)
    lane = lax.broadcasted_iota(jnp.int32, (rows, side), 1)
    zero = jnp.zeros((rows, side), jnp.float32)
    frame[...] = jnp.zeros_like(frame)
    for source, first, col in (
        (own_strip, 0, own_col),
        (from_core, base, jnp.clip(core_col, 0, cols - 1)),
        (from_beyond, 0, jnp.clip(beyond_col, 0, cols - 1)),
    ):
        at = col + half
        step = lax.rem(at, side)
        near = pl.multiple_of(at - step, side)
        here, there = pl.ds(near, side), pl.ds(pl.multiple_of(near + side, side), side)
        for plane in range(4):
            strip = pltpu.roll(source[pl.ds(first + plane * rows, rows), :], step, 1)
            frame[plane, :, here] += jnp.where(lane >= step, strip, zero)
            frame[plane, :, there] += jnp.where(lane < step, strip, zero)
    inner = lane < half
    for layer in range(2):
        real, imaginary = layer, 2 + layer
        left = jnp.where(inner, pltpu.roll(frame[imaginary, :, 0:side], half, 1), frame[real, :, 0:side])
        right = jnp.where(inner, frame[real, :, side + cols :], pltpu.roll(frame[imaginary, :, side + cols :], half, 1))
        with_even[layer] = jnp.where(even_col(), right, left)
        with_odd[layer] = jnp.where(even_col(), left, right)
        centre[0, layer] = frame[real, :, side : side + cols]
        centre[1, layer] = frame[imaginary, :, side : side + cols]


def add_kernel(keep, message, out):
    out[...] = keep[...] + message[0 : keep.shape[0], :]


def sum_kernel(parts, copies):
    total = parts[0]
    for n in range(1, parts.shape[0]):
        total = total + parts[n]
    for n in range(copies.shape[0]):
        copies[n] = total


def finish_kernel(centre, with_even, with_odd, whole, out, probe_grad, total, sem, out_sem):
    copy = pltpu.make_async_copy(whole, probe_grad.at[lax.axis_index("core")], sem)
    copy.start()
    rows, cols = centre.shape[2], centre.shape[3]
    side = with_even.shape[2]
    half = side // 2
    inner = lax.broadcasted_iota(jnp.int32, (rows, side), 1) < half
    zero = jnp.zeros((rows, side), jnp.float32)
    for layer in range(2):
        left = jnp.where(even_col(), with_odd[layer], with_even[layer])
        right = jnp.where(even_col(), with_even[layer], with_odd[layer])
        for part in range(2):
            if part:
                left, right = pltpu.roll(left, half, 1), pltpu.roll(right, half, 1)
            value = centre[part, layer]
            total[part, layer, :, 0:side] = value[:, :side] + jnp.where(inner, left, zero)
            total[part, layer, :, cols - side :] = value[:, cols - side :] + jnp.where(inner, zero, right)
    out_copy = pltpu.make_async_copy(total, out, out_sem)
    out_copy.start()
    copy.wait()
    out_copy.wait()


def other_half_kernel(facing, half_done, probe_grad, sem):
    copy = pltpu.make_async_copy(facing, probe_grad.at[1 - lax.axis_index("core")], sem)
    copy.start()
    copy.wait()


def call(kernel, out_shape, n_scalars, n_in, scratch=(), cost=None, n_far=0, out_far=(), aliases=None):
    many = isinstance(out_shape, (list, tuple))
    vmem = pl.BlockSpec(memory_space=pltpu.VMEM)
    far = pl.BlockSpec(memory_space=pltpu.HBM)
    return pl.pallas_call(
        kernel,
        out_shape=out_shape,
        in_specs=[pl.BlockSpec(memory_space=pltpu.SMEM)] * n_scalars + [vmem] * n_in + [far] * n_far,
        out_specs=[far if n in out_far else vmem for n in range(len(out_shape))] if many else vmem,
        input_output_aliases=aliases or {},
        scratch_shapes=list(scratch),
        compiler_params=pltpu.CompilerParams(vmem_limit_bytes=VMEM_LIMIT),
        cost_estimate=cost,
    )


def both_ways(pairs):
    return pairs + [(j, i) for i, j in pairs]


def peer_groups():
    sizes = {axis: lax.axis_size(axis) for axis in EVERY}
    n_x, n_y, n_z = sizes["x"], sizes["y"], sizes["zh"] * sizes["zl"]

    def index(x, y, z, core):
        at = {"x": x, "y": y, "zh": z // sizes["zl"], "zl": z % sizes["zl"], "core": core}
        flat = 0
        for axis in EVERY:
            flat = flat * sizes[axis] + at[axis]
        return flat

    planes = [[index(x, y, z, 0) for x in range(n_x) for y in range(n_y)] for z in range(n_z)]
    planes += [[index(x, y, z, 1) for x in range(n_x) for z in range(n_z)] for y in range(n_y)]
    lines = [[index(x, y, z, 0) for z in range(n_z)] for x in range(n_x) for y in range(n_y)]
    lines += [[index(x, y, z, 1) for y in range(n_y)] for x in range(n_x) for z in range(n_z)]
    return planes, lines


def body(obj_field, probe, scan_pos, live_count, patterns):
    side = probe.shape[2]
    modes = probe.shape[1]
    half = side // 2
    rows, cols = obj_field.shape[2], obj_field.shape[3]
    n_row, n_col = lax.axis_size(ROW), lax.axis_size(COL)
    f32 = jnp.float32
    scan = scan_pos.reshape(2)
    live = live_count.reshape(1)
    swap = [(0, 1), (1, 0)]
    pairs = both_ways([(i, i + 1) for i in range(1, n_row - 1, 2)])
    even_pairs = both_ways([(i, i + 1) for i in range(0, n_col - 1, 2)])
    odd_pairs = both_ways([(i, i + 1) for i in range(1, n_col - 1, 2)])
    strip = 4 * rows

    def shape(*dims):
        return jax.ShapeDtypeStruct(dims, f32)

    edge = shape(2, rows, side)
    large = pl.CostEstimate(flops=4_000_000_000, bytes_accessed=0, transcendentals=0)
    column, column_near = call(
        column_kernel, [shape(136, side), shape(8, side)], 0, 1, cost=large
    )(scan.reshape(1, 2))
    to_even, to_odd = call(edges_kernel, [edge, edge], 0, 1)(obj_field)
    column = lax.ppermute(column, ROW, pairs)
    with_even = lax.ppermute(to_even, COL, even_pairs)
    with_odd = lax.ppermute(to_odd, COL, odd_pairs)
    column_near = lax.ppermute(column_near, "core", swap)
    to_beyond, frame = call(
        beyond_kernel, [shape(strip + 8, side), shape(4, rows, cols + 2 * side)], 0, 4
    )(column, obj_field, with_even, with_odd)
    beyond = lax.ppermute(to_beyond, ROW, pairs)
    to_core = call(core_kernel, shape(strip, side), 0, 2)(column_near, frame)
    other = lax.ppermute(to_core, "core", swap)
    tabs = jnp.asarray(tables(side))
    small = pl.CostEstimate(flops=1000, bytes_accessed=1000, transcendentals=0)
    near = call(near_kernel, shape(strip, side), 1, 4, cost=small)(
        scan, frame, probe, patterns, tabs
    )
    near, other, beyond = lax.optimization_barrier((near, other, beyond))
    tall = pltpu.VMEM((4, 2 * half + rows, side), f32)
    keep, message_core, message_beyond, own_strip = call(
        main_kernel,
        [
            shape(modes * side, side),
            shape(modes * side + strip + 8, side),
            shape(strip + 8, side),
            shape(strip, side),
        ],
        2,
        6,
        [tall, tall],
    )(scan, live, near, other, beyond, probe, patterns, tabs)

    from_core = lax.ppermute(message_core, "core", swap)
    from_beyond = lax.ppermute(message_beyond, ROW, pairs)

    n_yx = lax.axis_size(("x", "y"))
    n_z = lax.axis_size(("zh", "zl"))
    total = modes * side
    chunk = total // n_yx
    summed = call(add_kernel, shape(total, side), 0, 2)(keep, from_core)
    planes, lines = peer_groups()
    spread = lax.all_to_all(
        summed.reshape(n_yx, chunk, side), EVERY, 0, 0, axis_index_groups=planes
    )

    centre, grad_even, grad_odd = call(
        merge_kernel,
        [shape(2, 2, rows, cols), edge, edge],
        1,
        3,
        [pltpu.VMEM((4, rows, cols + 2 * side), f32)],
    )(scan, own_strip, from_core, from_beyond)
    part = call(sum_kernel, shape(n_z, chunk, side), 0, 1)(spread)
    part = lax.all_to_all(part, EVERY, 0, 0, axis_index_groups=lines)
    part = call(sum_kernel, shape(n_yx, chunk, side), 0, 1)(part)
    got_even = lax.ppermute(grad_even, COL, even_pairs)
    part, got_even, grad_odd = lax.optimization_barrier((part, got_even, grad_odd))
    got_odd = lax.ppermute(grad_odd, COL, odd_pairs)
    whole = lax.all_to_all(part, EVERY, 0, 0, axis_index_groups=planes)
    whole, got_even, got_odd = lax.optimization_barrier((whole, got_even, got_odd))
    whole = whole.reshape(modes, side, side)
    facing = lax.ppermute(whole, "core", swap)
    obj_grad, probe_grad = call(
        finish_kernel,
        [shape(2, 2, rows, cols), shape(2, modes, side, side)],
        0,
        4,
        [pltpu.VMEM((2, 2, rows, cols), f32), pltpu.SemaphoreType.DMA, pltpu.SemaphoreType.DMA],
        out_far=(0, 1),
    )(centre, got_even, got_odd, whole)
    (probe_grad,) = call(
        other_half_kernel,
        [shape(2, modes, side, side)],
        0,
        1,
        [pltpu.SemaphoreType.DMA],
        n_far=1,
        out_far=(0,),
        aliases={1: 0},
    )(facing, probe_grad)
    return (obj_grad, probe_grad)


def solution(mesh):
    fine = Mesh(
        mesh.devices.reshape(8, 2, 2, 4, 4), ("y", "zh", "core", "x", "zl")
    )
    return jax.shard_map(
        body,
        mesh=fine,
        in_specs=(
            P(None, None, ROW, COL),
            P(),
            P(ROW, COL, None, None),
            P(ROW, COL),
            P(ROW, COL, None, None, None),
        ),
        out_specs=(P(None, None, ROW, COL), P()),
        check_vma=False,
    )
```

```python
import functools
import math

import jax
import jax.numpy as jnp
import ml_dtypes
import numpy as np
from jax import lax
from jax.experimental import pallas as pl
from jax.experimental.pallas import tpu as pltpu
from jax.sharding import Mesh
from jax.sharding import PartitionSpec as P

PHASE_COEF = 20.0
LOSS_WEIGHT = 0.125
ROW = ("y", "zh", "core")
COL = ("x", "zl")
EVERY = ("y", "zh", "core", "x", "zl")
VMEM_LIMIT = 48 * 1024 * 1024
TILE_COLS = 256


def split_bf16(table):
    high = table.astype(np.float32).astype(ml_dtypes.bfloat16)
    low = (table - high.astype(np.float64)).astype(np.float32).astype(ml_dtypes.bfloat16)
    return high, low


def tables(side):
    counter = np.arange(side)
    phase = 2.0 * math.pi / side * (counter[:, None] * counter[None, :] % side)
    fourier = np.exp(-1j * phase) / math.sqrt(side)
    spatial = ((counter + side // 2) % side - side // 2) / side
    factor = np.exp(-1j * PHASE_COEF * spatial * spatial)
    propagate = np.conj(fourier) @ (factor[:, None] * fourier)
    propagate = 0.5 * (propagate + propagate.T)
    parts = []
    for matrix in (propagate, fourier):
        for block in (matrix.real, matrix.imag, -matrix.imag):
            parts += split_bf16(block)
    return np.stack(parts)


def on_sides(tabs, which):
    def block(n, part):
        return tabs[6 * which + 2 * n + part]

    def square(a, b, c, d, part):
        return jnp.concatenate(
            [
                jnp.concatenate([block(a, part), block(b, part)], axis=1),
                jnp.concatenate([block(c, part), block(d, part)], axis=1),
            ],
            axis=0,
        )

    right = tuple(square(0, 1, 2, 0, part) for part in range(2))
    left = tuple(square(0, 2, 1, 0, part) for part in range(2))
    return right, left


def split(value):
    high = value.astype(jnp.bfloat16)
    low = (value - high.astype(jnp.float32)).astype(jnp.bfloat16)
    return high, low


def product(left, right):
    (left_high, left_low), (right_high, right_low) = left, right
    dot = functools.partial(jnp.dot, preferred_element_type=jnp.float32)
    return dot(left_high, right_high) + (dot(left_low, right_high) + dot(left_high, right_low))


def two_sided(real, imaginary, right, left, group=2):
    side = real[0].shape[0]
    middles = []
    for n in range(0, len(real), group):
        pairs = zip(real[n : n + group], imaginary[n : n + group])
        stacked = jnp.concatenate([jnp.concatenate(pair, axis=1) for pair in pairs], axis=0)
        middles.append(product(split(stacked), right))
    out_real, out_imaginary = [], []
    for middle in middles:
        blocks = [middle[m * side : (m + 1) * side] for m in range(group)]
        spread = jnp.concatenate(
            [
                jnp.concatenate([block[:, :side] for block in blocks], axis=1),
                jnp.concatenate([block[:, side:] for block in blocks], axis=1),
            ],
            axis=0,
        )
        out = product(left, split(spread))
        out_real += [out[:side, m * side : (m + 1) * side] for m in range(group)]
        out_imaginary += [out[side:, m * side : (m + 1) * side] for m in range(group)]
    return out_real, out_imaginary


def times(ar, ai, br, bi):
    return ar * br - ai * bi, ar * bi + ai * br


def times_conj(ar, ai, br, bi):
    return ar * br + ai * bi, ar * bi - ai * br


def model(window, probe, pattern, weight, tabs):
    (o0r, o1r), (o0i, o1i) = window
    qr, qi = probe
    modes = len(qr)
    prop_right, prop_left = on_sides(tabs, 0)
    four_right, four_left = on_sides(tabs, 1)
    e0 = [times(qr[m], qi[m], o0r, o0i) for m in range(modes)]
    a1r, a1i = two_sided([e[0] for e in e0], [e[1] for e in e0], prop_right, prop_left)
    e1 = [times(a1r[m], a1i[m], o1r, o1i) for m in range(modes)]
    gr, gi = two_sided([e[0] for e in e1], [e[1] for e in e1], four_right, four_left)
    intensity = gr[0] * gr[0] + gi[0] * gi[0]
    for m in range(1, modes):
        intensity = intensity + (gr[m] * gr[m] + gi[m] * gi[m])
    residue = (intensity - pattern) * (4.0 * LOSS_WEIGHT * weight)
    br, bi = two_sided(
        [residue * g for g in gr], [residue * g for g in gi], four_left, four_right
    )
    grad1 = [times_conj(a1r[m], a1i[m], br[m], bi[m]) for m in range(modes)]
    back = [times_conj(o1r, o1i, br[m], bi[m]) for m in range(modes)]
    cr, ci = two_sided([b[0] for b in back], [b[1] for b in back], prop_left, prop_right)
    grad0 = [times_conj(qr[m], qi[m], cr[m], ci[m]) for m in range(modes)]
    probe_grad = [times_conj(o0r, o0i, cr[m], ci[m]) for m in range(modes)]

    def over_modes(terms, part):
        return functools.reduce(lambda a, b: a + b, [t[part] for t in terms])

    window_grad = [
        [over_modes(grad0, 0), over_modes(grad1, 0)],
        [over_modes(grad0, 1), over_modes(grad1, 1)],
    ]
    return window_grad, probe_grad


def place_of(scan, rows, cols, half):
    row = scan[0] - (lax.axis_index(ROW) * rows - half)
    col = scan[1] - (lax.axis_index(COL) * cols - half)
    return row, col


def strips_at(half):
    core = lax.axis_index("core")
    return pl.multiple_of((1 - core) * 2 * half, 8), pl.multiple_of(core * 2 * half, 8)


def even_col():
    return lax.rem(lax.axis_index(COL), 2) == 0


def fill(frame, own, with_even, with_odd, part, layer):
    side = with_even.shape[2]
    half = side // 2
    cols = own.shape[3]
    plane = 2 * part + layer
    left = jnp.where(even_col(), with_odd[layer], with_even[layer])
    right = jnp.where(even_col(), with_even[layer], with_odd[layer])
    if part:
        left, right = pltpu.roll(left, half, 1), pltpu.roll(right, half, 1)
    frame[plane, :, 0:side] = left
    frame[plane, :, side : side + cols] = own[part, layer]
    frame[plane, :, side + cols :] = right


def cut(frame, plane, at, side):
    step = lax.rem(at, side)
    wide = frame[plane, :, pl.ds(pl.multiple_of(at - step, side), 2 * side)]
    return pltpu.roll(wide, lax.rem(2 * side - step, 2 * side), 1)[:, :side]


def column_kernel(scan, column, column_near):
    half = column.shape[1] // 2
    col = (scan[:, 1:2] - (lax.axis_index(COL) * TILE_COLS - half)).astype(jnp.float32)
    column[...] = jnp.broadcast_to(col, column.shape)
    column_near[...] = jnp.broadcast_to(col, column_near.shape)


def edges_kernel(own, with_even, with_odd):
    rows, cols = own.shape[2], own.shape[3]
    side = with_even.shape[2]
    half = side // 2
    inner = lax.broadcasted_iota(jnp.int32, (rows, side), 1) < half
    for layer in range(2):
        real, imaginary = own[0, layer], own[1, layer]
        left = jnp.where(inner, real[:, :side], pltpu.roll(imaginary[:, :side], half, 1))
        right = jnp.where(inner, pltpu.roll(imaginary[:, cols - side :], half, 1), real[:, cols - side :])
        with_even[layer] = jnp.where(even_col(), right, left)
        with_odd[layer] = jnp.where(even_col(), left, right)


def partner_column(column, cols):
    return jnp.clip(jnp.max(column[0:8, :]).astype(jnp.int32), 0, cols - 1)


def beyond_kernel(column, own, with_even, with_odd, to_beyond, frame):
    rows, cols = own.shape[2], own.shape[3]
    side = to_beyond.shape[1]
    col = partner_column(column, cols)
    for layer in range(2):
        for part in range(2):
            plane = 2 * part + layer
            fill(frame, own, with_even, with_odd, part, layer)
            to_beyond[pl.ds(plane * rows, rows), :] = cut(frame, plane, col + side // 2, side)
    to_beyond[pl.ds(4 * rows, 8), :] = jnp.zeros((8, side), jnp.float32)


def core_kernel(column, frame, to_core):
    side = to_core.shape[1]
    rows, cols = frame.shape[1], frame.shape[2] - 2 * side
    col = partner_column(column, cols)
    for plane in range(4):
        to_core[pl.ds(plane * rows, rows), :] = cut(frame, plane, col + side // 2, side)


def near_kernel(scan, frame, probe, pattern, tabs, near):
    rows, cols = frame.shape[1], frame.shape[2] - 2 * near.shape[1]
    side = near.shape[1]
    half = side // 2
    unused, col = place_of(scan, rows, cols, half)
    for plane in range(4):
        near[pl.ds(plane * rows, rows), :] = cut(frame, plane, col + half, side)


def main_kernel(
    scan, live, near, other, beyond, probe, pattern, tabs,
    keep, message_core, message_beyond, own_strip, column, shifted,
):
    side = probe.shape[-1]
    half = side // 2
    rows = own_strip.shape[0] // 4
    cols = TILE_COLS
    modes = probe.shape[1]
    row, col = place_of(scan, rows, cols, half)
    other_at, beyond_at = strips_at(half)
    for plane in range(4):
        at = pl.ds(plane * rows, rows)
        column[plane, half : half + rows, :] = near[at, :]
        column[plane, pl.ds(other_at, rows), :] = other[at, :]
        column[plane, pl.ds(beyond_at, rows), :] = beyond[at, :]
    tall = side + 8
    step = lax.rem(row, 8)
    base_row = pl.multiple_of(row - step, 8)

    def window_of(plane):
        high = column[plane, pl.ds(base_row, tall), :]
        return pltpu.roll(high, lax.rem(tall - step, tall), 0)[:side]

    window = [[window_of(2 * part + layer) for layer in range(2)] for part in range(2)]
    fields = [[probe[part, m] for m in range(modes)] for part in range(2)]
    weight = (live[0] > 0).astype(jnp.float32)
    window_grad, probe_grad = model(window, fields, pattern[0, 0, 0], weight, tabs)
    first = lax.axis_index("core") == 0
    for m in range(modes):
        at = pl.ds(m * side, side)
        real, imaginary = probe_grad[m]
        keep[at, :] = jnp.where(first, real, imaginary)
        message_core[at, :] = jnp.where(first, imaginary, real)
    base = modes * side
    shifted[...] = jnp.zeros_like(shifted)
    for part in range(2):
        for layer in range(2):
            plane = 2 * part + layer
            padded = jnp.concatenate(
                [window_grad[part][layer], jnp.zeros((8, side), jnp.float32)], axis=0
            )
            shifted[plane, pl.ds(base_row, tall), :] = pltpu.roll(padded, step, 0)
            at = pl.ds(plane * rows, rows)
            message_core[pl.ds(base + plane * rows, rows), :] = shifted[plane, pl.ds(other_at, rows), :]
            message_beyond[at, :] = shifted[plane, pl.ds(beyond_at, rows), :]
            own_strip[at, :] = shifted[plane, half : half + rows, :]
    offset = jnp.full((8, side), col.astype(jnp.float32))
    message_core[pl.ds(base + 4 * rows, 8), :] = offset
    message_beyond[pl.ds(4 * rows, 8), :] = offset


def merge_kernel(scan, own_strip, from_core, from_beyond, centre, with_even, with_odd, frame):
    side = own_strip.shape[1]
    half = side // 2
    rows = centre.shape[2]
    cols = centre.shape[3]
    base = from_core.shape[0] - from_beyond.shape[0]
    core_col = jnp.max(from_core[pl.ds(base + 4 * rows, 8), :]).astype(jnp.int32)
    beyond_col = jnp.max(from_beyond[pl.ds(4 * rows, 8), :]).astype(jnp.int32)
    unused, own_col = place_of(scan, rows, cols, half)
    lane = lax.broadcasted_iota(jnp.int32, (rows, side), 1)
    zero = jnp.zeros((rows, side), jnp.float32)
    frame[...] = jnp.zeros_like(frame)
    for source, first, col in (
        (own_strip, 0, own_col),
        (from_core, base, jnp.clip(core_col, 0, cols - 1)),
        (from_beyond, 0, jnp.clip(beyond_col, 0, cols - 1)),
    ):
        at = col + half
        step = lax.rem(at, side)
        near = pl.multiple_of(at - step, side)
        here, there = pl.ds(near, side), pl.ds(pl.multiple_of(near + side, side), side)
        for plane in range(4):
            strip = pltpu.roll(source[pl.ds(first + plane * rows, rows), :], step, 1)
            frame[plane, :, here] += jnp.where(lane >= step, strip, zero)
            frame[plane, :, there] += jnp.where(lane < step, strip, zero)
    inner = lane < half
    for layer in range(2):
        real, imaginary = layer, 2 + layer
        left = jnp.where(inner, pltpu.roll(frame[imaginary, :, 0:side], half, 1), frame[real, :, 0:side])
        right = jnp.where(inner, frame[real, :, side + cols :], pltpu.roll(frame[imaginary, :, side + cols :], half, 1))
        with_even[layer] = jnp.where(even_col(), right, left)
        with_odd[layer] = jnp.where(even_col(), left, right)
        centre[0, layer] = frame[real, :, side : side + cols]
        centre[1, layer] = frame[imaginary, :, side : side + cols]


def add_kernel(keep, message, out):
    out[...] = keep[...] + message[0 : keep.shape[0], :]


def sum_kernel(parts, copies):
    total = parts[0]
    for n in range(1, parts.shape[0]):
        total = total + parts[n]
    for n in range(copies.shape[0]):
        copies[n] = total


def finish_kernel(centre, with_even, with_odd, whole, out, probe_grad, total, sem, out_sem):
    copy = pltpu.make_async_copy(whole, probe_grad.at[lax.axis_index("core")], sem)
    copy.start()
    rows, cols = centre.shape[2], centre.shape[3]
    side = with_even.shape[2]
    half = side // 2
    inner = lax.broadcasted_iota(jnp.int32, (rows, side), 1) < half
    zero = jnp.zeros((rows, side), jnp.float32)
    for layer in range(2):
        left = jnp.where(even_col(), with_odd[layer], with_even[layer])
        right = jnp.where(even_col(), with_even[layer], with_odd[layer])
        for part in range(2):
            if part:
                left, right = pltpu.roll(left, half, 1), pltpu.roll(right, half, 1)
            value = centre[part, layer]
            total[part, layer, :, 0:side] = value[:, :side] + jnp.where(inner, left, zero)
            total[part, layer, :, cols - side :] = value[:, cols - side :] + jnp.where(inner, zero, right)
    out_copy = pltpu.make_async_copy(total, out, out_sem)
    out_copy.start()
    copy.wait()
    out_copy.wait()


def other_half_kernel(facing, half_done, probe_grad, sem):
    copy = pltpu.make_async_copy(facing, probe_grad.at[1 - lax.axis_index("core")], sem)
    copy.start()
    copy.wait()


def call(kernel, out_shape, n_scalars, n_in, scratch=(), cost=None, n_far=0, out_far=(), aliases=None):
    many = isinstance(out_shape, (list, tuple))
    vmem = pl.BlockSpec(memory_space=pltpu.VMEM)
    far = pl.BlockSpec(memory_space=pltpu.HBM)
    return pl.pallas_call(
        kernel,
        out_shape=out_shape,
        in_specs=[pl.BlockSpec(memory_space=pltpu.SMEM)] * n_scalars + [vmem] * n_in + [far] * n_far,
        out_specs=[far if n in out_far else vmem for n in range(len(out_shape))] if many else vmem,
        input_output_aliases=aliases or {},
        scratch_shapes=list(scratch),
        compiler_params=pltpu.CompilerParams(vmem_limit_bytes=VMEM_LIMIT),
        cost_estimate=cost,
    )


def both_ways(pairs):
    return pairs + [(j, i) for i, j in pairs]


def peer_groups():
    sizes = {axis: lax.axis_size(axis) for axis in EVERY}
    n_x, n_y, n_z = sizes["x"], sizes["y"], sizes["zh"] * sizes["zl"]

    def index(x, y, z, core):
        at = {"x": x, "y": y, "zh": z // sizes["zl"], "zl": z % sizes["zl"], "core": core}
        flat = 0
        for axis in EVERY:
            flat = flat * sizes[axis] + at[axis]
        return flat

    planes = [[index(x, y, z, 0) for x in range(n_x) for y in range(n_y)] for z in range(n_z)]
    planes += [[index(x, y, z, 1) for x in range(n_x) for z in range(n_z)] for y in range(n_y)]
    lines = [[index(x, y, z, 0) for z in range(n_z)] for x in range(n_x) for y in range(n_y)]
    lines += [[index(x, y, z, 1) for y in range(n_y)] for x in range(n_x) for z in range(n_z)]
    return planes, lines


def body(obj_field, probe, scan_pos, live_count, patterns):
    side = probe.shape[2]
    modes = probe.shape[1]
    half = side // 2
    rows, cols = obj_field.shape[2], obj_field.shape[3]
    n_row, n_col = lax.axis_size(ROW), lax.axis_size(COL)
    f32 = jnp.float32
    scan = scan_pos.reshape(2)
    live = live_count.reshape(1)
    swap = [(0, 1), (1, 0)]
    pairs = both_ways([(i, i + 1) for i in range(1, n_row - 1, 2)])
    even_pairs = both_ways([(i, i + 1) for i in range(0, n_col - 1, 2)])
    odd_pairs = both_ways([(i, i + 1) for i in range(1, n_col - 1, 2)])
    strip = 4 * rows

    def shape(*dims):
        return jax.ShapeDtypeStruct(dims, f32)

    edge = shape(2, rows, side)
    large = pl.CostEstimate(flops=4_000_000_000, bytes_accessed=0, transcendentals=0)
    column, column_near = call(
        column_kernel, [shape(8, side), shape(8, side)], 0, 1, cost=large
    )(scan.reshape(1, 2))
    to_even, to_odd = call(edges_kernel, [edge, edge], 0, 1)(obj_field)
    column = lax.ppermute(column, ROW, pairs)
    with_even = lax.ppermute(to_even, COL, even_pairs)
    with_odd = lax.ppermute(to_odd, COL, odd_pairs)
    column_near = lax.ppermute(column_near, "core", swap)
    to_beyond, frame = call(
        beyond_kernel, [shape(strip + 8, side), shape(4, rows, cols + 2 * side)], 0, 4
    )(column, obj_field, with_even, with_odd)
    beyond = lax.ppermute(to_beyond, ROW, pairs)
    to_core = call(core_kernel, shape(strip, side), 0, 2)(column_near, frame)
    other = lax.ppermute(to_core, "core", swap)
    tabs = jnp.asarray(tables(side))
    small = pl.CostEstimate(flops=1000, bytes_accessed=1000, transcendentals=0)
    near = call(near_kernel, shape(strip, side), 1, 4, cost=small)(
        scan, frame, probe, patterns, tabs
    )
    near, other, beyond = lax.optimization_barrier((near, other, beyond))
    tall = pltpu.VMEM((4, 2 * half + rows, side), f32)
    keep, message_core, message_beyond, own_strip = call(
        main_kernel,
        [
            shape(modes * side, side),
            shape(modes * side + strip + 8, side),
            shape(strip + 8, side),
            shape(strip, side),
        ],
        2,
        6,
        [tall, tall],
    )(scan, live, near, other, beyond, probe, patterns, tabs)

    from_core = lax.ppermute(message_core, "core", swap)
    from_beyond = lax.ppermute(message_beyond, ROW, pairs)

    n_yx = lax.axis_size(("x", "y"))
    n_z = lax.axis_size(("zh", "zl"))
    total = modes * side
    chunk = total // n_yx
    summed = call(add_kernel, shape(total, side), 0, 2)(keep, from_core)
    planes, lines = peer_groups()
    spread = lax.all_to_all(
        summed.reshape(n_yx, chunk, side), EVERY, 0, 0, axis_index_groups=planes
    )

    centre, grad_even, grad_odd = call(
        merge_kernel,
        [shape(2, 2, rows, cols), edge, edge],
        1,
        3,
        [pltpu.VMEM((4, rows, cols + 2 * side), f32)],
    )(scan, own_strip, from_core, from_beyond)
    part = call(sum_kernel, shape(n_z, chunk, side), 0, 1)(spread)
    part = lax.all_to_all(part, EVERY, 0, 0, axis_index_groups=lines)
    part = call(sum_kernel, shape(n_yx, chunk, side), 0, 1)(part)
    got_even = lax.ppermute(grad_even, COL, even_pairs)
    part, got_even, grad_odd = lax.optimization_barrier((part, got_even, grad_odd))
    got_odd = lax.ppermute(grad_odd, COL, odd_pairs)
    whole = lax.all_to_all(part, EVERY, 0, 0, axis_index_groups=planes)
    whole, got_even, got_odd = lax.optimization_barrier((whole, got_even, got_odd))
    whole = whole.reshape(modes, side, side)
    facing = lax.ppermute(whole, "core", swap)
    obj_grad, probe_grad = call(
        finish_kernel,
        [shape(2, 2, rows, cols), shape(2, modes, side, side)],
        0,
        4,
        [pltpu.VMEM((2, 2, rows, cols), f32), pltpu.SemaphoreType.DMA, pltpu.SemaphoreType.DMA],
        out_far=(0, 1),
    )(centre, got_even, got_odd, whole)
    (probe_grad,) = call(
        other_half_kernel,
        [shape(2, modes, side, side)],
        0,
        1,
        [pltpu.SemaphoreType.DMA],
        n_far=1,
        out_far=(0,),
        aliases={1: 0},
    )(facing, probe_grad)
    return (obj_grad, probe_grad)


def solution(mesh):
    fine = Mesh(
        mesh.devices.reshape(8, 2, 2, 4, 4), ("y", "zh", "core", "x", "zl")
    )
    return jax.shard_map(
        body,
        mesh=fine,
        in_specs=(
            P(None, None, ROW, COL),
            P(),
            P(ROW, COL, None, None),
            P(ROW, COL),
            P(ROW, COL, None, None, None),
        ),
        out_specs=(P(None, None, ROW, COL), P()),
        check_vma=False,
    )
```

```python
import functools
import math

import jax
import jax.numpy as jnp
import ml_dtypes
import numpy as np
from jax import lax
from jax.experimental import pallas as pl
from jax.experimental.pallas import tpu as pltpu
from jax.sharding import Mesh
from jax.sharding import PartitionSpec as P

PHASE_COEF = 20.0
LOSS_WEIGHT = 0.125
ROW = ("y", "zh", "core")
COL = ("x", "zl")
EVERY = ("y", "zh", "core", "x", "zl")
VMEM_LIMIT = 48 * 1024 * 1024
TILE_COLS = 256


def split_bf16(table):
    high = table.astype(np.float32).astype(ml_dtypes.bfloat16)
    low = (table - high.astype(np.float64)).astype(np.float32).astype(ml_dtypes.bfloat16)
    return high, low


def tables(side):
    counter = np.arange(side)
    phase = 2.0 * math.pi / side * (counter[:, None] * counter[None, :] % side)
    fourier = np.exp(-1j * phase) / math.sqrt(side)
    spatial = ((counter + side // 2) % side - side // 2) / side
    factor = np.exp(-1j * PHASE_COEF * spatial * spatial)
    propagate = np.conj(fourier) @ (factor[:, None] * fourier)
    propagate = 0.5 * (propagate + propagate.T)
    parts = []
    for matrix in (propagate, fourier):
        for block in (matrix.real, matrix.imag, -matrix.imag):
            parts += split_bf16(block)
    return np.stack(parts)


def on_sides(tabs, which):
    def block(n, part):
        return tabs[6 * which + 2 * n + part]

    def square(a, b, c, d, part):
        return jnp.concatenate(
            [
                jnp.concatenate([block(a, part), block(b, part)], axis=1),
                jnp.concatenate([block(c, part), block(d, part)], axis=1),
            ],
            axis=0,
        )

    right = tuple(square(0, 1, 2, 0, part) for part in range(2))
    left = tuple(square(0, 2, 1, 0, part) for part in range(2))
    return right, left


def split(value):
    high = value.astype(jnp.bfloat16)
    low = (value - high.astype(jnp.float32)).astype(jnp.bfloat16)
    return high, low


def product(left, right):
    (left_high, left_low), (right_high, right_low) = left, right
    dot = functools.partial(jnp.dot, preferred_element_type=jnp.float32)
    return dot(left_high, right_high) + (dot(left_low, right_high) + dot(left_high, right_low))


def two_sided(real, imaginary, right, left, group=2):
    side = real[0].shape[0]
    middles = []
    for n in range(0, len(real), group):
        pairs = zip(real[n : n + group], imaginary[n : n + group])
        stacked = jnp.concatenate([jnp.concatenate(pair, axis=1) for pair in pairs], axis=0)
        middles.append(product(split(stacked), right))
    out_real, out_imaginary = [], []
    for middle in middles:
        blocks = [middle[m * side : (m + 1) * side] for m in range(group)]
        spread = jnp.concatenate(
            [
                jnp.concatenate([block[:, :side] for block in blocks], axis=1),
                jnp.concatenate([block[:, side:] for block in blocks], axis=1),
            ],
            axis=0,
        )
        out = product(left, split(spread))
        out_real += [out[:side, m * side : (m + 1) * side] for m in range(group)]
        out_imaginary += [out[side:, m * side : (m + 1) * side] for m in range(group)]
    return out_real, out_imaginary


def times(ar, ai, br, bi):
    return ar * br - ai * bi, ar * bi + ai * br


def times_conj(ar, ai, br, bi):
    return ar * br + ai * bi, ar * bi - ai * br


def model(window, probe, pattern, weight, tabs):
    (o0r, o1r), (o0i, o1i) = window
    qr, qi = probe
    modes = len(qr)
    prop_right, prop_left = on_sides(tabs, 0)
    four_right, four_left = on_sides(tabs, 1)
    e0 = [times(qr[m], qi[m], o0r, o0i) for m in range(modes)]
    a1r, a1i = two_sided([e[0] for e in e0], [e[1] for e in e0], prop_right, prop_left)
    e1 = [times(a1r[m], a1i[m], o1r, o1i) for m in range(modes)]
    gr, gi = two_sided([e[0] for e in e1], [e[1] for e in e1], four_right, four_left)
    intensity = gr[0] * gr[0] + gi[0] * gi[0]
    for m in range(1, modes):
        intensity = intensity + (gr[m] * gr[m] + gi[m] * gi[m])
    residue = (intensity - pattern) * (4.0 * LOSS_WEIGHT * weight)
    br, bi = two_sided(
        [residue * g for g in gr], [residue * g for g in gi], four_left, four_right
    )
    grad1 = [times_conj(a1r[m], a1i[m], br[m], bi[m]) for m in range(modes)]
    back = [times_conj(o1r, o1i, br[m], bi[m]) for m in range(modes)]
    cr, ci = two_sided([b[0] for b in back], [b[1] for b in back], prop_left, prop_right)
    grad0 = [times_conj(qr[m], qi[m], cr[m], ci[m]) for m in range(modes)]
    probe_grad = [times_conj(o0r, o0i, cr[m], ci[m]) for m in range(modes)]

    def over_modes(terms, part):
        return functools.reduce(lambda a, b: a + b, [t[part] for t in terms])

    window_grad = [
        [over_modes(grad0, 0), over_modes(grad1, 0)],
        [over_modes(grad0, 1), over_modes(grad1, 1)],
    ]
    return window_grad, probe_grad


def place_of(scan, rows, cols, half):
    row = scan[0] - (lax.axis_index(ROW) * rows - half)
    col = scan[1] - (lax.axis_index(COL) * cols - half)
    return row, col


def strips_at(half):
    core = lax.axis_index("core")
    return pl.multiple_of((1 - core) * 2 * half, 8), pl.multiple_of(core * 2 * half, 8)


def even_col():
    return lax.rem(lax.axis_index(COL), 2) == 0


def fill(frame, own, with_even, with_odd, part, layer):
    side = with_even.shape[2]
    half = side // 2
    cols = own.shape[3]
    plane = 2 * part + layer
    left = jnp.where(even_col(), with_odd[layer], with_even[layer])
    right = jnp.where(even_col(), with_even[layer], with_odd[layer])
    if part:
        left, right = pltpu.roll(left, half, 1), pltpu.roll(right, half, 1)
    frame[plane, :, 0:side] = left
    frame[plane, :, side : side + cols] = own[part, layer]
    frame[plane, :, side + cols :] = right


def cut(frame, plane, at, side):
    step = lax.rem(at, side)
    wide = frame[plane, :, pl.ds(pl.multiple_of(at - step, side), 2 * side)]
    return pltpu.roll(wide, lax.rem(2 * side - step, 2 * side), 1)[:, :side]


def column_kernel(scan, column, column_near):
    half = column.shape[1] // 2
    col = (scan[:, 1:2] - (lax.axis_index(COL) * TILE_COLS - half)).astype(jnp.float32)
    column[...] = jnp.broadcast_to(col, column.shape)
    column_near[...] = jnp.broadcast_to(col, column_near.shape)


def edges_kernel(own, with_even, with_odd):
    rows, cols = own.shape[2], own.shape[3]
    side = with_even.shape[2]
    half = side // 2
    inner = lax.broadcasted_iota(jnp.int32, (rows, side), 1) < half
    for layer in range(2):
        real, imaginary = own[0, layer], own[1, layer]
        left = jnp.where(inner, real[:, :side], pltpu.roll(imaginary[:, :side], half, 1))
        right = jnp.where(inner, pltpu.roll(imaginary[:, cols - side :], half, 1), real[:, cols - side :])
        with_even[layer] = jnp.where(even_col(), right, left)
        with_odd[layer] = jnp.where(even_col(), left, right)


def partner_column(column, cols):
    return jnp.clip(jnp.max(column[0:8, :]).astype(jnp.int32), 0, cols - 1)


def beyond_kernel(column, own, with_even, with_odd, to_beyond, frame):
    rows, cols = own.shape[2], own.shape[3]
    side = to_beyond.shape[1]
    col = partner_column(column, cols)
    for layer in range(2):
        for part in range(2):
            plane = 2 * part + layer
            fill(frame, own, with_even, with_odd, part, layer)
            to_beyond[pl.ds(plane * rows, rows), :] = cut(frame, plane, col + side // 2, side)
    to_beyond[pl.ds(4 * rows, 8), :] = jnp.zeros((8, side), jnp.float32)


def core_kernel(column, frame, to_core):
    side = to_core.shape[1]
    rows, cols = frame.shape[1], frame.shape[2] - 2 * side
    col = partner_column(column, cols)
    for plane in range(4):
        to_core[pl.ds(plane * rows, rows), :] = cut(frame, plane, col + side // 2, side)


def near_kernel(scan, frame, probe, pattern, tabs, near):
    rows, cols = frame.shape[1], frame.shape[2] - 2 * near.shape[1]
    side = near.shape[1]
    half = side // 2
    unused, col = place_of(scan, rows, cols, half)
    for plane in range(4):
        near[pl.ds(plane * rows, rows), :] = cut(frame, plane, col + half, side)


def main_kernel(
    scan, live, near, other, beyond, probe, pattern, tabs,
    keep, message_core, message_beyond, own_strip, column, shifted,
):
    side = probe.shape[-1]
    half = side // 2
    rows = own_strip.shape[0] // 4
    cols = TILE_COLS
    modes = probe.shape[1]
    row, col = place_of(scan, rows, cols, half)
    other_at, beyond_at = strips_at(half)
    for plane in range(4):
        at = pl.ds(plane * rows, rows)
        column[plane, half : half + rows, :] = near[at, :]
        column[plane, pl.ds(other_at, rows), :] = other[at, :]
        column[plane, pl.ds(beyond_at, rows), :] = beyond[at, :]
    tall = side + 8
    step = lax.rem(row, 8)
    base_row = pl.multiple_of(row - step, 8)

    def window_of(plane):
        high = column[plane, pl.ds(base_row, tall), :]
        return pltpu.roll(high, lax.rem(tall - step, tall), 0)[:side]

    window = [[window_of(2 * part + layer) for layer in range(2)] for part in range(2)]
    fields = [[probe[part, m] for m in range(modes)] for part in range(2)]
    weight = (live[0] > 0).astype(jnp.float32)
    window_grad, probe_grad = model(window, fields, pattern[0, 0, 0], weight, tabs)
    first = lax.axis_index("core") == 0
    for m in range(modes):
        at = pl.ds(m * side, side)
        real, imaginary = probe_grad[m]
        keep[at, :] = jnp.where(first, real, imaginary)
        message_core[at, :] = jnp.where(first, imaginary, real)
    base = modes * side
    shifted[...] = jnp.zeros_like(shifted)
    for part in range(2):
        for layer in range(2):
            plane = 2 * part + layer
            padded = jnp.concatenate(
                [window_grad[part][layer], jnp.zeros((8, side), jnp.float32)], axis=0
            )
            shifted[plane, pl.ds(base_row, tall), :] = pltpu.roll(padded, step, 0)
            at = pl.ds(plane * rows, rows)
            message_core[pl.ds(base + plane * rows, rows), :] = shifted[plane, pl.ds(other_at, rows), :]
            message_beyond[at, :] = shifted[plane, pl.ds(beyond_at, rows), :]
            own_strip[at, :] = shifted[plane, half : half + rows, :]
    offset = jnp.full((8, side), col.astype(jnp.float32))
    message_core[pl.ds(base + 4 * rows, 8), :] = offset
    message_beyond[pl.ds(4 * rows, 8), :] = offset


def merge_kernel(scan, own_strip, from_core, from_beyond, centre, with_even, with_odd, frame):
    side = own_strip.shape[1]
    half = side // 2
    rows = centre.shape[2]
    cols = centre.shape[3]
    base = from_core.shape[0] - from_beyond.shape[0]
    core_col = jnp.max(from_core[pl.ds(base + 4 * rows, 8), :]).astype(jnp.int32)
    beyond_col = jnp.max(from_beyond[pl.ds(4 * rows, 8), :]).astype(jnp.int32)
    unused, own_col = place_of(scan, rows, cols, half)
    lane = lax.broadcasted_iota(jnp.int32, (rows, side), 1)
    zero = jnp.zeros((rows, side), jnp.float32)
    frame[...] = jnp.zeros_like(frame)
    for source, first, col in (
        (own_strip, 0, own_col),
        (from_core, base, jnp.clip(core_col, 0, cols - 1)),
        (from_beyond, 0, jnp.clip(beyond_col, 0, cols - 1)),
    ):
        at = col + half
        step = lax.rem(at, side)
        near = pl.multiple_of(at - step, side)
        here, there = pl.ds(near, side), pl.ds(pl.multiple_of(near + side, side), side)
        for plane in range(4):
            strip = pltpu.roll(source[pl.ds(first + plane * rows, rows), :], step, 1)
            frame[plane, :, here] += jnp.where(lane >= step, strip, zero)
            frame[plane, :, there] += jnp.where(lane < step, strip, zero)
    inner = lane < half
    for layer in range(2):
        real, imaginary = layer, 2 + layer
        left = jnp.where(inner, pltpu.roll(frame[imaginary, :, 0:side], half, 1), frame[real, :, 0:side])
        right = jnp.where(inner, frame[real, :, side + cols :], pltpu.roll(frame[imaginary, :, side + cols :], half, 1))
        with_even[layer] = jnp.where(even_col(), right, left)
        with_odd[layer] = jnp.where(even_col(), left, right)
        centre[0, layer] = frame[real, :, side : side + cols]
        centre[1, layer] = frame[imaginary, :, side : side + cols]


def add_kernel(keep, message, out):
    out[...] = keep[...] + message[0 : keep.shape[0], :]


def sum_kernel(parts, copies):
    total = parts[0]
    for n in range(1, parts.shape[0]):
        total = total + parts[n]
    for n in range(copies.shape[0]):
        copies[n] = total


def finish_kernel(centre, with_even, with_odd, whole, out, probe_grad, total, sem, out_sem):
    copy = pltpu.make_async_copy(whole, probe_grad.at[lax.axis_index("core")], sem)
    copy.start()
    rows, cols = centre.shape[2], centre.shape[3]
    side = with_even.shape[2]
    half = side // 2
    inner = lax.broadcasted_iota(jnp.int32, (rows, side), 1) < half
    zero = jnp.zeros((rows, side), jnp.float32)
    for layer in range(2):
        left = jnp.where(even_col(), with_odd[layer], with_even[layer])
        right = jnp.where(even_col(), with_even[layer], with_odd[layer])
        for part in range(2):
            if part:
                left, right = pltpu.roll(left, half, 1), pltpu.roll(right, half, 1)
            value = centre[part, layer]
            total[part, layer, :, 0:side] = value[:, :side] + jnp.where(inner, left, zero)
            total[part, layer, :, cols - side :] = value[:, cols - side :] + jnp.where(inner, zero, right)
    out_copy = pltpu.make_async_copy(total, out, out_sem)
    out_copy.start()
    copy.wait()
    out_copy.wait()


def other_half_kernel(facing, half_done, probe_grad, sem):
    copy = pltpu.make_async_copy(facing, probe_grad.at[1 - lax.axis_index("core")], sem)
    copy.start()
    copy.wait()


def call(kernel, out_shape, n_scalars, n_in, scratch=(), cost=None, n_far=0, out_far=(), aliases=None):
    many = isinstance(out_shape, (list, tuple))
    vmem = pl.BlockSpec(memory_space=pltpu.VMEM)
    far = pl.BlockSpec(memory_space=pltpu.HBM)
    return pl.pallas_call(
        kernel,
        out_shape=out_shape,
        in_specs=[pl.BlockSpec(memory_space=pltpu.SMEM)] * n_scalars + [vmem] * n_in + [far] * n_far,
        out_specs=[far if n in out_far else vmem for n in range(len(out_shape))] if many else vmem,
        input_output_aliases=aliases or {},
        scratch_shapes=list(scratch),
        compiler_params=pltpu.CompilerParams(vmem_limit_bytes=VMEM_LIMIT),
        cost_estimate=cost,
    )


def both_ways(pairs):
    return pairs + [(j, i) for i, j in pairs]


def peer_groups():
    sizes = {axis: lax.axis_size(axis) for axis in EVERY}
    n_x, n_y, n_z = sizes["x"], sizes["y"], sizes["zh"] * sizes["zl"]

    def index(x, y, z, core):
        at = {"x": x, "y": y, "zh": z // sizes["zl"], "zl": z % sizes["zl"], "core": core}
        flat = 0
        for axis in EVERY:
            flat = flat * sizes[axis] + at[axis]
        return flat

    planes = [[index(x, y, z, 0) for x in range(n_x) for y in range(n_y)] for z in range(n_z)]
    planes += [[index(x, y, z, 1) for z in range(n_z) for x in range(n_x)] for y in range(n_y)]
    lines = [[index(x, y, z, 0) for z in range(n_z)] for x in range(n_x) for y in range(n_y)]
    lines += [[index(x, y, z, 1) for y in range(n_y)] for x in range(n_x) for z in range(n_z)]
    return planes, lines


def body(obj_field, probe, scan_pos, live_count, patterns):
    side = probe.shape[2]
    modes = probe.shape[1]
    half = side // 2
    rows, cols = obj_field.shape[2], obj_field.shape[3]
    n_row, n_col = lax.axis_size(ROW), lax.axis_size(COL)
    f32 = jnp.float32
    scan = scan_pos.reshape(2)
    live = live_count.reshape(1)
    swap = [(0, 1), (1, 0)]
    pairs = both_ways([(i, i + 1) for i in range(1, n_row - 1, 2)])
    even_pairs = both_ways([(i, i + 1) for i in range(0, n_col - 1, 2)])
    odd_pairs = both_ways([(i, i + 1) for i in range(1, n_col - 1, 2)])
    strip = 4 * rows

    def shape(*dims):
        return jax.ShapeDtypeStruct(dims, f32)

    edge = shape(2, rows, side)
    large = pl.CostEstimate(flops=4_000_000_000, bytes_accessed=0, transcendentals=0)
    column, column_near = call(
        column_kernel, [shape(136, side), shape(8, side)], 0, 1, cost=large
    )(scan.reshape(1, 2))
    to_even, to_odd = call(edges_kernel, [edge, edge], 0, 1)(obj_field)
    column = lax.ppermute(column, ROW, pairs)
    with_even = lax.ppermute(to_even, COL, even_pairs)
    with_odd = lax.ppermute(to_odd, COL, odd_pairs)
    column_near = lax.ppermute(column_near, "core", swap)
    to_beyond, frame = call(
        beyond_kernel, [shape(strip + 8, side), shape(4, rows, cols + 2 * side)], 0, 4
    )(column, obj_field, with_even, with_odd)
    beyond = lax.ppermute(to_beyond, ROW, pairs)
    to_core = call(core_kernel, shape(strip, side), 0, 2)(column_near, frame)
    other = lax.ppermute(to_core, "core", swap)
    tabs = jnp.asarray(tables(side))
    small = pl.CostEstimate(flops=1000, bytes_accessed=1000, transcendentals=0)
    near = call(near_kernel, shape(strip, side), 1, 4, cost=small)(
        scan, frame, probe, patterns, tabs
    )
    near, other, beyond = lax.optimization_barrier((near, other, beyond))
    tall = pltpu.VMEM((4, 2 * half + rows, side), f32)
    keep, message_core, message_beyond, own_strip = call(
        main_kernel,
        [
            shape(modes * side, side),
            shape(modes * side + strip + 8, side),
            shape(strip + 8, side),
            shape(strip, side),
        ],
        2,
        6,
        [tall, tall],
    )(scan, live, near, other, beyond, probe, patterns, tabs)

    from_core = lax.ppermute(message_core, "core", swap)
    from_beyond = lax.ppermute(message_beyond, ROW, pairs)

    n_yx = lax.axis_size(("x", "y"))
    n_z = lax.axis_size(("zh", "zl"))
    total = modes * side
    chunk = total // n_yx
    summed = call(add_kernel, shape(total, side), 0, 2)(keep, from_core)
    planes, lines = peer_groups()
    spread = lax.all_to_all(
        summed.reshape(n_yx, chunk, side), EVERY, 0, 0, axis_index_groups=planes
    )

    centre, grad_even, grad_odd = call(
        merge_kernel,
        [shape(2, 2, rows, cols), edge, edge],
        1,
        3,
        [pltpu.VMEM((4, rows, cols + 2 * side), f32)],
    )(scan, own_strip, from_core, from_beyond)
    part = call(sum_kernel, shape(n_z, chunk, side), 0, 1)(spread)
    part = lax.all_to_all(part, EVERY, 0, 0, axis_index_groups=lines)
    part = call(sum_kernel, shape(n_yx, chunk, side), 0, 1)(part)
    got_even = lax.ppermute(grad_even, COL, even_pairs)
    part, got_even, grad_odd = lax.optimization_barrier((part, got_even, grad_odd))
    got_odd = lax.ppermute(grad_odd, COL, odd_pairs)
    whole = lax.all_to_all(part, EVERY, 0, 0, axis_index_groups=planes)
    whole, got_even, got_odd = lax.optimization_barrier((whole, got_even, got_odd))
    whole = whole.reshape(modes, side, side)
    facing = lax.ppermute(whole, "core", swap)
    obj_grad, probe_grad = call(
        finish_kernel,
        [shape(2, 2, rows, cols), shape(2, modes, side, side)],
        0,
        4,
        [pltpu.VMEM((2, 2, rows, cols), f32), pltpu.SemaphoreType.DMA, pltpu.SemaphoreType.DMA],
        out_far=(0, 1),
    )(centre, got_even, got_odd, whole)
    (probe_grad,) = call(
        other_half_kernel,
        [shape(2, modes, side, side)],
        0,
        1,
        [pltpu.SemaphoreType.DMA],
        n_far=1,
        out_far=(0,),
        aliases={1: 0},
    )(facing, probe_grad)
    return (obj_grad, probe_grad)


def solution(mesh):
    fine = Mesh(
        mesh.devices.reshape(8, 2, 2, 4, 4), ("y", "zh", "core", "x", "zl")
    )
    return jax.shard_map(
        body,
        mesh=fine,
        in_specs=(
            P(None, None, ROW, COL),
            P(),
            P(ROW, COL, None, None),
            P(ROW, COL),
            P(ROW, COL, None, None, None),
        ),
        out_specs=(P(None, None, ROW, COL), P()),
        check_vma=False,
    )
```

```python
import functools
import math

import jax
import jax.numpy as jnp
import ml_dtypes
import numpy as np
from jax import lax
from jax.experimental import pallas as pl
from jax.experimental.pallas import tpu as pltpu
from jax.sharding import Mesh
from jax.sharding import PartitionSpec as P

PHASE_COEF = 20.0
LOSS_WEIGHT = 0.125
ROW = ("y", "zh", "core")
COL = ("x", "zl")
EVERY = ("y", "zh", "core", "x", "zl")
VMEM_LIMIT = 48 * 1024 * 1024
TILE_COLS = 256


def split_bf16(table):
    high = table.astype(np.float32).astype(ml_dtypes.bfloat16)
    low = (table - high.astype(np.float64)).astype(np.float32).astype(ml_dtypes.bfloat16)
    return high, low


def tables(side):
    counter = np.arange(side)
    phase = 2.0 * math.pi / side * (counter[:, None] * counter[None, :] % side)
    fourier = np.exp(-1j * phase) / math.sqrt(side)
    spatial = ((counter + side // 2) % side - side // 2) / side
    factor = np.exp(-1j * PHASE_COEF * spatial * spatial)
    propagate = np.conj(fourier) @ (factor[:, None] * fourier)
    propagate = 0.5 * (propagate + propagate.T)
    parts = []
    for matrix in (propagate, fourier):
        for block in (matrix.real, matrix.imag, -matrix.imag):
            parts += split_bf16(block)
    return np.stack(parts)


def on_sides(tabs, which):
    def block(n, part):
        return tabs[6 * which + 2 * n + part]

    def square(a, b, c, d, part):
        return jnp.concatenate(
            [
                jnp.concatenate([block(a, part), block(b, part)], axis=1),
                jnp.concatenate([block(c, part), block(d, part)], axis=1),
            ],
            axis=0,
        )

    right = tuple(square(0, 1, 2, 0, part) for part in range(2))
    left = tuple(square(0, 2, 1, 0, part) for part in range(2))
    return right, left


def split(value):
    high = value.astype(jnp.bfloat16)
    low = (value - high.astype(jnp.float32)).astype(jnp.bfloat16)
    return high, low


def product(left, right):
    (left_high, left_low), (right_high, right_low) = left, right
    dot = functools.partial(jnp.dot, preferred_element_type=jnp.float32)
    return dot(left_high, right_high) + (dot(left_low, right_high) + dot(left_high, right_low))


def two_sided(real, imaginary, right, left, group=2):
    side = real[0].shape[0]
    middles = []
    for n in range(0, len(real), group):
        pairs = zip(real[n : n + group], imaginary[n : n + group])
        stacked = jnp.concatenate([jnp.concatenate(pair, axis=1) for pair in pairs], axis=0)
        middles.append(product(split(stacked), right))
    out_real, out_imaginary = [], []
    for middle in middles:
        blocks = [middle[m * side : (m + 1) * side] for m in range(group)]
        spread = jnp.concatenate(
            [
                jnp.concatenate([block[:, :side] for block in blocks], axis=1),
                jnp.concatenate([block[:, side:] for block in blocks], axis=1),
            ],
            axis=0,
        )
        out = product(left, split(spread))
        out_real += [out[:side, m * side : (m + 1) * side] for m in range(group)]
        out_imaginary += [out[side:, m * side : (m + 1) * side] for m in range(group)]
    return out_real, out_imaginary


def times(ar, ai, br, bi):
    return ar * br - ai * bi, ar * bi + ai * br


def times_conj(ar, ai, br, bi):
    return ar * br + ai * bi, ar * bi - ai * br


def model(window, probe, pattern, weight, tabs):
    (o0r, o1r), (o0i, o1i) = window
    qr, qi = probe
    modes = len(qr)
    prop_right, prop_left = on_sides(tabs, 0)
    four_right, four_left = on_sides(tabs, 1)
    e0 = [times(qr[m], qi[m], o0r, o0i) for m in range(modes)]
    a1r, a1i = two_sided([e[0] for e in e0], [e[1] for e in e0], prop_right, prop_left)
    e1 = [times(a1r[m], a1i[m], o1r, o1i) for m in range(modes)]
    gr, gi = two_sided([e[0] for e in e1], [e[1] for e in e1], four_right, four_left)
    intensity = gr[0] * gr[0] + gi[0] * gi[0]
    for m in range(1, modes):
        intensity = intensity + (gr[m] * gr[m] + gi[m] * gi[m])
    residue = (intensity - pattern) * (4.0 * LOSS_WEIGHT * weight)
    br, bi = two_sided(
        [residue * g for g in gr], [residue * g for g in gi], four_left, four_right
    )
    grad1 = [times_conj(a1r[m], a1i[m], br[m], bi[m]) for m in range(modes)]
    back = [times_conj(o1r, o1i, br[m], bi[m]) for m in range(modes)]
    cr, ci = two_sided([b[0] for b in back], [b[1] for b in back], prop_left, prop_right)
    grad0 = [times_conj(qr[m], qi[m], cr[m], ci[m]) for m in range(modes)]
    probe_grad = [times_conj(o0r, o0i, cr[m], ci[m]) for m in range(modes)]

    def over_modes(terms, part):
        return functools.reduce(lambda a, b: a + b, [t[part] for t in terms])

    window_grad = [
        [over_modes(grad0, 0), over_modes(grad1, 0)],
        [over_modes(grad0, 1), over_modes(grad1, 1)],
    ]
    return window_grad, probe_grad


def place_of(scan, rows, cols, half):
    row = scan[0] - (lax.axis_index(ROW) * rows - half)
    col = scan[1] - (lax.axis_index(COL) * cols - half)
    return row, col


def strips_at(half):
    core = lax.axis_index("core")
    return pl.multiple_of((1 - core) * 2 * half, 8), pl.multiple_of(core * 2 * half, 8)


def even_col():
    return lax.rem(lax.axis_index(COL), 2) == 0


def fill(frame, own, with_even, with_odd, part, layer):
    side = with_even.shape[2]
    half = side // 2
    cols = own.shape[3]
    plane = 2 * part + layer
    left = jnp.where(even_col(), with_odd[layer], with_even[layer])
    right = jnp.where(even_col(), with_even[layer], with_odd[layer])
    if part:
        left, right = pltpu.roll(left, half, 1), pltpu.roll(right, half, 1)
    frame[plane, :, 0:side] = left
    frame[plane, :, side : side + cols] = own[part, layer]
    frame[plane, :, side + cols :] = right


def cut(frame, plane, at, side):
    step = lax.rem(at, side)
    wide = frame[plane, :, pl.ds(pl.multiple_of(at - step, side), 2 * side)]
    return pltpu.roll(wide, lax.rem(2 * side - step, 2 * side), 1)[:, :side]


def column_kernel(scan, column, column_near):
    half = column.shape[1] // 2
    col = (scan[:, 1:2] - (lax.axis_index(COL) * TILE_COLS - half)).astype(jnp.float32)
    column[...] = jnp.broadcast_to(col, column.shape)
    column_near[...] = jnp.broadcast_to(col, column_near.shape)


def edges_kernel(own, with_even, with_odd):
    rows, cols = own.shape[2], own.shape[3]
    side = with_even.shape[2]
    half = side // 2
    inner = lax.broadcasted_iota(jnp.int32, (rows, side), 1) < half
    for layer in range(2):
        real, imaginary = own[0, layer], own[1, layer]
        left = jnp.where(inner, real[:, :side], pltpu.roll(imaginary[:, :side], half, 1))
        right = jnp.where(inner, pltpu.roll(imaginary[:, cols - side :], half, 1), real[:, cols - side :])
        with_even[layer] = jnp.where(even_col(), right, left)
        with_odd[layer] = jnp.where(even_col(), left, right)


def partner_column(column, cols):
    return jnp.clip(jnp.max(column[0:8, :]).astype(jnp.int32), 0, cols - 1)


def beyond_kernel(column, own, with_even, with_odd, to_beyond, frame):
    rows, cols = own.shape[2], own.shape[3]
    side = to_beyond.shape[1]
    col = partner_column(column, cols)
    for layer in range(2):
        for part in range(2):
            plane = 2 * part + layer
            fill(frame, own, with_even, with_odd, part, layer)
            to_beyond[pl.ds(plane * rows, rows), :] = cut(frame, plane, col + side // 2, side)
    to_beyond[pl.ds(4 * rows, 8), :] = jnp.zeros((8, side), jnp.float32)


def core_kernel(column, frame, to_core):
    side = to_core.shape[1]
    rows, cols = frame.shape[1], frame.shape[2] - 2 * side
    col = partner_column(column, cols)
    for plane in range(4):
        to_core[pl.ds(plane * rows, rows), :] = cut(frame, plane, col + side // 2, side)


def near_kernel(scan, frame, probe, pattern, tabs, near):
    rows, cols = frame.shape[1], frame.shape[2] - 2 * near.shape[1]
    side = near.shape[1]
    half = side // 2
    unused, col = place_of(scan, rows, cols, half)
    for plane in range(4):
        near[pl.ds(plane * rows, rows), :] = cut(frame, plane, col + half, side)


def main_kernel(
    scan, live, near, other, beyond, probe, pattern, tabs,
    keep, message_core, message_beyond, own_strip, column, shifted,
):
    side = probe.shape[-1]
    half = side // 2
    rows = own_strip.shape[0] // 4
    cols = TILE_COLS
    modes = probe.shape[1]
    row, col = place_of(scan, rows, cols, half)
    other_at, beyond_at = strips_at(half)
    for plane in range(4):
        at = pl.ds(plane * rows, rows)
        column[plane, half : half + rows, :] = near[at, :]
        column[plane, pl.ds(other_at, rows), :] = other[at, :]
        column[plane, pl.ds(beyond_at, rows), :] = beyond[at, :]
    tall = side + 8
    step = lax.rem(row, 8)
    base_row = pl.multiple_of(row - step, 8)

    def window_of(plane):
        high = column[plane, pl.ds(base_row, tall), :]
        return pltpu.roll(high, lax.rem(tall - step, tall), 0)[:side]

    window = [[window_of(2 * part + layer) for layer in range(2)] for part in range(2)]
    fields = [[probe[part, m] for m in range(modes)] for part in range(2)]
    weight = (live[0] > 0).astype(jnp.float32)
    window_grad, probe_grad = model(window, fields, pattern[0, 0, 0], weight, tabs)
    first = lax.axis_index("core") == 0
    for m in range(modes):
        at = pl.ds(m * side, side)
        real, imaginary = probe_grad[m]
        keep[at, :] = jnp.where(first, real, imaginary)
        message_core[at, :] = jnp.where(first, imaginary, real)
    base = modes * side
    shifted[...] = jnp.zeros_like(shifted)
    for part in range(2):
        for layer in range(2):
            plane = 2 * part + layer
            padded = jnp.concatenate(
                [window_grad[part][layer], jnp.zeros((8, side), jnp.float32)], axis=0
            )
            shifted[plane, pl.ds(base_row, tall), :] = pltpu.roll(padded, step, 0)
            at = pl.ds(plane * rows, rows)
            message_core[pl.ds(base + plane * rows, rows), :] = shifted[plane, pl.ds(other_at, rows), :]
            message_beyond[at, :] = shifted[plane, pl.ds(beyond_at, rows), :]
            own_strip[at, :] = shifted[plane, half : half + rows, :]
    offset = jnp.full((8, side), col.astype(jnp.float32))
    message_core[pl.ds(base + 4 * rows, 8), :] = offset
    message_beyond[pl.ds(4 * rows, 8), :] = offset


def merge_kernel(scan, own_strip, from_core, from_beyond, centre, with_even, with_odd, frame):
    side = own_strip.shape[1]
    half = side // 2
    rows = centre.shape[2]
    cols = centre.shape[3]
    base = from_core.shape[0] - from_beyond.shape[0]
    core_col = jnp.max(from_core[pl.ds(base + 4 * rows, 8), :]).astype(jnp.int32)
    beyond_col = jnp.max(from_beyond[pl.ds(4 * rows, 8), :]).astype(jnp.int32)
    unused, own_col = place_of(scan, rows, cols, half)
    lane = lax.broadcasted_iota(jnp.int32, (rows, side), 1)
    zero = jnp.zeros((rows, side), jnp.float32)
    frame[...] = jnp.zeros_like(frame)
    for source, first, col in (
        (own_strip, 0, own_col),
        (from_core, base, jnp.clip(core_col, 0, cols - 1)),
        (from_beyond, 0, jnp.clip(beyond_col, 0, cols - 1)),
    ):
        at = col + half
        step = lax.rem(at, side)
        near = pl.multiple_of(at - step, side)
        here, there = pl.ds(near, side), pl.ds(pl.multiple_of(near + side, side), side)
        for plane in range(4):
            strip = pltpu.roll(source[pl.ds(first + plane * rows, rows), :], step, 1)
            frame[plane, :, here] += jnp.where(lane >= step, strip, zero)
            frame[plane, :, there] += jnp.where(lane < step, strip, zero)
    inner = lane < half
    for layer in range(2):
        real, imaginary = layer, 2 + layer
        left = jnp.where(inner, pltpu.roll(frame[imaginary, :, 0:side], half, 1), frame[real, :, 0:side])
        right = jnp.where(inner, frame[real, :, side + cols :], pltpu.roll(frame[imaginary, :, side + cols :], half, 1))
        with_even[layer] = jnp.where(even_col(), right, left)
        with_odd[layer] = jnp.where(even_col(), left, right)
        centre[0, layer] = frame[real, :, side : side + cols]
        centre[1, layer] = frame[imaginary, :, side : side + cols]


def add_kernel(keep, message, out):
    out[...] = keep[...] + message[0 : keep.shape[0], :]


def sum_kernel(parts, copies):
    total = parts[0]
    for n in range(1, parts.shape[0]):
        total = total + parts[n]
    for n in range(copies.shape[0]):
        copies[n] = total


def finish_kernel(centre, with_even, with_odd, whole, out, probe_grad, total, sem, out_sem):
    copy = pltpu.make_async_copy(whole, probe_grad.at[lax.axis_index("core")], sem)
    copy.start()
    rows, cols = centre.shape[2], centre.shape[3]
    side = with_even.shape[2]
    half = side // 2
    inner = lax.broadcasted_iota(jnp.int32, (rows, side), 1) < half
    zero = jnp.zeros((rows, side), jnp.float32)
    for layer in range(2):
        left = jnp.where(even_col(), with_odd[layer], with_even[layer])
        right = jnp.where(even_col(), with_even[layer], with_odd[layer])
        for part in range(2):
            if part:
                left, right = pltpu.roll(left, half, 1), pltpu.roll(right, half, 1)
            value = centre[part, layer]
            total[part, layer, :, 0:side] = value[:, :side] + jnp.where(inner, left, zero)
            total[part, layer, :, cols - side :] = value[:, cols - side :] + jnp.where(inner, zero, right)
    out_copy = pltpu.make_async_copy(total, out, out_sem)
    out_copy.start()
    copy.wait()
    out_copy.wait()


def other_half_kernel(facing, half_done, probe_grad, sem):
    copy = pltpu.make_async_copy(facing, probe_grad.at[1 - lax.axis_index("core")], sem)
    copy.start()
    copy.wait()


def call(kernel, out_shape, n_scalars, n_in, scratch=(), cost=None, n_far=0, out_far=(), aliases=None):
    many = isinstance(out_shape, (list, tuple))
    vmem = pl.BlockSpec(memory_space=pltpu.VMEM)
    far = pl.BlockSpec(memory_space=pltpu.HBM)
    return pl.pallas_call(
        kernel,
        out_shape=out_shape,
        in_specs=[pl.BlockSpec(memory_space=pltpu.SMEM)] * n_scalars + [vmem] * n_in + [far] * n_far,
        out_specs=[far if n in out_far else vmem for n in range(len(out_shape))] if many else vmem,
        input_output_aliases=aliases or {},
        scratch_shapes=list(scratch),
        compiler_params=pltpu.CompilerParams(vmem_limit_bytes=VMEM_LIMIT),
        cost_estimate=cost,
    )


def both_ways(pairs):
    return pairs + [(j, i) for i, j in pairs]


def peer_groups():
    sizes = {axis: lax.axis_size(axis) for axis in EVERY}
    n_x, n_y, n_z = sizes["x"], sizes["y"], sizes["zh"] * sizes["zl"]

    def index(x, y, z, core):
        at = {"x": x, "y": y, "zh": z // sizes["zl"], "zl": z % sizes["zl"], "core": core}
        flat = 0
        for axis in EVERY:
            flat = flat * sizes[axis] + at[axis]
        return flat

    planes = [[index(x, y, z, 0) for x in range(n_x) for y in range(n_y)] for z in range(n_z)]
    planes += [[index(x, y, z, 1) for x in range(n_x) for z in range(n_z)] for y in range(n_y)]
    lines = [[index(x, y, z, 0) for z in range(n_z)] for x in range(n_x) for y in range(n_y)]
    lines += [[index(x, y, z, 1) for y in range(n_y)] for x in range(n_x) for z in range(n_z)]
    return planes, lines


def body(obj_field, probe, scan_pos, live_count, patterns):
    side = probe.shape[2]
    modes = probe.shape[1]
    half = side // 2
    rows, cols = obj_field.shape[2], obj_field.shape[3]
    n_row, n_col = lax.axis_size(ROW), lax.axis_size(COL)
    f32 = jnp.float32
    scan = scan_pos.reshape(2)
    live = live_count.reshape(1)
    swap = [(0, 1), (1, 0)]
    pairs = both_ways([(i, i + 1) for i in range(1, n_row - 1, 2)])
    even_pairs = both_ways([(i, i + 1) for i in range(0, n_col - 1, 2)])
    odd_pairs = both_ways([(i, i + 1) for i in range(1, n_col - 1, 2)])
    strip = 4 * rows

    def shape(*dims):
        return jax.ShapeDtypeStruct(dims, f32)

    edge = shape(2, rows, side)
    large = pl.CostEstimate(flops=4_000_000_000, bytes_accessed=0, transcendentals=0)
    column, column_near = call(
        column_kernel, [shape(136, side), shape(8, side)], 0, 1, cost=large
    )(scan.reshape(1, 2))
    to_even, to_odd = call(edges_kernel, [edge, edge], 0, 1)(obj_field)
    column = lax.ppermute(column, ROW, pairs)
    with_even = lax.ppermute(to_even, COL, even_pairs)
    with_odd = lax.ppermute(to_odd, COL, odd_pairs)
    column_near = lax.ppermute(column_near, "core", swap)
    to_beyond, frame = call(
        beyond_kernel, [shape(strip + 8, side), shape(4, rows, cols + 2 * side)], 0, 4
    )(column, obj_field, with_even, with_odd)
    beyond = lax.ppermute(to_beyond, ROW, pairs)
    to_core = call(core_kernel, shape(strip, side), 0, 2)(column_near, frame)
    other = lax.ppermute(to_core, "core", swap)
    tabs = jnp.asarray(tables(side))
    small = pl.CostEstimate(flops=1000, bytes_accessed=1000, transcendentals=0)
    near = call(near_kernel, shape(strip, side), 1, 4, cost=small)(
        scan, frame, probe, patterns, tabs
    )
    near, other, beyond = lax.optimization_barrier((near, other, beyond))
    tall = pltpu.VMEM((4, 2 * half + rows, side), f32)
    keep, message_core, message_beyond, own_strip = call(
        main_kernel,
        [
            shape(modes * side, side),
            shape(modes * side + strip + 8, side),
            shape(strip + 8, side),
            shape(strip, side),
        ],
        2,
        6,
        [tall, tall],
    )(scan, live, near, other, beyond, probe, patterns, tabs)

    from_core = lax.ppermute(message_core, "core", swap)
    from_beyond = lax.ppermute(message_beyond, ROW, pairs)

    n_yx = lax.axis_size(("x", "y"))
    n_z = lax.axis_size(("zh", "zl"))
    total = modes * side
    chunk = total // n_yx
    summed = call(add_kernel, shape(total, side), 0, 2)(keep, from_core)
    planes, lines = peer_groups()
    spread = lax.all_to_all(
        summed.reshape(n_yx, chunk, side), EVERY, 0, 0, axis_index_groups=planes
    )

    centre, grad_even, grad_odd = call(
        merge_kernel,
        [shape(2, 2, rows, cols), edge, edge],
        1,
        3,
        [pltpu.VMEM((4, rows, cols + 2 * side), f32)],
    )(scan, own_strip, from_core, from_beyond)
    part = call(sum_kernel, shape(n_z, chunk, side), 0, 1)(spread)
    part = lax.all_to_all(part, EVERY, 0, 0, axis_index_groups=lines)
    part = call(sum_kernel, shape(n_yx, chunk, side), 0, 1)(part)
    part, grad_even, grad_odd = lax.optimization_barrier((part, grad_even, grad_odd))
    got_even = lax.ppermute(grad_even, COL, even_pairs)
    got_odd = lax.ppermute(grad_odd, COL, odd_pairs)
    whole = lax.all_to_all(part, EVERY, 0, 0, axis_index_groups=planes)
    whole, got_even, got_odd = lax.optimization_barrier((whole, got_even, got_odd))
    whole = whole.reshape(modes, side, side)
    facing = lax.ppermute(whole, "core", swap)
    obj_grad, probe_grad = call(
        finish_kernel,
        [shape(2, 2, rows, cols), shape(2, modes, side, side)],
        0,
        4,
        [pltpu.VMEM((2, 2, rows, cols), f32), pltpu.SemaphoreType.DMA, pltpu.SemaphoreType.DMA],
        out_far=(0, 1),
    )(centre, got_even, got_odd, whole)
    (probe_grad,) = call(
        other_half_kernel,
        [shape(2, modes, side, side)],
        0,
        1,
        [pltpu.SemaphoreType.DMA],
        n_far=1,
        out_far=(0,),
        aliases={1: 0},
    )(facing, probe_grad)
    return (obj_grad, probe_grad)


def solution(mesh):
    fine = Mesh(
        mesh.devices.reshape(8, 2, 2, 4, 4), ("y", "zh", "core", "x", "zl")
    )
    return jax.shard_map(
        body,
        mesh=fine,
        in_specs=(
            P(None, None, ROW, COL),
            P(),
            P(ROW, COL, None, None),
            P(ROW, COL),
            P(ROW, COL, None, None, None),
        ),
        out_specs=(P(None, None, ROW, COL), P()),
        check_vma=False,
    )
```
